32 devices in a mesh: dp: 4 (over z), seq: 4 (over x, core), expert: 2 (over y).
Axes of the slice: x: 2, y: 2, z: 4, core: 2. Of those that a mesh axis runs over, the one named last changes fastest.
Arguments:
- tokens: bfloat16 [16, 1024, 768], P(('dp', 'expert'), 'seq'), may hold values from -6 to 6
- token_ids: int32 [16, 1024], P(('dp', 'expert'), 'seq'), may hold values from 0 to 8191, as said below
- hash_table: int32 [8192], replicated, may hold values from 0 to 1, as said below
- lengths: int32 [16, 2], P(('dp', 'expert')), may hold values from 0 to 1024, as said below
- gain_attn: float32 [768], replicated, may hold values from 0.5 to 1.5
- w_query: bfloat16 [768, 768], replicated, may hold values from -0.21875 to 0.21875
- w_key: bfloat16 [768, 768], replicated, may hold values from -0.21875 to 0.21875
- w_value: bfloat16 [768, 768], replicated, may hold values from -0.21875 to 0.21875
- w_output: bfloat16 [768, 768], replicated, may hold values from -1.25 to 1.25
- gain_ffn: float32 [768], replicated, may hold values from 0.5 to 1.5
- w_in: bfloat16 [2, 768, 3072], P('expert', None, 'seq'), may hold values from -0.21875 to 0.21875
- w_out: bfloat16 [2, 3072, 768], P('expert', 'seq'), may hold values from -0.109375 to 0.109375
- cotangent: bfloat16 [16, 1024, 768], P(('dp', 'expert'), 'seq'), may hold values from -6 to 6
Outputs:
- output: bfloat16 [16, 1024, 768], P(('dp', 'expert'), 'seq')
- input_grad: float32 [16, 1024, 768], P(('dp', 'expert'), 'seq')
- grad_gain_attn: float32 [768], replicated
- grad_query: float32 [768, 768], replicated
- grad_key: float32 [768, 768], replicated
- grad_value: float32 [768, 768], replicated
- grad_output: float32 [768, 768], replicated
- grad_gain_ffn: float32 [768], replicated
- grad_in: float32 [2, 768, 3072], P('expert', None, 'seq')
- grad_out: float32 [2, 3072, 768], P('expert', 'seq')
The draws below stay inside these ranges and needn't reach their ends.
Inputs may be any that keep to these rules, and one draw needn't show every extreme that they name: `token_ids`: among the 512 tokens of one device (positions s * 256 to (s + 1) * 256 - 1 of each of its 2 rows), at most 384 are hashed to any one expert; on every device exactly 384 are hashed to one expert, and that expert is the same on all devices that share a dp index and a seq index. `hash_table`: each expert is the image of 4096 token ids. `lengths`: each row holds either one document of 1024 positions (its second length is 0) or two documents of 512 positions; among the 2 rows that one device holds, at least one is a single document.
All inputs are finite; a program needn't handle non-finite values.
Results may differ from the reference program's by a relative error of at most 0.015.
Values may be sent and summed in bfloat16 or wider, within the bound.
A program may use at most 192 MiB of HBM per device.

```python
import jax
import jax.numpy as jnp
from jax import lax

D = 768
H = 12
HD = 64
FF = 3072
VOCAB = 8192
SPAN = 256
ROWS = 2
TOK_DEV = 512
EXPERTS = 2
SEQS = 16
GROUP_TOK = 1024
CAP = 384


def shared_order(key):
    return jax.random.permutation(jax.random.fold_in(key, 7), VOCAB).astype(jnp.int32)


def draw_hash_table(key, part):
    order = shared_order(key)
    labels = jnp.arange(VOCAB, dtype=jnp.int32) % EXPERTS
    return jnp.zeros((VOCAB,), jnp.int32).at[order].set(labels)


def draw_lengths(key, part):
    key = jax.random.fold_in(key, 17)
    groups = SEQS // ROWS
    split = jax.random.randint(jax.random.fold_in(key, 1), (groups, ROWS), 0, 2, dtype=jnp.int32)
    whole_pick = jax.random.randint(jax.random.fold_in(key, 2), (groups,), 0, ROWS, dtype=jnp.int32)
    split = jnp.where(jnp.arange(ROWS, dtype=jnp.int32)[None, :] == whole_pick[:, None], 0, split)
    first = jnp.where(split == 1, GROUP_TOK // 2, GROUP_TOK).astype(jnp.int32)
    second = (GROUP_TOK - first).astype(jnp.int32)
    return jnp.stack([first, second], axis=-1).reshape(SEQS, 2).astype(jnp.int32)


def draw_token_ids(key, part):
    order = shared_order(key)
    key = jax.random.fold_in(key, 13)
    pieces = GROUP_TOK // SPAN
    groups = SEQS // ROWS
    blocks = groups * pieces
    rest = TOK_DEV - CAP
    hot_table = jax.random.randint(jax.random.fold_in(key, 1), (groups // EXPERTS, pieces), 0, EXPERTS, dtype=jnp.int32)
    block_numbers = jnp.arange(blocks, dtype=jnp.int32)
    hot = hot_table[block_numbers // pieces // EXPERTS, block_numbers % pieces]
    order_in = jnp.arange(TOK_DEV, dtype=jnp.int32)[None, :]
    if EXPERTS == 2:
        offset = jnp.where(order_in < CAP, 0, 1).astype(jnp.int32)
    else:
        spare = EXPERTS - 2
        lowest = (rest - CAP + spare - 1) // spare
        top_count = (rest - 1) // spare
        counts = jax.random.randint(jax.random.fold_in(key, 2), (blocks, spare), lowest, top_count + 1, dtype=jnp.int32)
        warm = rest - jnp.sum(counts, axis=1)
        warm_pick = jax.random.randint(jax.random.fold_in(key, 3), (blocks,), 0, EXPERTS - 1, dtype=jnp.int32)
        ends = jnp.cumsum(counts, axis=1)
        after = order_in - CAP - warm[:, None]
        rest_index = jnp.sum((after[:, :, None] >= ends[:, None, :]).astype(jnp.int32), axis=2)
        shifted = rest_index + (rest_index >= warm_pick[:, None]).astype(jnp.int32)
        other = jnp.where(order_in < CAP + warm[:, None], warm_pick[:, None], shifted)
        offset = jnp.where(order_in < CAP, 0, 1 + other).astype(jnp.int32)
    labels = (hot[:, None] + offset) % EXPERTS
    shuffles = jax.vmap(lambda one_key: jax.random.permutation(one_key, TOK_DEV))(jax.random.split(jax.random.fold_in(key, 4), blocks)).astype(jnp.int32)
    expert_of = jax.vmap(lambda places, picked: jnp.zeros((TOK_DEV,), jnp.int32).at[places].set(picked))(shuffles, labels)
    picks = jax.random.randint(jax.random.fold_in(key, 5), (blocks, TOK_DEV), 0, VOCAB // EXPERTS, dtype=jnp.int32)
    ids = order[expert_of + EXPERTS * picks]
    return ids.reshape(groups, pieces, ROWS, SPAN).transpose(0, 2, 1, 3).reshape(SEQS, GROUP_TOK).astype(jnp.int32)


def block_levels(rng, dims, cuts, smallest, high):
    def one(position, blocks):
        heights = jax.random.uniform(jax.random.fold_in(jax.random.fold_in(rng, 6), position), (blocks,), jnp.float32, smallest / len(cuts), high / len(cuts))
        return jnp.repeat(jnp.exp(heights), dims[position] // blocks).reshape((-1,) + (1,) * (len(dims) - position - 1))

    loudness = one(*cuts[0])
    for cut in cuts[1:]:
        loudness = loudness * one(*cut)
    return loudness


def scatter_about(key, shape, scale, most, cuts=(), kind=jnp.bfloat16):
    values = jax.random.normal(key, shape, jnp.float32) * scale
    if len(cuts) > 0:
        values = block_levels(key, shape, cuts, -0.22, 0.18) * values
    return jnp.clip(values, min=-most, max=most).astype(kind)


def setup_inputs(seed: int = 0) -> dict:
    splits = jax.random.split(jax.random.key(seed), 14)
    return {
        "tokens": scatter_about(splits[0], (SEQS, GROUP_TOK, D), 1.0, 6.0, ((0, 8), (1, 4))),
        "token_ids": draw_token_ids(jax.random.fold_in(splits[13], 71), 0),
        "hash_table": draw_hash_table(jax.random.fold_in(splits[13], 71), 0),
        "lengths": draw_lengths(jax.random.fold_in(splits[13], 71), 0),
        "gain_attn": jnp.clip(1.0 + 0.1 * jax.random.normal(splits[4], (D,), jnp.float32), 0.5, 1.5),
        "w_query": scatter_about(splits[5], (D, D), D ** -0.5, 0.21875),
        "w_key": scatter_about(splits[6], (D, D), D ** -0.5, 0.21875),
        "w_value": scatter_about(splits[7], (D, D), D ** -0.5, 0.21875),
        "w_output": scatter_about(splits[8], (D, D), (D // 32) ** -0.5, 1.25),
        "gain_ffn": jnp.clip(1.0 + 0.1 * jax.random.normal(splits[9], (D,), jnp.float32), 0.5, 1.5),
        "w_in": scatter_about(splits[10], (EXPERTS, D, FF), D ** -0.5, 0.21875, ((0, 2), (2, 4))),
        "w_out": scatter_about(splits[11], (EXPERTS, FF, D), FF ** -0.5, 0.109375, ((0, 2), (1, 4))),
        "cotangent": scatter_about(splits[12], (SEQS, GROUP_TOK, D), 1.0, 6.0, ((0, 8), (1, 4))),
    }


@jax.custom_vjp
def low(v):
    return lax.optimization_barrier(v.astype(jnp.bfloat16)).astype(jnp.float32)

@jax.custom_vjp
def low_back(v):
    return v

def low_keep(v):
    return (low(v), None)

def low_pass(kept, grad):
    return (grad,)

def back_keep(v):
    return (v, None)

def back_low(kept, grad):
    return (low(grad),)
low.defvjp(low_keep, low_pass)
low_back.defvjp(back_keep, back_low)
epsilon = 1e-05
highest = lax.Precision.HIGHEST
masked_score = -1e+30

def norm_rows(values, gain):
    average = lax.optimization_barrier(jnp.mean(values, axis=-1, keepdims=True))
    centred = values - average
    spread = lax.optimization_barrier(jnp.mean(centred * centred, axis=-1, keepdims=True))
    return centred * lax.rsqrt(spread + epsilon) * gain

def document_numbers(lengths_row, positions):
    ends = jnp.cumsum(lengths_row)
    return lax.optimization_barrier(jnp.sum((positions[:, None] >= ends[None, :]).astype(jnp.int32), axis=1))

def to_blocks(rows_all):
    groups = rows_all.shape[0] // ROWS
    pieces = rows_all.shape[1] // SPAN
    shaped = rows_all.reshape(groups, ROWS, pieces, SPAN, D).transpose(0, 2, 1, 3, 4)
    return shaped.reshape(groups * pieces, ROWS * SPAN, D)

def from_blocks(blocked, shape):
    groups = shape[0] // ROWS
    pieces = shape[1] // SPAN
    shaped = blocked.reshape(groups, pieces, ROWS, SPAN, D).transpose(0, 2, 1, 3, 4)
    return shaped.reshape(shape)

def attend_row(parts):
    query, keys, values, documents = parts
    length = query.shape[0]
    query_heads = query.reshape(length, H, HD).transpose(1, 0, 2)
    key_heads = keys.reshape(length, H, HD).transpose(1, 0, 2)
    value_heads = values.reshape(length, H, HD).transpose(1, 0, 2)
    scores = jnp.einsum('hqd,hkd->hqk', query_heads, key_heads, precision=highest) * HD ** (-0.5)
    scores = low_back(scores)
    positions = jnp.arange(length, dtype=jnp.int32)
    visible = (positions[None, :] <= positions[:, None]) & (documents[:, None] == documents[None, :])
    scores = jnp.where(visible[None], scores, masked_score)
    probs = low(jax.nn.softmax(scores, axis=-1))
    mixed = jnp.einsum('hqk,hkd->hqd', probs, value_heads, precision=highest)
    return mixed.transpose(1, 0, 2).reshape(length, H * HD)

def expert_rows(parts):
    rows_in, weight_in, weight_out = parts
    pre = low_back(jnp.dot(rows_in, weight_in, precision=highest))
    hidden = low(jax.nn.gelu(pre))
    return low(low_back(jnp.dot(hidden, weight_out, precision=highest)))

def slot_plan(expert_of):
    local = expert_of.shape[1]
    labels = jnp.arange(EXPERTS, dtype=jnp.int32)
    onehot = (expert_of[..., None] == labels).astype(jnp.int32)
    own_rank = lax.optimization_barrier(jnp.sum((jnp.cumsum(onehot, axis=1) - 1) * onehot, axis=-1))
    slots = (expert_of * CAP + own_rank).astype(jnp.int32)

    def sources_of(slot_row):
        return jnp.full((EXPERTS * CAP,), local, jnp.int32).at[slot_row].set(jnp.arange(local, dtype=jnp.int32))
    return (slots, jax.vmap(sources_of)(slots))

def forward(tokens, gain_attn, w_query, w_key, w_value, w_output, gain_ffn, w_in, w_out, documents, slots, sources):
    normed = low(norm_rows(tokens, gain_attn))

    def project(weight):
        return low(low_back(jnp.einsum('sgd,de->sge', normed, weight, precision=highest)))
    query = project(w_query)
    keys = project(w_key)
    values = project(w_value)
    mixed = lax.map(jax.checkpoint(attend_row), (query, keys, values, documents))
    attended = low(low_back(mixed))
    middle = tokens + low_back(jnp.einsum('sgd,de->sge', attended, w_output, precision=highest))
    ffn_in = low_back(low(norm_rows(middle, gain_ffn)))
    blocks = sources.shape[0]
    flat_in = to_blocks(ffn_in)
    padded = jnp.concatenate([flat_in, jnp.zeros((blocks, 1, D), flat_in.dtype)], axis=1)
    sent = jnp.take_along_axis(padded, sources[:, :, None], axis=1)
    by_expert = sent.reshape(blocks, EXPERTS, CAP, D).transpose(1, 0, 2, 3).reshape(EXPERTS, blocks * CAP, D)
    produced = lax.map(jax.checkpoint(expert_rows), (by_expert, w_in, w_out))
    back = produced.reshape(EXPERTS, blocks, CAP, D).transpose(1, 0, 2, 3).reshape(blocks, EXPERTS * CAP, D)
    returned = jnp.take_along_axis(back, slots[:, :, None], axis=1)
    return middle + from_blocks(returned, tokens.shape)

def reference(tokens, token_ids, hash_table, lengths, gain_attn, w_query, w_key, w_value, w_output, gain_ffn, w_in, w_out, cotangent):
    length = tokens.shape[1]
    positions = jnp.arange(length, dtype=jnp.int32)
    documents = jax.vmap(lambda lengths_row: document_numbers(lengths_row, positions))(lengths)
    groups = tokens.shape[0] // ROWS
    pieces = length // SPAN
    id_experts = jnp.take(hash_table, token_ids, axis=0).astype(jnp.int32)
    expert_of = id_experts.reshape(groups, ROWS, pieces, SPAN).transpose(0, 2, 1, 3).reshape(groups * pieces, ROWS * SPAN).astype(jnp.int32)
    slots, sources = slot_plan(expert_of)
    floats = [array.astype(jnp.float32) for array in (tokens, gain_attn, w_query, w_key, w_value, w_output, gain_ffn, w_in, w_out)]

    def wrapped(*weights):
        return forward(*weights, documents, slots, sources)
    output, pullback = jax.vjp(wrapped, *floats)
    grads = pullback(cotangent.astype(jnp.float32))
    return (output.astype(jnp.bfloat16), grads[0], grads[1], grads[2], grads[3], grads[4], grads[5], grads[6], grads[7], grads[8])
```

```python
import functools
import jax
import jax.numpy as jnp
from jax import lax
from jax.experimental import pallas as pl
from jax.experimental.pallas import tpu as pltpu
from jax.sharding import PartitionSpec as P

MESH = pl.DeviceIdType.MESH
F32 = jnp.float32
BF16 = jnp.bfloat16
H = 12
HD = 64
epsilon = 1e-05
masked_score = -1e30


def dot_nn(a, b):
    return jnp.dot(a, b, preferred_element_type=F32)


def dot_nt(a, b):
    return lax.dot_general(a, b, (((1,), (1,)), ((), ())), preferred_element_type=F32)


def dot_tn(a, b):
    return lax.dot_general(a, b, (((0,), (0,)), ((), ())), preferred_element_type=F32)


def norm_stats(values):
    average = jnp.mean(values, axis=-1, keepdims=True)
    centred = values - average
    spread = jnp.mean(centred * centred, axis=-1, keepdims=True)
    return centred * lax.rsqrt(spread + epsilon)


def attention_kernel(
    tokens_hbm, lengths_ref, gain_ref, wq_ref, wk_ref, wv_ref, wo_ref,
    middle_ref, att_ref, log_ref,
    nb, wkt, wvt, qs, ks, vs, kt, vt, es, oa, stat, facs,
    local_sem, tok_send, tok_recv, fwd_send, fwd_recv, core_send, core_recv,
):
    dp = lax.axis_index("dp")
    s = lax.axis_index("seq")
    y = lax.axis_index("expert")
    c = lax.rem(s, 2)
    x = s // 2
    core_peer = (dp, x * 2 + 1 - c, y)
    x_peer = (dp, (1 - x) * 2 + c, y)
    span = tokens_hbm.shape[1]

    own_copy = pltpu.make_async_copy(tokens_hbm, nb.at[s], local_sem)
    own_copy.start()
    barrier = pltpu.get_barrier_semaphore()
    for peer in (core_peer, x_peer):
        pl.semaphore_signal(barrier, inc=1, device_id=peer, device_id_type=MESH)
    pl.semaphore_wait(barrier, 2)

    def token_copy(r):
        return pltpu.make_async_remote_copy(
            src_ref=tokens_hbm.at[r], dst_ref=nb.at[s, r], send_sem=tok_send.at[r], recv_sem=tok_recv.at[r],
            device_id=x_peer, device_id_type=MESH)

    def core_copy(r):
        return pltpu.make_async_remote_copy(
            src_ref=tokens_hbm.at[r], dst_ref=nb.at[s, r], send_sem=core_send.at[r], recv_sem=core_recv.at[r],
            device_id=core_peer, device_id_type=MESH)

    def forward_copy(r):
        return pltpu.make_async_remote_copy(
            src_ref=nb.at[c, r], dst_ref=nb.at[c, r], send_sem=fwd_send.at[r], recv_sem=fwd_recv.at[r],
            device_id=core_peer, device_id_type=MESH)

    @pl.when(x == 0)
    def _():
        for r in range(2):
            token_copy(r).start()

    @pl.when(c == 0)
    def _():
        for r in range(2):
            core_copy(r).start()

    wkt[...] = wk_ref[...].T
    wvt[...] = wv_ref[...].T
    gain = gain_ref[...]

    def normalise(part, r):
        nb[part, r] = (norm_stats(nb[part, r].astype(F32)) * gain).astype(BF16)

    def project(part, r):
        normed = nb[part, r]
        ks[part, r] = dot_nn(normed, wk_ref[...]).astype(BF16)
        vs[part, r] = dot_nn(normed, wv_ref[...]).astype(BF16)
        kt[part, r] = dot_nt(wkt[...], normed).astype(BF16)
        vt[part, r] = dot_nt(wvt[...], normed).astype(BF16)

    def attend(r, p, parts, diagonal):
        lanes = pl.ds(pl.multiple_of(p * 128, 128), 128)
        q_pair = qs[r, :, lanes]
        first = lax.broadcasted_iota(jnp.int32, (span, 128), 1) < HD
        results = []
        for hh in range(2):
            q_one = jnp.where(first if hh == 0 else jnp.logical_not(first), q_pair, jnp.zeros_like(q_pair))
            scores = [dot_nt(ks[part, r, :, lanes], q_one) for part in parts]
            if diagonal:
                ki = lax.broadcasted_iota(jnp.int32, (span, span), 0)
                qi = lax.broadcasted_iota(jnp.int32, (span, span), 1)
                scores[-1] = jnp.where(ki <= qi, scores[-1], masked_score)
            peak = jnp.max(scores[0], axis=0, keepdims=True)
            for extra in scores[1:]:
                peak = jnp.maximum(peak, jnp.max(extra, axis=0, keepdims=True))
            total = 0.0
            mixed = 0.0
            h = 2 * p + hh
            rows = pl.ds(pl.multiple_of(p * 128 + hh * HD, HD), HD)
            for part, one in zip(parts, scores):
                weights = jnp.exp(one - peak)
                total = total + jnp.sum(weights, axis=0, keepdims=True)
                low = weights.astype(BF16)
                es[r, h, part] = low
                mixed = mixed + dot_nn(vt[part, r, rows, :], low)
            results.append((h, rows, peak, total, mixed))
        return results

    own_copy.wait()

    def own_rows(r, carry):
        normalise(s, r)
        project(s, r)
        qs[r] = (dot_nn(nb[s, r], wq_ref[...]) * (HD ** -0.5)).astype(BF16)
        return carry

    lax.fori_loop(0, 2, own_rows, 0)

    def near(i, parts):
        r, p = i // 6, lax.rem(i, 6)
        for h, rows, peak, total, mixed in attend(r, p, parts, True):
            stat[r, h, 0] = peak
            stat[r, h, 1] = total
            oa[r, rows, :] = mixed

    @pl.when(c == 0)
    def _():
        def step(i, carry):
            near(i, [s])
            return carry
        lax.fori_loop(0, 12, step, 0)

    @pl.when(c == 1)
    def _():
        for r in range(2):
            core_copy(r).wait_recv()

        def partner_rows(r, carry):
            normalise(s - 1, r)
            project(s - 1, r)
            return carry

        lax.fori_loop(0, 2, partner_rows, 0)

        def step(i, carry):
            near(i, [s - 1, s])
            return carry
        lax.fori_loop(0, 12, step, 0)

    @pl.when(x == 0)
    def _():
        def step(i, carry):
            r, h = i // H, lax.rem(i, H)
            rows = pl.ds(pl.multiple_of(h * HD, HD), HD)
            inverse = 1.0 / stat[r, h, 1]
            facs[r, h, 0] = inverse
            facs[r, h, 1] = jnp.zeros_like(inverse)
            log_ref[r, h] = stat[r, h, 0] + jnp.log(stat[r, h, 1])
            oa[r, rows, :] = oa[r, rows, :] * inverse
            return carry
        lax.fori_loop(0, 2 * H, step, 0)

    @pl.when(x == 1)
    def _():
        for r in range(2):
            token_copy(r).wait_recv()
            normalise(c, r)
            forward_copy(r).start()
            project(c, r)
            forward_copy(r).wait()
            project(1 - c, r)
            single = lengths_ref[r, 1] == 0

            def step(p, carry):
                for h, rows, peak, total, mixed in attend(r, p, [0, 1], False):
                    near_peak = stat[r, h, 0]
                    peak = jnp.where(single, peak, near_peak)
                    top = jnp.maximum(peak, near_peak)
                    near_f = jnp.exp(near_peak - top)
                    far_f = jnp.where(single, jnp.exp(peak - top), 0.0)
                    whole = near_f * stat[r, h, 1] + far_f * total
                    log_ref[r, h] = top + jnp.log(whole)
                    near_f = near_f / whole
                    far_f = far_f / whole
                    facs[r, h, 0] = near_f
                    facs[r, h, 1] = far_f
                    oa[r, rows, :] = oa[r, rows, :] * near_f + mixed * far_f
                return carry
            lax.fori_loop(0, 6, step, 0)

    def out_rows(r, carry):
        att = oa[r].astype(BF16).T
        att_ref[r] = att
        middle_ref[r] = dot_nn(att, wo_ref[...])
        return carry
    lax.fori_loop(0, 2, out_rows, 0)

    @pl.when(x == 0)
    def _():
        for r in range(2):
            token_copy(r).wait_send()

    @pl.when(c == 0)
    def _():
        for r in range(2):
            core_copy(r).wait_send()


def attention(tokens, lengths, gain, wq, wk, wv, wo):
    rows, span, width = tokens.shape
    vmem = pl.BlockSpec(memory_space=pltpu.VMEM)
    sem = pltpu.SemaphoreType.DMA
    blocks = (4, rows, span, width)
    flipped = (4, rows, width, span)
    return pl.pallas_call(
        attention_kernel,
        out_shape=(
            jax.ShapeDtypeStruct((rows, span, width), F32),
            jax.ShapeDtypeStruct((rows, span, width), BF16),
            jax.ShapeDtypeStruct((rows, H, 1, span), F32),
        ),
        in_specs=[pl.BlockSpec(memory_space=pl.ANY), pl.BlockSpec(memory_space=pltpu.SMEM)] + [vmem] * 5,
        out_specs=(vmem, vmem, vmem),
        scratch_shapes=[
            pltpu.VMEM(blocks, BF16),
            pltpu.VMEM((width, width), BF16),
            pltpu.VMEM((width, width), BF16),
            pltpu.VMEM((rows, span, width), BF16),
            pltpu.VMEM(blocks, BF16),
            pltpu.VMEM(blocks, BF16),
            pltpu.VMEM(flipped, BF16),
            pltpu.VMEM(flipped, BF16),
            pltpu.VMEM((rows, H, 4, span, span), BF16),
            pltpu.VMEM((rows, width, span), F32),
            pltpu.VMEM((rows, H, 2, 1, span), F32),
            pltpu.VMEM((rows, H, 2, 1, span), F32),
            sem, sem((2,)), sem((2,)), sem((2,)), sem((2,)), sem((2,)), sem((2,)),
        ],
        compiler_params=pltpu.CompilerParams(collective_id=1, has_side_effects=True, vmem_limit_bytes=60 << 20),
        name="attention_forward",
    )(tokens, lengths, gain.reshape(1, -1), wq, wk, wv, wo)


def norm_rows(values, gain):
    average = jnp.mean(values, axis=-1, keepdims=True)
    centred = values - average
    spread = jnp.mean(centred * centred, axis=-1, keepdims=True)
    return centred * lax.rsqrt(spread + epsilon) * gain


def gelu_grad(pre, upstream):
    unused, pullback = jax.vjp(jax.nn.gelu, pre)
    return pullback(upstream)[0]


def split_heads(matrix):
    return matrix.reshape(matrix.shape[0], matrix.shape[1], H, HD).transpose(2, 0, 1, 3)


def join_heads(stacked):
    return stacked.transpose(1, 2, 0, 3).reshape(stacked.shape[1], stacked.shape[2], H * HD)


def per_device(
    tokens,
    token_ids,
    hash_table,
    lengths,
    gain_attn,
    w_query,
    w_key,
    w_value,
    w_output,
    gain_ffn,
    w_in,
    w_out,
    cotangent,
):
    row_count, span, width = tokens.shape
    local_tok = row_count * span
    whole = span * lax.axis_size("seq")
    place = lax.axis_index("seq")
    scale = HD ** (-0.5)
    inputs = tokens.reshape(local_tok, width).astype(jnp.float32)
    key_positions = jnp.arange(whole, dtype=jnp.int32)
    query_positions = place * span + jnp.arange(span, dtype=jnp.int32)
    ends = jnp.cumsum(lengths, axis=1)
    key_document = jnp.sum(
        (key_positions[None, :, None] >= ends[:, None, :]).astype(jnp.int32), axis=2
    )
    query_document = jnp.sum(
        (query_positions[None, :, None] >= ends[:, None, :]).astype(jnp.int32), axis=2
    )
    visible = (key_positions[None, None, :] <= query_positions[None, :, None]) & (
        query_document[:, :, None] == key_document[:, None, :]
    )
    normed, first_norm_back = jax.vjp(norm_rows, inputs, gain_attn)
    normed_low = normed.astype(jnp.bfloat16)
    query = jnp.dot(normed_low, w_query, preferred_element_type=jnp.float32).astype(jnp.bfloat16)
    keys = jnp.dot(normed_low, w_key, preferred_element_type=jnp.float32).astype(jnp.bfloat16)
    values = jnp.dot(normed_low, w_value, preferred_element_type=jnp.float32).astype(jnp.bfloat16)
    own_pair = jnp.concatenate([keys, values], axis=1).reshape(row_count, span, 2 * width)

    def pair_heads(pairs):
        return (split_heads(pairs[:, :, :width]), split_heads(pairs[:, :, width:]))

    query_heads = split_heads(query.reshape(row_count, span, width))
    projected, attended, log_rows = attention(tokens, lengths, gain_attn, w_query, w_key, w_value, w_output)
    attended = attended.reshape(local_tok, width)
    log_totals = log_rows.transpose(1, 0, 2, 3).reshape(H, row_count, span)
    middle = inputs + projected.reshape(local_tok, width)
    ffn_norm, second_norm_back = jax.vjp(norm_rows, middle, gain_ffn)
    ffn_in = ffn_norm.astype(jnp.bfloat16)
    experts = lax.axis_size("expert")
    capacity = min(2 * local_tok // experts, 3 * local_tok // 4)
    expert_of = jnp.take(hash_table, token_ids.reshape(local_tok), axis=0)
    labels = jnp.arange(experts, dtype=jnp.int32)
    onehot = (expert_of[:, None] == labels[None, :]).astype(jnp.int32)
    own_rank = jnp.sum((jnp.cumsum(onehot, axis=0) - 1) * onehot, axis=1)
    slots = expert_of * capacity + own_rank
    sources = (
        jnp.full((experts * capacity,), local_tok, jnp.int32)
        .at[slots]
        .set(jnp.arange(local_tok, dtype=jnp.int32))
    )

    def to_slots(rows_low):
        padded = jnp.concatenate([rows_low, jnp.zeros((1, width), rows_low.dtype)], axis=0)
        return jnp.take(padded, sources, axis=0).reshape(experts, capacity, width)

    received = lax.all_to_all(
        to_slots(ffn_in), "expert", split_axis=0, concat_axis=0, tiled=True
    ).reshape(-1, width)
    full_in, full_out = (
        lax.all_gather(w_in, "seq", axis=2, tiled=True),
        lax.all_gather(w_out, "seq", axis=1, tiled=True),
    )
    full_in = full_in[0]
    full_out = full_out[0]
    first = jnp.dot(received, full_in, preferred_element_type=jnp.float32)
    produced = jnp.dot(
        jax.nn.gelu(first).astype(jnp.bfloat16), full_out, preferred_element_type=jnp.float32
    ).astype(jnp.bfloat16)
    returned = lax.all_to_all(
        produced.reshape(experts, capacity, width),
        "expert",
        split_axis=0,
        concat_axis=0,
        tiled=True,
    ).reshape(-1, width)
    output = middle + jnp.take(returned, slots, axis=0).astype(jnp.float32)
    upstream = cotangent.reshape(local_tok, width)
    grad_received_out = lax.all_to_all(
        to_slots(upstream), "expert", split_axis=0, concat_axis=0, tiled=True
    ).reshape(-1, width)
    pre = jnp.dot(received, full_in, preferred_element_type=jnp.float32)
    hidden = jax.nn.gelu(pre).astype(jnp.bfloat16)
    grad_full_out = jnp.einsum(
        "rf,rd->fd", hidden, grad_received_out, preferred_element_type=jnp.float32
    )
    grad_hidden = jnp.einsum(
        "rd,fd->rf", grad_received_out, full_out, preferred_element_type=jnp.float32
    )
    grad_pre = gelu_grad(pre, grad_hidden).astype(jnp.bfloat16)
    grad_full_in = jnp.einsum("rd,rf->df", received, grad_pre, preferred_element_type=jnp.float32)
    grad_received = jnp.einsum(
        "rf,df->rd", grad_pre, full_in, preferred_element_type=jnp.float32
    ).astype(jnp.bfloat16)
    grad_in_part, grad_out_part = (
        lax.psum_scatter(
            grad_full_in[None].astype(jnp.bfloat16), "seq", scatter_dimension=2, tiled=True
        ).astype(jnp.float32),
        lax.psum_scatter(
            grad_full_out[None].astype(jnp.bfloat16), "seq", scatter_dimension=1, tiled=True
        ).astype(jnp.float32),
    )
    grad_in, grad_out = (
        lax.psum(grad_in_part.astype(jnp.bfloat16), "dp").astype(jnp.float32),
        lax.psum(grad_out_part.astype(jnp.bfloat16), "dp").astype(jnp.float32),
    )
    grad_back = lax.all_to_all(
        grad_received.reshape(experts, capacity, width),
        "expert",
        split_axis=0,
        concat_axis=0,
        tiled=True,
    ).reshape(-1, width)
    grad_ffn_in = jnp.take(grad_back, slots, axis=0).astype(jnp.float32)
    grad_middle_norm, grad_gain_ffn = second_norm_back(grad_ffn_in)
    grad_middle = upstream.astype(jnp.float32) + grad_middle_norm
    grad_branch = grad_middle.astype(jnp.bfloat16)
    grad_w_output = jnp.einsum(
        "cd,ce->de", attended, grad_branch, preferred_element_type=jnp.float32
    )
    grad_attended = jnp.einsum(
        "ce,de->cd", grad_branch, w_output, preferred_element_type=jnp.float32
    ).astype(jnp.bfloat16)
    again_pairs = lax.all_gather(own_pair, "seq", axis=1, tiled=True)
    key_back, value_back = pair_heads(again_pairs)

    def head_backward(parts):
        query_one, key_one, value_one, grad_one, log_one = parts
        scores = (
            jnp.einsum("rqd,rkd->rqk", query_one, key_one, preferred_element_type=jnp.float32)
            * scale
        )
        scores = jnp.where(visible, scores, masked_score)
        probs_full = jnp.exp(scores - log_one[:, :, None])
        probs = probs_full.astype(jnp.bfloat16)
        grad_probs = jnp.einsum(
            "rqd,rkd->rqk", grad_one, value_one, preferred_element_type=jnp.float32
        )
        inner = jnp.sum(probs_full * grad_probs, axis=2, keepdims=True)
        grad_scores = (probs_full * (grad_probs - inner)).astype(jnp.bfloat16)
        grad_query_one = (
            jnp.einsum("rqk,rkd->rqd", grad_scores, key_one, preferred_element_type=jnp.float32)
            * scale
        )
        grad_key_one = (
            jnp.einsum("rqk,rqd->rkd", grad_scores, query_one, preferred_element_type=jnp.float32)
            * scale
        )
        grad_value_one = jnp.einsum(
            "rqk,rqd->rkd", probs, grad_one, preferred_element_type=jnp.float32
        )
        return (grad_query_one, grad_key_one, grad_value_one)

    grad_att_heads = split_heads(grad_attended.reshape(row_count, span, width))
    grad_query_heads, grad_key_heads, grad_value_heads = lax.map(
        head_backward, (query_heads, key_back, value_back, grad_att_heads, log_totals)
    )
    grad_query_rows = join_heads(grad_query_heads).reshape(local_tok, width).astype(jnp.bfloat16)
    pair_grads = jnp.concatenate([join_heads(grad_key_heads), join_heads(grad_value_heads)], axis=2)
    own_grads = (
        lax.psum_scatter(pair_grads, "seq", scatter_dimension=1, tiled=True)
        .reshape(local_tok, 2 * width)
        .astype(jnp.bfloat16)
    )
    grad_key_rows = own_grads[:, :width]
    grad_value_rows = own_grads[:, width:]
    grad_w_query = jnp.einsum(
        "cd,ce->de", normed_low, grad_query_rows, preferred_element_type=jnp.float32
    )
    grad_w_key = jnp.einsum(
        "cd,ce->de", normed_low, grad_key_rows, preferred_element_type=jnp.float32
    )
    grad_w_value = jnp.einsum(
        "cd,ce->de", normed_low, grad_value_rows, preferred_element_type=jnp.float32
    )
    grad_normed = jnp.einsum(
        "ce,de->cd", grad_query_rows, w_query, preferred_element_type=jnp.float32
    )
    grad_normed = grad_normed + jnp.einsum(
        "ce,de->cd", grad_key_rows, w_key, preferred_element_type=jnp.float32
    )
    grad_normed = grad_normed + jnp.einsum(
        "ce,de->cd", grad_value_rows, w_value, preferred_element_type=jnp.float32
    )
    grad_inputs_norm, grad_gain_attn = first_norm_back(grad_normed)
    input_grad = grad_middle + grad_inputs_norm
    summed = lax.psum(
        (grad_gain_attn, grad_w_query, grad_w_key, grad_w_value, grad_w_output, grad_gain_ffn),
        ("dp", "seq", "expert"),
    )
    shaped_output = output.astype(jnp.bfloat16).reshape(row_count, span, width)
    shaped_grad = input_grad.reshape(row_count, span, width)
    return (
        shaped_output,
        shaped_grad,
        summed[0],
        summed[1],
        summed[2],
        summed[3],
        summed[4],
        summed[5],
        grad_in,
        grad_out,
    )


def solution(mesh):
    return jax.shard_map(
        per_device,
        mesh=mesh,
        in_specs=(
            P(("dp", "expert"), "seq", None),
            P(("dp", "expert"), "seq"),
            P(),
            P(("dp", "expert"), None),
            P(),
            P(),
            P(),
            P(),
            P(),
            P(),
            P("expert", None, "seq"),
            P("expert", "seq", None),
            P(("dp", "expert"), "seq", None),
        ),
        out_specs=(
            P(("dp", "expert"), "seq", None),
            P(("dp", "expert"), "seq", None),
            P(),
            P(),
            P(),
            P(),
            P(),
            P(),
            P("expert", None, "seq"),
            P("expert", "seq", None),
        ),
        check_vma=False,
    )
```

```python
import functools
import jax
import jax.numpy as jnp
from jax import lax
from jax.experimental import pallas as pl
from jax.experimental.pallas import tpu as pltpu
from jax.sharding import PartitionSpec as P

MESH = pl.DeviceIdType.MESH
F32 = jnp.float32
BF16 = jnp.bfloat16
I32 = jnp.int32
H = 12
HD = 64
epsilon = 1e-05
masked_score = -1e30
gelu_a = 0.7978845608028654
gelu_b = 0.044715


def dot_nn(a, b):
    return jnp.dot(a, b, preferred_element_type=F32)


def dot_nt(a, b):
    return lax.dot_general(a, b, (((1,), (1,)), ((), ())), preferred_element_type=F32)


def dot_tn(a, b):
    return lax.dot_general(a, b, (((0,), (0,)), ((), ())), preferred_element_type=F32)


def norm_parts(values):
    average = jnp.mean(values, axis=-1, keepdims=True)
    centred = values - average
    spread = jnp.mean(centred * centred, axis=-1, keepdims=True)
    root = lax.rsqrt(spread + epsilon)
    return centred * root, root


def norm_back(upstream, gain, xhat, root):
    scaled = upstream * gain
    first = jnp.mean(scaled, axis=-1, keepdims=True)
    second = jnp.mean(scaled * xhat, axis=-1, keepdims=True)
    return root * (scaled - first - xhat * second)


def block_kernel(
    tokens_hbm, cot_ref, ids_ref, table_ref, lengths_ref, gain_a_ref, gain_f_ref,
    wq_ref, wk_ref, wv_ref, wo_ref, win_hbm, wout_hbm,
    out_hbm, ig_hbm, dwq_hbm, dwk_hbm, dwv_hbm, dwo_hbm, dwin_hbm, dwout_hbm, gg_ref, es_hbm,
    nb, xgb, eob, qs, ks, vs, dot, ebuf, oa, stat, facs, dl, route, cs, xs, stage, do, mid,
    win, wout, acc, preg, hid, gp, gback, eback, dnr0, dnr1,
    local_sem, e_sem, tok_send, tok_recv, fwd_send, fwd_recv, core_send, core_recv,
    wx_send, wx_recv, wc_send, wc_recv, y_send, y_recv, dn_send, dn_recv, dw_sem,
):
    dp = lax.axis_index("dp")
    s = lax.axis_index("seq")
    y = lax.axis_index("expert")
    c = lax.rem(s, 2)
    x = s // 2
    core_peer = (dp, x * 2 + 1 - c, y)
    x_peer = (dp, (1 - x) * 2 + c, y)
    y_peer = (dp, s, 1 - y)
    span = tokens_hbm.shape[1]
    width = tokens_hbm.shape[2]
    local = 2 * span
    cap = stage.shape[0]

    def remote(src, dst, send, recv, peer):
        return pltpu.make_async_remote_copy(
            src_ref=src, dst_ref=dst, send_sem=send, recv_sem=recv, device_id=peer, device_id_type=MESH)

    own_copy = pltpu.make_async_copy(tokens_hbm, nb.at[s], local_sem.at[0])
    win_copy = pltpu.make_async_copy(win_hbm, win.at[s], local_sem.at[1])
    wout_copy = pltpu.make_async_copy(wout_hbm, wout.at[s], local_sem.at[2])
    own_copy.start()
    win_copy.start()
    wout_copy.start()
    barrier = pltpu.get_barrier_semaphore()
    for peer in (core_peer, x_peer, y_peer):
        pl.semaphore_signal(barrier, inc=1, device_id=peer, device_id_type=MESH)
    pl.semaphore_wait(barrier, 3)

    far_s = (1 - x) * 2 + c

    def token_copy(r):
        return remote(tokens_hbm.at[r], nb.at[s, r], tok_send.at[r], tok_recv.at[r], x_peer)

    def core_copy(r):
        return remote(tokens_hbm.at[r], nb.at[s, r], core_send.at[r], core_recv.at[r], core_peer)

    def forward_copy(r):
        return remote(nb.at[c, r], nb.at[c, r], fwd_send.at[r], fwd_recv.at[r], core_peer)

    wx_copies = [
        remote(win_hbm, win.at[s], wx_send.at[0], wx_recv.at[0], x_peer),
        remote(wout_hbm, wout.at[s], wx_send.at[1], wx_recv.at[1], x_peer),
    ]
    wc_copies = [
        remote(win_hbm, win.at[s], wc_send.at[0], wc_recv.at[0], core_peer),
        remote(wout_hbm, wout.at[s], wc_send.at[1], wc_recv.at[1], core_peer),
        remote(win.at[far_s], win.at[far_s], wc_send.at[2], wc_recv.at[2], core_peer),
        remote(wout.at[far_s], wout.at[far_s], wc_send.at[3], wc_recv.at[3], core_peer),
    ]

    @pl.when(x == 0)
    def _():
        for r in range(2):
            token_copy(r).start()

    @pl.when(x == 1)
    def _():
        for one in wx_copies:
            one.start()

    @pl.when(c == 0)
    def _():
        for r in range(2):
            core_copy(r).start()

    wc_copies[0].start()
    wc_copies[1].start()

    ids = jnp.concatenate([ids_ref[0:1, :], ids_ref[1:2, :]], axis=1)
    high = ids // 128
    low = ids - high * 128
    pick = jnp.where(lax.broadcasted_iota(I32, (64, local), 0) == high, 1.0, 0.0).astype(BF16)
    looked = dot_tn(table_ref[...].astype(F32).astype(BF16), pick)
    expert_row = jnp.sum(
        jnp.where(lax.broadcasted_iota(I32, (128, local), 0) == low, looked, 0.0), axis=0, keepdims=True)
    mine = jnp.where(expert_row == y.astype(F32), 1.0, 0.0)
    sixteen = lax.broadcasted_iota(I32, (16, local), 0)
    both = jnp.where(sixteen == 0, mine, jnp.where(sixteen == 1, 1.0 - mine, 0.0)).astype(BF16)
    before = jnp.where(
        lax.broadcasted_iota(I32, (local, local), 0) < lax.broadcasted_iota(I32, (local, local), 1), 1.0, 0.0
    ).astype(BF16)
    ranks = dot_nn(both, before)
    slot_rows = lax.broadcasted_iota(I32, (cap, local), 0).astype(F32)
    for u in range(2):
        chosen = mine if u == 0 else 1.0 - mine
        route[u] = jnp.where(slot_rows == ranks[u:u + 1, :], chosen, 0.0).astype(BF16)

    cot_copy = remote(stage, cs.at[cap:], y_send.at[0], y_recv.at[0], y_peer)
    xs_copy = remote(stage, xs.at[cap:], y_send.at[1], y_recv.at[1], y_peer)
    stage[...] = dot_nn(route[1], cot_ref[...]).astype(BF16)
    cot_copy.start()
    cs[0:cap] = dot_nn(route[0], cot_ref[...]).astype(BF16)

    gain_a = gain_a_ref[...]
    gain_f = gain_f_ref[...]

    def normalise(part, r):
        nb[part, r] = (norm_parts(nb[part, r].astype(F32))[0] * gain_a).astype(BF16)

    def project(part, r):
        normed = nb[part, r]
        ks[part, r] = dot_nn(normed, wk_ref[...]).astype(BF16)
        vs[part, r] = dot_nn(normed, wv_ref[...]).astype(BF16)

    first_half = lax.broadcasted_iota(I32, (span, 128), 1) < HD
    first_rows = lax.broadcasted_iota(I32, (128, span), 0) < HD

    def only(values, keep, hh):
        return jnp.where(keep if hh == 0 else jnp.logical_not(keep), values, jnp.zeros_like(values))

    def pair_lanes(p):
        return pl.ds(pl.multiple_of(p * 128, 128), 128)

    def head_rows(p, hh):
        return pl.ds(pl.multiple_of(p * 128 + hh * HD, HD), HD)

    def e_near(r, p, slot, write, both_parts):
        here = ebuf.at[slot] if both_parts else ebuf.at[slot, :, 1]
        there = es_hbm.at[0, r, p] if both_parts else es_hbm.at[0, r, p, :, 1]
        return pltpu.make_async_copy(here if write else there, there if write else here, e_sem.at[slot])

    def e_far(r, p, slot, write):
        here = ebuf.at[slot]
        there = es_hbm.at[1, r, p]
        return pltpu.make_async_copy(here if write else there, there if write else here, e_sem.at[slot])

    def attend(r, p, slot, parts, places, diagonal):
        lanes = pair_lanes(p)
        q_pair = qs[r, :, lanes]
        v_flipped = [vs[part, r, :, lanes].T for part in parts]
        results = []
        for hh in range(2):
            q_one = only(q_pair, first_half, hh)
            scores = [dot_nt(ks[part, r, :, lanes], q_one) for part in parts]
            if diagonal:
                ki = lax.broadcasted_iota(I32, (span, span), 0)
                qi = lax.broadcasted_iota(I32, (span, span), 1)
                scores[-1] = jnp.where(ki <= qi, scores[-1], masked_score)
            peak = jnp.max(scores[0], axis=0, keepdims=True)
            for extra in scores[1:]:
                peak = jnp.maximum(peak, jnp.max(extra, axis=0, keepdims=True))
            total = 0.0
            mixed = 0.0
            rows = head_rows(p, hh)
            for v_one, place, one in zip(v_flipped, places, scores):
                weights = jnp.exp(one - peak)
                total = total + jnp.sum(weights, axis=0, keepdims=True)
                low_weights = weights.astype(BF16)
                ebuf[slot, hh, place] = low_weights
                mixed = mixed + dot_nn(v_one[hh * HD:(hh + 1) * HD], low_weights)
            results.append((2 * p + hh, rows, peak, total, mixed))
        return results

    own_copy.wait()

    def own_rows(r, carry):
        mid[r] = nb[s, r].astype(F32)
        normalise(s, r)
        project(s, r)
        qs[r] = (dot_nn(nb[s, r], wq_ref[...]) * (HD ** -0.5)).astype(BF16)
        return carry

    lax.fori_loop(0, 2, own_rows, 0)

    def near_loop(parts, places):
        wide = len(parts) == 2

        def step(i, carry):
            r, p, slot = i // 6, lax.rem(i, 6), lax.rem(i, 2)

            @pl.when(i >= 2)
            def _():
                e_near(r, p, slot, True, wide).wait()

            for h, rows, peak, total, mixed in attend(r, p, slot, parts, places, True):
                stat[r, h, 0] = peak
                stat[r, h, 1] = total
                oa[r, rows, :] = mixed
            e_near(r, p, slot, True, wide).start()
            return carry

        lax.fori_loop(0, 12, step, 0)
        for slot in range(2):
            e_near(1, 4 + slot, slot, True, wide).wait()

    @pl.when(c == 0)
    def _():
        near_loop([s], [1])

    @pl.when(c == 1)
    def _():
        for r in range(2):
            core_copy(r).wait_recv()

        def partner_rows(r, carry):
            normalise(s - 1, r)
            project(s - 1, r)
            return carry

        lax.fori_loop(0, 2, partner_rows, 0)
        near_loop([s - 1, s], [0, 1])

    @pl.when(x == 0)
    def _():
        for r in range(2):
            token_copy(r).wait_send()
        for one in wx_copies:
            one.start()

        def step(i, carry):
            r, h = i // H, lax.rem(i, H)
            rows = pl.ds(pl.multiple_of(h * HD, HD), HD)
            inverse = 1.0 / stat[r, h, 1]
            facs[r, h, 0] = inverse
            facs[r, h, 1] = jnp.zeros_like(inverse)
            oa[r, rows, :] = oa[r, rows, :] * inverse
            return carry

        lax.fori_loop(0, 2 * H, step, 0)

    @pl.when(x == 1)
    def _():
        for r in range(2):
            token_copy(r).wait_recv()
            normalise(c, r)
            forward_copy(r).start()
            project(c, r)
            forward_copy(r).wait()
            project(1 - c, r)
            single = lengths_ref[r, 1] == 0

            def step(p, carry):
                slot = lax.rem(p, 2)

                @pl.when(p >= 2)
                def _():
                    e_far(r, p, slot, True).wait()

                for h, rows, peak, total, mixed in attend(r, p, slot, [0, 1], [0, 1], False):
                    near_peak = stat[r, h, 0]
                    peak = jnp.where(single, peak, near_peak)
                    top = jnp.maximum(peak, near_peak)
                    near_f = jnp.exp(near_peak - top)
                    far_f = jnp.where(single, jnp.exp(peak - top), 0.0)
                    whole = near_f * stat[r, h, 1] + far_f * total
                    near_f = near_f / whole
                    far_f = far_f / whole
                    facs[r, h, 0] = near_f
                    facs[r, h, 1] = far_f
                    oa[r, rows, :] = oa[r, rows, :] * near_f + mixed * far_f
                e_far(r, p, slot, True).start()
                return carry

            lax.fori_loop(0, 6, step, 0)
            for slot in range(2):
                e_far(r, 4 + slot, slot, True).wait()

    def out_rows(r, carry):
        att = oa[r].astype(BF16).T
        value = mid[r] + dot_nn(att, wo_ref[...])
        mid[r] = value
        do[0, r] = (norm_parts(value)[0] * gain_f).astype(BF16)
        return carry

    lax.fori_loop(0, 2, out_rows, 0)

    ffn_in = do[0].reshape(local, width)
    cot_copy.wait_send()
    stage[...] = dot_nn(route[1], ffn_in).astype(BF16)
    xs_copy.start()
    xs[0:cap] = dot_nn(route[0], ffn_in).astype(BF16)
    win_copy.wait()
    wout_copy.wait()
    acc[...] = jnp.zeros_like(acc)

    def expert_rows(u, f):
        rows = slice(u * cap, (u + 1) * cap)
        preg[0] = dot_nn(xs[rows], win[f])
        preg[1] = dot_nt(cs[rows], wout[f])

        def gelu_rows(k, carry):
            piece = pl.ds(pl.multiple_of(k * 16, 16), 16)
            where = pl.ds(pl.multiple_of(u * cap + k * 16, 16), 16)
            pre = preg[0, piece]
            square = pre * pre
            bent = jnp.tanh(gelu_a * pre * (1.0 + gelu_b * square))
            half = 0.5 * (1.0 + bent)
            slope = half + 0.5 * pre * (1.0 - bent * bent) * (gelu_a * (1.0 + 3.0 * gelu_b * square))
            hid[f, where] = (pre * half).astype(BF16)
            gp[f, where] = (preg[1, piece] * slope).astype(BF16)
            return carry

        lax.fori_loop(0, cap // 16, gelu_rows, 0, unroll=2)
        acc[rows] += dot_nt(gp[f, rows], win[f])

    def expert_number(ix, ic):
        return 2 * lax.rem(x + ix, 2) + lax.rem(c + ic, 2)

    def far_weights():
        for k in range(2):
            wx_copies[k].wait_recv()
            wc_copies[2 + k].start()

    for ix in range(2):
        if ix == 1:
            far_weights()
        for u in range(2):
            if ix == 0 and u == 1:
                xs_copy.wait_recv()
                cot_copy.wait_recv()

            def two(ic, carry):
                @pl.when(ic == 1)
                def _():
                    if u == 0:
                        for k in range(2):
                            wc_copies[2 * ix + k].wait_recv()
                expert_rows(u, expert_number(ix, ic))
                return carry

            lax.fori_loop(0, 2, two, 0)

    grad_copy = remote(xgb.at[cap:], gback, y_send.at[2], y_recv.at[2], y_peer)
    out_copy = remote(eob.at[cap:], eback, y_send.at[3], y_recv.at[3], y_peer)
    xgb[...] = acc[...].astype(BF16)
    grad_copy.start()
    acc[...] = jnp.zeros_like(acc)
    wc_copies[0].wait_send()
    wc_copies[1].wait_send()
    wc_copies[2].wait_send()
    wc_copies[3].wait_send()

    def weight_grads(i, carry):
        f = expert_number(1 - i // 2, lax.rem(i, 2))
        acc[...] += dot_nn(hid[f], wout[f])
        wout[f] = dot_tn(hid[f], cs[...]).astype(BF16)
        win[f] = dot_tn(xs[...], gp[f]).astype(BF16)
        pltpu.make_async_copy(wout.at[f], dwout_hbm.at[f], dw_sem.at[0, f]).start()
        pltpu.make_async_copy(win.at[f], dwin_hbm.at[f], dw_sem.at[1, f]).start()
        return carry

    lax.fori_loop(0, 4, weight_grads, 0)
    eob[...] = acc[...].astype(BF16)
    out_copy.start()

    grad_copy.wait_recv()
    acc[...] = jnp.zeros_like(acc)
    gg_ref[...] = jnp.zeros_like(gg_ref)

    def take_back(r, own, returned):
        picked = pl.ds(pl.multiple_of(r * span, span), span)
        return dot_tn(route[0, :, picked], own) + dot_tn(route[1, :, picked], returned)

    def ffn_back(r, carry):
        rows = pl.ds(pl.multiple_of(r * span, span), span)
        grad = take_back(r, xgb[0:cap], gback[...])
        xhat, root = norm_parts(mid[r])
        gg_ref[0:1] += jnp.sum(grad * xhat, axis=0, keepdims=True)
        whole = cot_ref[rows].astype(F32) + norm_back(grad, gain_f, xhat, root)
        preg_rows = preg.at[r, 0:span]
        preg_rows[...] = whole
        branch = whole.astype(BF16)
        att = oa[r]
        acc[...] += dot_nn(att.astype(BF16), branch)
        up = dot_nt(wo_ref[...], branch)
        up3 = up.reshape(H, HD, span)
        inner = jnp.sum(up3 * att.reshape(H, HD, span), axis=1, keepdims=True)
        for g in range(2):
            factor = facs[r, :, g]
            dl[r, :, g] = inner * factor
            flipped = (up3 * factor).reshape(width, span).astype(BF16)
            dot[g, r] = flipped
            do[g, r] = flipped.T
        oa[r] = jnp.zeros_like(oa[r])
        return carry

    lax.fori_loop(0, 2, ffn_back, 0)
    dwo_out = pltpu.make_async_copy(xs, dwo_hbm, local_sem.at[3])
    xs[...] = acc[...].astype(BF16)
    dwo_out.start()

    def attend_back(r, p, slot, g, parts, places):
        lanes = pair_lanes(p)
        q_pair = qs[r, :, lanes]
        do_pair = do[g, r, :, lanes]
        dot_pair = dot[g, r, lanes, :]
        for part, place in zip(parts, places):
            v_pair = vs[part, r, :, lanes]
            k_flipped = ks[part, r, :, lanes].T
            grad_k = 0.0
            grad_v = 0.0
            for hh in range(2):
                h = 2 * p + hh
                rows = head_rows(p, hh)
                weights = ebuf[slot, hh, place]
                grad_p = dot_nn(v_pair, only(dot_pair, first_rows, hh))
                grad_s = (weights.astype(F32) * (grad_p - dl[r, h, g])).astype(BF16)
                grad_v = grad_v + dot_nn(weights, only(do_pair, first_half, hh))
                grad_k = grad_k + dot_nn(grad_s, only(q_pair, first_half, hh))
                oa[r, rows, :] += dot_nn(k_flipped[hh * HD:(hh + 1) * HD], grad_s)
            place_rows = pl.ds(pl.multiple_of(r * span, span), span)
            hid[part, place_rows, lanes] = grad_k.astype(BF16)
            gp[part, place_rows, lanes] = grad_v.astype(BF16)

    def back_loop(g, parts, places):
        wide = len(parts) == 2

        def fetch(i):
            r, p, slot = i // 6, lax.rem(i, 6), lax.rem(i, 2)
            return e_near(r, p, slot, False, wide) if g == 0 else e_far(r, p, slot, False)

        fetch(0).start()

        def step(i, carry):
            @pl.when(i < 11)
            def _():
                fetch(i + 1).start()
            fetch(i).wait()
            attend_back(i // 6, lax.rem(i, 6), lax.rem(i, 2), g, parts, places)
            return carry

        lax.fori_loop(0, 12, step, 0)

    def normed_grad(part):
        return dot_nt(hid[part, 0:local], wk_ref[...]) + dot_nt(gp[part, 0:local], wv_ref[...])

    far_core = remote(cs.at[0:local], dnr0, dn_send.at[0], dn_recv.at[0], core_peer)
    far_x = remote(cs.at[0:local], dnr0, dn_send.at[1], dn_recv.at[1], x_peer)
    near_core = remote(xgb.at[0:local], dnr1, dn_send.at[2], dn_recv.at[2], core_peer)

    @pl.when(x == 1)
    def _():
        back_loop(1, [0, 1], [0, 1])
        cs[0:local] = normed_grad(1 - c).astype(BF16)
        far_core.start()
        mine_far = normed_grad(c)
        far_core.wait()
        cs[0:local] = (mine_far + dnr0[...].astype(F32)).astype(BF16)
        far_x.start()

    grad_copy.wait_send()

    @pl.when(c == 0)
    def _():
        back_loop(0, [s], [1])

    @pl.when(c == 1)
    def _():
        back_loop(0, [s - 1, s], [0, 1])
        xgb[0:local] = normed_grad(s - 1).astype(BF16)
        near_core.start()

    out_copy.wait()

    def out_add(r, carry):
        rows = pl.ds(pl.multiple_of(r * span, span), span)
        do[0, r] = (mid[r] + take_back(r, eob[0:cap], eback[...])).astype(BF16)
        return carry

    lax.fori_loop(0, 2, out_add, 0)
    out_done = pltpu.make_async_copy(do.at[0], out_hbm, local_sem.at[4])
    out_done.start()

    tokens_again = pltpu.make_async_copy(tokens_hbm, do.at[1], local_sem.at[0])
    tokens_again.start()
    for r in range(2):
        qs[r] = (oa[r] * (HD ** -0.5)).astype(BF16).T

    def all_parts(grads):
        acc[...] = jnp.zeros_like(acc)

        def step(part, carry):
            acc[...] += dot_tn(nb[part].reshape(local, width), grads[part, 0:local])
            return carry

        @pl.when(x == 1)
        def _():
            lax.fori_loop(0, 2, step, 0)

        @pl.when(c == 1)
        def _():
            step(s - 1, 0)

        step(s, 0)

    all_parts(hid)
    dwo_out.wait()
    xs[...] = acc[...].astype(BF16)
    dwk_out = pltpu.make_async_copy(xs, dwk_hbm, local_sem.at[3])
    dwk_out.start()
    all_parts(gp)
    dwk_out.wait()
    xs[...] = acc[...].astype(BF16)
    dwv_out = pltpu.make_async_copy(xs, dwv_hbm, local_sem.at[3])
    dwv_out.start()
    query_grads = qs[...].reshape(local, width)
    acc[...] = dot_tn(nb[s].reshape(local, width), query_grads)
    dwv_out.wait()
    xs[...] = acc[...].astype(BF16)
    dwq_out = pltpu.make_async_copy(xs, dwq_hbm, local_sem.at[3])
    dwq_out.start()
    acc[0:local] = normed_grad(s) + dot_nt(query_grads, wq_ref[...])

    @pl.when(c == 0)
    def _():
        near_core.wait_recv()
        acc[0:local] += dnr1[...].astype(F32)

    @pl.when(x == 0)
    def _():
        far_x.wait_recv()
        acc[0:local] += dnr0[...].astype(F32)

    tokens_again.wait()

    def first_back(r, carry):
        rows = pl.ds(pl.multiple_of(r * span, span), span)
        grad = acc[rows]
        xhat, root = norm_parts(do[1, r].astype(F32))
        gg_ref[1:2] += jnp.sum(grad * xhat, axis=0, keepdims=True)
        mid[r] = preg[r, 0:span] + norm_back(grad, gain_a, xhat, root)
        return carry

    lax.fori_loop(0, 2, first_back, 0)
    ig_done = pltpu.make_async_copy(mid, ig_hbm, local_sem.at[0])
    ig_done.start()
    ig_done.wait()
    out_done.wait()
    dwq_out.wait()
    for f in range(4):
        pltpu.make_async_copy(wout.at[f], dwout_hbm.at[f], dw_sem.at[0, f]).wait()
        pltpu.make_async_copy(win.at[f], dwin_hbm.at[f], dw_sem.at[1, f]).wait()
    xs_copy.wait_send()
    for one in wx_copies:
        one.wait_send()

    @pl.when(x == 1)
    def _():
        far_x.wait_send()

    @pl.when(c == 1)
    def _():
        near_core.wait_send()

    @pl.when(c == 0)
    def _():
        for r in range(2):
            core_copy(r).wait_send()


def block(tokens, cot, ids, table, lengths, gain_a, gain_f, wq, wk, wv, wo, w_in, w_out):
    rows, span, width = tokens.shape
    local = rows * span
    cap = 3 * local // 4
    vmem = pl.BlockSpec(memory_space=pltpu.VMEM)
    hbm = pl.BlockSpec(memory_space=pl.ANY)
    smem = pl.BlockSpec(memory_space=pltpu.SMEM)
    sem = pltpu.SemaphoreType.DMA
    square = (width, width)
    blocks = (4, rows, span, width)
    flipped = (2, rows, width, span)
    shape = jax.ShapeDtypeStruct
    return pl.pallas_call(
        block_kernel,
        out_shape=(
            shape((rows, span, width), BF16),
            shape((rows, span, width), F32),
            shape(square, BF16), shape(square, BF16), shape(square, BF16), shape(square, BF16),
            shape((4,) + square, BF16), shape((4,) + square, BF16),
            shape((2, width), F32),
            shape((2, rows, 6, 2, 2, span, span), BF16),
        ),
        in_specs=[hbm, vmem, vmem, vmem, smem, vmem, vmem, vmem, vmem, vmem, vmem, hbm, hbm],
        out_specs=(hbm,) * 8 + (vmem, hbm),
        scratch_shapes=[
            pltpu.VMEM(blocks, BF16),
            pltpu.VMEM(square, BF16),
            pltpu.VMEM(square, BF16),
            pltpu.VMEM((rows, span, width), BF16),
            pltpu.VMEM(blocks, BF16),
            pltpu.VMEM(blocks, BF16),
            pltpu.VMEM(flipped, BF16),
            pltpu.VMEM((2, 2, 2, span, span), BF16),
            pltpu.VMEM((rows, width, span), F32),
            pltpu.VMEM((rows, H, 2, 1, span), F32),
            pltpu.VMEM((rows, H, 2, 1, span), F32),
            pltpu.VMEM((rows, H, 2, 1, span), F32),
            pltpu.VMEM((2, cap, local), BF16),
            pltpu.VMEM((2 * cap, width), BF16),
            pltpu.VMEM((2 * cap, width), BF16),
            pltpu.VMEM((cap, width), BF16),
            pltpu.VMEM((2, rows, span, width), BF16),
            pltpu.VMEM((rows, span, width), F32),
            pltpu.VMEM((4,) + square, BF16),
            pltpu.VMEM((4,) + square, BF16),
            pltpu.VMEM((2 * cap, width), F32),
            pltpu.VMEM((2, cap, width), F32),
            pltpu.VMEM((4, 2 * cap, width), BF16),
            pltpu.VMEM((4, 2 * cap, width), BF16),
            pltpu.VMEM((cap, width), BF16),
            pltpu.VMEM((cap, width), BF16),
            pltpu.VMEM((local, width), BF16),
            pltpu.VMEM((local, width), BF16),
            sem((5,)), sem((2,)), sem((2,)), sem((2,)), sem((2,)), sem((2,)), sem((2,)), sem((2,)),
            sem((2,)), sem((2,)), sem((4,)), sem((4,)), sem((4,)), sem((4,)), sem((3,)), sem((3,)), sem((2, 4)),
        ],
        compiler_params=pltpu.CompilerParams(collective_id=1, has_side_effects=True, vmem_limit_bytes=60 << 20),
        name="block_step",
    )(tokens, cot, ids, table, lengths, gain_a, gain_f, wq, wk, wv, wo, w_in, w_out)


def norm_rows(values, gain):
    average = jnp.mean(values, axis=-1, keepdims=True)
    centred = values - average
    spread = jnp.mean(centred * centred, axis=-1, keepdims=True)
    return centred * lax.rsqrt(spread + epsilon) * gain


def gelu_grad(pre, upstream):
    unused, pullback = jax.vjp(jax.nn.gelu, pre)
    return pullback(upstream)[0]


def split_heads(matrix):
    return matrix.reshape(matrix.shape[0], matrix.shape[1], H, HD).transpose(2, 0, 1, 3)


def join_heads(stacked):
    return stacked.transpose(1, 2, 0, 3).reshape(stacked.shape[1], stacked.shape[2], H * HD)


def per_device_plain(
    tokens,
    token_ids,
    hash_table,
    lengths,
    gain_attn,
    w_query,
    w_key,
    w_value,
    w_output,
    gain_ffn,
    w_in,
    w_out,
    cotangent,
):
    row_count, span, width = tokens.shape
    local_tok = row_count * span
    whole = span * lax.axis_size("seq")
    place = lax.axis_index("seq")
    scale = HD ** (-0.5)
    inputs = tokens.reshape(local_tok, width).astype(jnp.float32)
    key_positions = jnp.arange(whole, dtype=jnp.int32)
    query_positions = place * span + jnp.arange(span, dtype=jnp.int32)
    ends = jnp.cumsum(lengths, axis=1)
    key_document = jnp.sum(
        (key_positions[None, :, None] >= ends[:, None, :]).astype(jnp.int32), axis=2
    )
    query_document = jnp.sum(
        (query_positions[None, :, None] >= ends[:, None, :]).astype(jnp.int32), axis=2
    )
    visible = (key_positions[None, None, :] <= query_positions[None, :, None]) & (
        query_document[:, :, None] == key_document[:, None, :]
    )
    normed, first_norm_back = jax.vjp(norm_rows, inputs, gain_attn)
    normed_low = normed.astype(jnp.bfloat16)
    query = jnp.dot(normed_low, w_query, preferred_element_type=jnp.float32).astype(jnp.bfloat16)
    keys = jnp.dot(normed_low, w_key, preferred_element_type=jnp.float32).astype(jnp.bfloat16)
    values = jnp.dot(normed_low, w_value, preferred_element_type=jnp.float32).astype(jnp.bfloat16)
    own_pair = jnp.concatenate([keys, values], axis=1).reshape(row_count, span, 2 * width)
    all_pairs = lax.all_gather(own_pair, "seq", axis=1, tiled=True)

    def pair_heads(pairs):
        return (split_heads(pairs[:, :, :width]), split_heads(pairs[:, :, width:]))

    query_heads = split_heads(query.reshape(row_count, span, width))
    key_heads, value_heads = pair_heads(all_pairs)

    def head_forward(parts):
        query_one, key_one, value_one = parts
        scores = (
            jnp.einsum("rqd,rkd->rqk", query_one, key_one, preferred_element_type=jnp.float32)
            * scale
        )
        scores = jnp.where(visible, scores, masked_score)
        peak = jnp.max(scores, axis=2, keepdims=True)
        weights = jnp.exp(scores - peak)
        totals = jnp.sum(weights, axis=2, keepdims=True)
        probs = (weights / totals).astype(jnp.bfloat16)
        mixed = jnp.einsum("rqk,rkd->rqd", probs, value_one, preferred_element_type=jnp.float32)
        return (mixed, (peak + jnp.log(totals))[:, :, 0])

    mixed_heads, log_totals = lax.map(head_forward, (query_heads, key_heads, value_heads))
    attended = join_heads(mixed_heads).reshape(local_tok, width).astype(jnp.bfloat16)
    middle = inputs + jnp.dot(attended, w_output, preferred_element_type=jnp.float32)
    ffn_norm, second_norm_back = jax.vjp(norm_rows, middle, gain_ffn)
    ffn_in = ffn_norm.astype(jnp.bfloat16)
    experts = lax.axis_size("expert")
    capacity = min(2 * local_tok // experts, 3 * local_tok // 4)
    expert_of = jnp.take(hash_table, token_ids.reshape(local_tok), axis=0)
    labels = jnp.arange(experts, dtype=jnp.int32)
    onehot = (expert_of[:, None] == labels[None, :]).astype(jnp.int32)
    own_rank = jnp.sum((jnp.cumsum(onehot, axis=0) - 1) * onehot, axis=1)
    slots = expert_of * capacity + own_rank
    sources = (
        jnp.full((experts * capacity,), local_tok, jnp.int32)
        .at[slots]
        .set(jnp.arange(local_tok, dtype=jnp.int32))
    )

    def to_slots(rows_low):
        padded = jnp.concatenate([rows_low, jnp.zeros((1, width), rows_low.dtype)], axis=0)
        return jnp.take(padded, sources, axis=0).reshape(experts, capacity, width)

    received = lax.all_to_all(
        to_slots(ffn_in), "expert", split_axis=0, concat_axis=0, tiled=True
    ).reshape(-1, width)
    full_in, full_out = (
        lax.all_gather(w_in, "seq", axis=2, tiled=True),
        lax.all_gather(w_out, "seq", axis=1, tiled=True),
    )
    full_in = full_in[0]
    full_out = full_out[0]
    first = jnp.dot(received, full_in, preferred_element_type=jnp.float32)
    produced = jnp.dot(
        jax.nn.gelu(first).astype(jnp.bfloat16), full_out, preferred_element_type=jnp.float32
    ).astype(jnp.bfloat16)
    returned = lax.all_to_all(
        produced.reshape(experts, capacity, width),
        "expert",
        split_axis=0,
        concat_axis=0,
        tiled=True,
    ).reshape(-1, width)
    output = middle + jnp.take(returned, slots, axis=0).astype(jnp.float32)
    upstream = cotangent.reshape(local_tok, width)
    grad_received_out = lax.all_to_all(
        to_slots(upstream), "expert", split_axis=0, concat_axis=0, tiled=True
    ).reshape(-1, width)
    pre = jnp.dot(received, full_in, preferred_element_type=jnp.float32)
    hidden = jax.nn.gelu(pre).astype(jnp.bfloat16)
    grad_full_out = jnp.einsum(
        "rf,rd->fd", hidden, grad_received_out, preferred_element_type=jnp.float32
    )
    grad_hidden = jnp.einsum(
        "rd,fd->rf", grad_received_out, full_out, preferred_element_type=jnp.float32
    )
    grad_pre = gelu_grad(pre, grad_hidden).astype(jnp.bfloat16)
    grad_full_in = jnp.einsum("rd,rf->df", received, grad_pre, preferred_element_type=jnp.float32)
    grad_received = jnp.einsum(
        "rf,df->rd", grad_pre, full_in, preferred_element_type=jnp.float32
    ).astype(jnp.bfloat16)
    grad_in_part, grad_out_part = (
        lax.psum_scatter(
            grad_full_in[None].astype(jnp.bfloat16), "seq", scatter_dimension=2, tiled=True
        ).astype(jnp.float32),
        lax.psum_scatter(
            grad_full_out[None].astype(jnp.bfloat16), "seq", scatter_dimension=1, tiled=True
        ).astype(jnp.float32),
    )
    grad_in, grad_out = (
        lax.psum(grad_in_part.astype(jnp.bfloat16), "dp").astype(jnp.float32),
        lax.psum(grad_out_part.astype(jnp.bfloat16), "dp").astype(jnp.float32),
    )
    grad_back = lax.all_to_all(
        grad_received.reshape(experts, capacity, width),
        "expert",
        split_axis=0,
        concat_axis=0,
        tiled=True,
    ).reshape(-1, width)
    grad_ffn_in = jnp.take(grad_back, slots, axis=0).astype(jnp.float32)
    grad_middle_norm, grad_gain_ffn = second_norm_back(grad_ffn_in)
    grad_middle = upstream.astype(jnp.float32) + grad_middle_norm
    grad_branch = grad_middle.astype(jnp.bfloat16)
    grad_w_output = jnp.einsum(
        "cd,ce->de", attended, grad_branch, preferred_element_type=jnp.float32
    )
    grad_attended = jnp.einsum(
        "ce,de->cd", grad_branch, w_output, preferred_element_type=jnp.float32
    ).astype(jnp.bfloat16)
    again_pairs = lax.all_gather(own_pair, "seq", axis=1, tiled=True)
    key_back, value_back = pair_heads(again_pairs)

    def head_backward(parts):
        query_one, key_one, value_one, grad_one, log_one = parts
        scores = (
            jnp.einsum("rqd,rkd->rqk", query_one, key_one, preferred_element_type=jnp.float32)
            * scale
        )
        scores = jnp.where(visible, scores, masked_score)
        probs_full = jnp.exp(scores - log_one[:, :, None])
        probs = probs_full.astype(jnp.bfloat16)
        grad_probs = jnp.einsum(
            "rqd,rkd->rqk", grad_one, value_one, preferred_element_type=jnp.float32
        )
        inner = jnp.sum(probs_full * grad_probs, axis=2, keepdims=True)
        grad_scores = (probs_full * (grad_probs - inner)).astype(jnp.bfloat16)
        grad_query_one = (
            jnp.einsum("rqk,rkd->rqd", grad_scores, key_one, preferred_element_type=jnp.float32)
            * scale
        )
        grad_key_one = (
            jnp.einsum("rqk,rqd->rkd", grad_scores, query_one, preferred_element_type=jnp.float32)
            * scale
        )
        grad_value_one = jnp.einsum(
            "rqk,rqd->rkd", probs, grad_one, preferred_element_type=jnp.float32
        )
        return (grad_query_one, grad_key_one, grad_value_one)

    grad_att_heads = split_heads(grad_attended.reshape(row_count, span, width))
    grad_query_heads, grad_key_heads, grad_value_heads = lax.map(
        head_backward, (query_heads, key_back, value_back, grad_att_heads, log_totals)
    )
    grad_query_rows = join_heads(grad_query_heads).reshape(local_tok, width).astype(jnp.bfloat16)
    pair_grads = jnp.concatenate([join_heads(grad_key_heads), join_heads(grad_value_heads)], axis=2)
    own_grads = (
        lax.psum_scatter(pair_grads, "seq", scatter_dimension=1, tiled=True)
        .reshape(local_tok, 2 * width)
        .astype(jnp.bfloat16)
    )
    grad_key_rows = own_grads[:, :width]
    grad_value_rows = own_grads[:, width:]
    grad_w_query = jnp.einsum(
        "cd,ce->de", normed_low, grad_query_rows, preferred_element_type=jnp.float32
    )
    grad_w_key = jnp.einsum(
        "cd,ce->de", normed_low, grad_key_rows, preferred_element_type=jnp.float32
    )
    grad_w_value = jnp.einsum(
        "cd,ce->de", normed_low, grad_value_rows, preferred_element_type=jnp.float32
    )
    grad_normed = jnp.einsum(
        "ce,de->cd", grad_query_rows, w_query, preferred_element_type=jnp.float32
    )
    grad_normed = grad_normed + jnp.einsum(
        "ce,de->cd", grad_key_rows, w_key, preferred_element_type=jnp.float32
    )
    grad_normed = grad_normed + jnp.einsum(
        "ce,de->cd", grad_value_rows, w_value, preferred_element_type=jnp.float32
    )
    grad_inputs_norm, grad_gain_attn = first_norm_back(grad_normed)
    input_grad = grad_middle + grad_inputs_norm
    summed = lax.psum(
        (grad_gain_attn, grad_w_query, grad_w_key, grad_w_value, grad_w_output, grad_gain_ffn),
        ("dp", "seq", "expert"),
    )
    shaped_output = output.astype(jnp.bfloat16).reshape(row_count, span, width)
    shaped_grad = input_grad.reshape(row_count, span, width)
    return (
        shaped_output,
        shaped_grad,
        summed[0],
        summed[1],
        summed[2],
        summed[3],
        summed[4],
        summed[5],
        grad_in,
        grad_out,
    )


def per_device(
    tokens,
    token_ids,
    hash_table,
    lengths,
    gain_attn,
    w_query,
    w_key,
    w_value,
    w_output,
    gain_ffn,
    w_in,
    w_out,
    cotangent,
):
    row_count, span, width = tokens.shape
    local_tok = row_count * span
    output, input_grad, grad_q, grad_k, grad_v, grad_o, part_in, part_out, gains, unused = block(
        tokens, cotangent.reshape(local_tok, width), token_ids, hash_table.reshape(-1, 128), lengths,
        gain_attn.reshape(1, width), gain_ffn.reshape(1, width),
        w_query, w_key, w_value, w_output, w_in[0], w_out[0])
    grad_in, grad_out = (
        lax.psum(lax.psum_scatter(part, "seq", scatter_dimension=0, tiled=True), "dp").astype(F32)
        for part in (part_in, part_out)
    )
    summed = lax.psum((grad_q, grad_k, grad_v, grad_o, gains), ("dp", "seq", "expert"))
    return (
        output,
        input_grad,
        summed[4][1],
        summed[0].astype(F32),
        summed[1].astype(F32),
        summed[2].astype(F32),
        summed[3].astype(F32),
        summed[4][0],
        grad_in,
        grad_out,
    )


def solution(mesh):
    sizes = (mesh.shape["dp"], mesh.shape["seq"], mesh.shape["expert"])
    return jax.shard_map(
        per_device if sizes == (4, 4, 2) else per_device_plain,
        mesh=mesh,
        in_specs=(
            P(("dp", "expert"), "seq", None),
            P(("dp", "expert"), "seq"),
            P(),
            P(("dp", "expert"), None),
            P(),
            P(),
            P(),
            P(),
            P(),
            P(),
            P("expert", None, "seq"),
            P("expert", "seq", None),
            P(("dp", "expert"), "seq", None),
        ),
        out_specs=(
            P(("dp", "expert"), "seq", None),
            P(("dp", "expert"), "seq", None),
            P(),
            P(),
            P(),
            P(),
            P(),
            P(),
            P("expert", None, "seq"),
            P("expert", "seq", None),
        ),
        check_vma=False,
    )
```

```python
import functools
import jax
import jax.numpy as jnp
from jax import lax
from jax.experimental import pallas as pl
from jax.experimental.pallas import tpu as pltpu
from jax.sharding import PartitionSpec as P

MESH = pl.DeviceIdType.MESH
F32 = jnp.float32
BF16 = jnp.bfloat16
I32 = jnp.int32
H = 12
HD = 64
epsilon = 1e-05
masked_score = -1e30
gelu_a = 0.7978845608028654
gelu_b = 0.044715


def dot_nn(a, b):
    return jnp.dot(a, b, preferred_element_type=F32)


def dot_nt(a, b):
    return lax.dot_general(a, b, (((1,), (1,)), ((), ())), preferred_element_type=F32)


def dot_tn(a, b):
    return lax.dot_general(a, b, (((0,), (0,)), ((), ())), preferred_element_type=F32)


def norm_parts(values):
    average = jnp.mean(values, axis=-1, keepdims=True)
    centred = values - average
    spread = jnp.mean(centred * centred, axis=-1, keepdims=True)
    root = lax.rsqrt(spread + epsilon)
    return centred * root, root


def norm_back(upstream, gain, xhat, root):
    scaled = upstream * gain
    first = jnp.mean(scaled, axis=-1, keepdims=True)
    second = jnp.mean(scaled * xhat, axis=-1, keepdims=True)
    return root * (scaled - first - xhat * second)


def block_kernel(
    tokens_hbm, cot_ref, ids_ref, table_ref, lengths_ref, gain_a_ref, gain_f_ref,
    wq_ref, wk_ref, wv_ref, wo_ref, win_hbm, wout_hbm,
    out_hbm, ig_hbm, dwq_hbm, dwk_hbm, dwv_hbm, dwo_hbm, dwin_hbm, dwout_hbm, gg_ref, es_hbm, ra_hbm, ro_hbm,
    nb, xgb, eob, qs, ks, vs, dot, ebuf, oa, stat, facs, dl, route, cs, xs, do, mid,
    win, wout, acc, preg, hid, gp, gback, eback, dnr0, dnr1,
    local_sem, e_sem, tok_send, tok_recv, fwd_send, fwd_recv, core_send, core_recv,
    wx_send, wx_recv, wz_send, wz_recv, wf_send, wf_recv, wc_send, wc_recv, y_send, y_recv, dn_send, dn_recv,
    recv_d, recv_p, gsum, ed_send, ed_recv, ex_send, ex_recv, ee_send, ee_recv, em_send, em_recv,
    eb_send, eb_recv, eo_sem, free_x, free_z, free_m, free_d,
    rd_send, rd_recv, rp_send, rp_recv, rz_send, rz_recv, gd_send, gd_recv,
    own_sem, gn_send, gn_recv,
):
    dp = lax.axis_index("dp")
    s = lax.axis_index("seq")
    y = lax.axis_index("expert")
    c = lax.rem(s, 2)
    x = s // 2
    core_peer = (dp, x * 2 + 1 - c, y)
    x_peer = (dp, (1 - x) * 2 + c, y)
    y_peer = (dp, s, 1 - y)
    span = tokens_hbm.shape[1]
    width = tokens_hbm.shape[2]
    local = 2 * span
    cap = gback.shape[0]
    stage = eob.at[0:cap]

    def remote(src, dst, send, recv, peer):
        return pltpu.make_async_remote_copy(
            src_ref=src, dst_ref=dst, send_sem=send, recv_sem=recv, device_id=peer, device_id_type=MESH)

    own_copy = pltpu.make_async_copy(tokens_hbm, nb.at[s], local_sem.at[0])
    win_copy = pltpu.make_async_copy(win_hbm, win.at[s], local_sem.at[1])
    wout_copy = pltpu.make_async_copy(wout_hbm, wout.at[s], local_sem.at[2])
    own_copy.start()
    win_copy.start()
    wout_copy.start()
    barrier = pltpu.get_barrier_semaphore()
    plane_peers = [x_peer, y_peer, (dp, (1 - x) * 2 + c, 1 - y)]
    z_peers = [(lax.rem(dp + d, 4), s, y) for d in range(1, 4)]
    for peer in [core_peer] + plane_peers + z_peers:
        pl.semaphore_signal(barrier, inc=1, device_id=peer, device_id_type=MESH)
    pl.semaphore_wait(barrier, 7)

    far_s = (1 - x) * 2 + c

    def token_copy(r):
        return remote(tokens_hbm.at[r], nb.at[s, r], tok_send.at[r], tok_recv.at[r], x_peer)

    def core_copy(r):
        return remote(tokens_hbm.at[r], nb.at[s, r], core_send.at[r], core_recv.at[r], core_peer)

    def forward_copy(r):
        return remote(nb.at[c, r], nb.at[c, r], fwd_send.at[r], fwd_recv.at[r], core_peer)

    wc_copies = [
        remote(win_hbm, win.at[s], wc_send.at[0], wc_recv.at[0], core_peer),
        remote(wout_hbm, wout.at[s], wc_send.at[1], wc_recv.at[1], core_peer),
    ]
    chunk = width // 4
    even = lax.rem(dp, 2) == 0
    swap_peer = (dp + 1 - 2 * lax.rem(dp, 2), s, y)

    def by_parity(action):
        @pl.when(even)
        def _():
            action(win, wout, win_hbm)

        @pl.when(jnp.logical_not(even))
        def _():
            action(wout, win, wout_hbm)

    def rows_of(j):
        return slice(j * chunk, (j + 1) * chunk)

    def wx_copy(j, matrix, source):
        return remote(source.at[rows_of(j)], matrix.at[s, rows_of(j)], wx_send.at[j], wx_recv.at[j], x_peer)

    def wz_copy(j, matrix):
        return remote(matrix.at[far_s, rows_of(j)], matrix.at[far_s, rows_of(j)], wz_send.at[j], wz_recv.at[j], swap_peer)

    def wf_copy(k, j, matrix):
        return remote(matrix.at[far_s, rows_of(j)], matrix.at[far_s, rows_of(j)],
                      wf_send.at[4 * k + j], wf_recv.at[4 * k + j], core_peer)

    def from_x(j):
        def action(first, second, source):
            wx_copy(j, first, source).wait_recv()
            wz_copy(j, first).start()
            wf_copy(0, j, first).start()
        by_parity(action)

    def from_z(j):
        def action(first, second, source):
            wz_copy(j, second).wait_recv()
            wf_copy(1, j, second).start()
        by_parity(action)

    @pl.when(x == 0)
    def _():
        for r in range(2):
            token_copy(r).start()

    by_parity(lambda first, second, source: [wx_copy(j, first, source).start() for j in range(4)] and None)

    @pl.when(c == 0)
    def _():
        for r in range(2):
            core_copy(r).start()

    wc_copies[0].start()
    wc_copies[1].start()

    ids = jnp.concatenate([ids_ref[0:1, :], ids_ref[1:2, :]], axis=1)
    high = ids // 128
    low = ids - high * 128
    pick = jnp.where(lax.broadcasted_iota(I32, (64, local), 0) == high, 1.0, 0.0).astype(BF16)
    looked = dot_tn(table_ref[...].astype(F32).astype(BF16), pick)
    expert_row = jnp.sum(
        jnp.where(lax.broadcasted_iota(I32, (128, local), 0) == low, looked, 0.0), axis=0, keepdims=True)
    mine = jnp.where(expert_row == y.astype(F32), 1.0, 0.0)
    sixteen = lax.broadcasted_iota(I32, (16, local), 0)
    both = jnp.where(sixteen == 0, mine, jnp.where(sixteen == 1, 1.0 - mine, 0.0)).astype(BF16)
    before = jnp.where(
        lax.broadcasted_iota(I32, (local, local), 0) < lax.broadcasted_iota(I32, (local, local), 1), 1.0, 0.0
    ).astype(BF16)
    ranks = dot_nn(both, before)
    slot_rows = lax.broadcasted_iota(I32, (cap, local), 0).astype(F32)
    for u in range(2):
        chosen = mine if u == 0 else 1.0 - mine
        route[u] = jnp.where(slot_rows == ranks[u:u + 1, :], chosen, 0.0).astype(BF16)

    cot_copy = remote(stage, cs.at[cap:], y_send.at[0], y_recv.at[0], y_peer)
    xs_copy = remote(stage, xs.at[cap:], y_send.at[1], y_recv.at[1], y_peer)
    stage[...] = dot_nn(route[1], cot_ref[...]).astype(BF16)
    cot_copy.start()
    cs[0:cap] = dot_nn(route[0], cot_ref[...]).astype(BF16)

    gain_a = gain_a_ref[...].reshape(1, width)
    gain_f = gain_f_ref[...].reshape(1, width)

    def normalise(part, r):
        nb[part, r] = (norm_parts(nb[part, r].astype(F32))[0] * gain_a).astype(BF16)

    def project(part, r):
        normed = nb[part, r]
        ks[part, r] = dot_nn(normed, wk_ref[...]).astype(BF16)
        vs[part, r] = dot_nn(normed, wv_ref[...]).astype(BF16)

    first_half = lax.broadcasted_iota(I32, (span, 128), 1) < HD
    first_rows = lax.broadcasted_iota(I32, (128, span), 0) < HD

    def only(values, keep, hh):
        return jnp.where(keep if hh == 0 else jnp.logical_not(keep), values, jnp.zeros_like(values))

    def pair_lanes(p):
        return pl.ds(pl.multiple_of(p * 128, 128), 128)

    def head_rows(p, hh):
        return pl.ds(pl.multiple_of(p * 128 + hh * HD, HD), HD)

    def e_near(r, p, slot, write, both_parts):
        here = ebuf.at[slot] if both_parts else ebuf.at[slot, :, 1]
        there = es_hbm.at[0, r, p] if both_parts else es_hbm.at[0, r, p, :, 1]
        return pltpu.make_async_copy(here if write else there, there if write else here, e_sem.at[slot])

    def e_far(r, p, slot, write):
        here = ebuf.at[slot]
        there = es_hbm.at[1, r, p]
        return pltpu.make_async_copy(here if write else there, there if write else here, e_sem.at[slot])

    def attend(r, p, slot, parts, places, diagonal):
        lanes = pair_lanes(p)
        q_pair = qs[r, :, lanes]
        v_flipped = [vs[part, r, :, lanes].T for part in parts]
        results = []
        for hh in range(2):
            q_one = only(q_pair, first_half, hh)
            scores = [dot_nt(ks[part, r, :, lanes], q_one) for part in parts]
            if diagonal:
                ki = lax.broadcasted_iota(I32, (span, span), 0)
                qi = lax.broadcasted_iota(I32, (span, span), 1)
                scores[-1] = jnp.where(ki <= qi, scores[-1], masked_score)
            peak = jnp.max(scores[0], axis=0, keepdims=True)
            for extra in scores[1:]:
                peak = jnp.maximum(peak, jnp.max(extra, axis=0, keepdims=True))
            total = 0.0
            mixed = 0.0
            rows = head_rows(p, hh)
            for v_one, place, one in zip(v_flipped, places, scores):
                weights = jnp.exp(one - peak)
                total = total + jnp.sum(weights, axis=0, keepdims=True)
                low_weights = weights.astype(BF16)
                ebuf[slot, hh, place] = low_weights
                mixed = mixed + dot_nn(v_one[hh * HD:(hh + 1) * HD], low_weights)
            results.append((2 * p + hh, rows, peak, total, mixed))
        return results

    own_copy.wait()

    def own_rows(r, carry):
        mid[r] = nb[s, r].astype(F32)
        normalise(s, r)
        project(s, r)
        qs[r] = (dot_nn(nb[s, r], wq_ref[...]) * (HD ** -0.5)).astype(BF16)
        return carry

    lax.fori_loop(0, 2, own_rows, 0)

    def near_loop(parts, places):
        wide = len(parts) == 2

        def step(i, carry):
            r, p, slot = i // 6, lax.rem(i, 6), lax.rem(i, 2)

            @pl.when(i >= 2)
            def _():
                e_near(r, p, slot, True, wide).wait()

            for h, rows, peak, total, mixed in attend(r, p, slot, parts, places, True):
                stat[r, h, 0] = peak
                stat[r, h, 1] = total
                oa[r, rows, :] = mixed
            e_near(r, p, slot, True, wide).start()
            return carry

        lax.fori_loop(0, 12, step, 0)
        for slot in range(2):
            e_near(1, 4 + slot, slot, True, wide).wait()

    @pl.when(c == 0)
    def _():
        near_loop([s], [1])

    @pl.when(c == 1)
    def _():
        for r in range(2):
            core_copy(r).wait_recv()

        def partner_rows(r, carry):
            normalise(s - 1, r)
            project(s - 1, r)
            return carry

        lax.fori_loop(0, 2, partner_rows, 0)
        near_loop([s - 1, s], [0, 1])

    @pl.when(x == 0)
    def _():
        def step(i, carry):
            r, h = i // H, lax.rem(i, H)
            rows = pl.ds(pl.multiple_of(h * HD, HD), HD)
            inverse = 1.0 / stat[r, h, 1]
            facs[r, h, 0] = inverse
            facs[r, h, 1] = jnp.zeros_like(inverse)
            oa[r, rows, :] = oa[r, rows, :] * inverse
            return carry

        lax.fori_loop(0, 2 * H, step, 0)
        from_x(0)
        from_x(1)

    @pl.when(x == 1)
    def _():
        for r in range(2):
            token_copy(r).wait_recv()
            normalise(c, r)
            forward_copy(r).start()
            project(c, r)
            forward_copy(r).wait()
            project(1 - c, r)
            single = lengths_ref[r, 1] == 0

            def step(p, carry):
                slot = lax.rem(p, 2)

                @pl.when(p >= 2)
                def _():
                    e_far(r, p, slot, True).wait()

                for h, rows, peak, total, mixed in attend(r, p, slot, [0, 1], [0, 1], False):
                    near_peak = stat[r, h, 0]
                    peak = jnp.where(single, peak, near_peak)
                    top = jnp.maximum(peak, near_peak)
                    near_f = jnp.exp(near_peak - top)
                    far_f = jnp.where(single, jnp.exp(peak - top), 0.0)
                    whole = near_f * stat[r, h, 1] + far_f * total
                    near_f = near_f / whole
                    far_f = far_f / whole
                    facs[r, h, 0] = near_f
                    facs[r, h, 1] = far_f
                    oa[r, rows, :] = oa[r, rows, :] * near_f + mixed * far_f
                e_far(r, p, slot, True).start()
                return carry

            lax.fori_loop(0, 6, step, 0)
            for slot in range(2):
                e_far(r, 4 + slot, slot, True).wait()
            from_x(r)

    def out_rows(r, carry):
        att = oa[r].astype(BF16).T
        value = mid[r] + dot_nn(att, wo_ref[...])
        mid[r] = value
        do[0, r] = (norm_parts(value)[0] * gain_f).astype(BF16)
        return carry

    lax.fori_loop(0, 2, out_rows, 0)

    ffn_in = do[0].reshape(local, width)
    cot_copy.wait_send()
    stage[...] = dot_nn(route[1], ffn_in).astype(BF16)
    xs_copy.start()
    xs[0:cap] = dot_nn(route[0], ffn_in).astype(BF16)
    win_copy.wait()
    wout_copy.wait()
    acc[...] = jnp.zeros_like(acc)

    def expert_rows(u, f):
        rows = pl.ds(pl.multiple_of(u * cap, cap), cap)
        tokens_in = xs[rows]
        grads_in = cs[rows]
        for n in range(3):
            lanes = slice(n * 256, (n + 1) * 256)
            pre = dot_nn(tokens_in, win[f, :, lanes])
            up = dot_nt(grads_in, wout[f, lanes])
            square = pre * pre
            bent = jnp.tanh(gelu_a * pre * (1.0 + gelu_b * square))
            half = 0.5 * (1.0 + bent)
            slope = half + 0.5 * pre * (1.0 - bent * bent) * (gelu_a * (1.0 + 3.0 * gelu_b * square))
            hid[f, rows, lanes] = (pre * half).astype(BF16)
            gp[f, rows, lanes] = (up * slope).astype(BF16)
        acc[rows] += dot_nt(gp[f, rows], win[f])

    def expert_number(ix, ic):
        return 2 * lax.rem(x + ix, 2) + lax.rem(c + ic, 2)

    def moe_step(i, carry):
        ix = i // 4
        outer, inner = lax.rem(i // 2, 2), lax.rem(i, 2)

        @pl.when(i == 2)
        def _():
            xs_copy.wait_recv()
            cot_copy.wait_recv()

        @pl.when(i == 6)
        def _():
            by_parity(lambda first, second, source: [
                wf_copy(k, j, (first, second)[k]).wait_recv() for k in range(2) for j in range(4)] and None)

        @pl.when(i == 1)
        def _():
            wc_copies[0].wait_recv()
            wc_copies[1].wait_recv()
        expert_rows(jnp.where(ix == 0, outer, inner), expert_number(ix, jnp.where(ix == 0, inner, outer)))

        @pl.when(i == 0)
        def _():
            from_z(1)

        @pl.when(i == 1)
        def _():
            from_x(3)
            from_z(2)

        @pl.when(i == 2)
        def _():
            from_z(3)
        return carry

    from_x(2)
    from_z(0)
    lax.fori_loop(0, 8, moe_step, 0)

    grad_copy = remote(xgb.at[cap:], gback, y_send.at[2], y_recv.at[2], y_peer)
    out_copy = remote(eob.at[cap:], eback, y_send.at[3], y_recv.at[3], y_peer)
    xgb[...] = acc[...].astype(BF16)
    grad_copy.start()
    acc[...] = jnp.zeros_like(acc)
    wc_copies[0].wait_send()
    wc_copies[1].wait_send()
    by_parity(lambda first, second, source: [
        wf_copy(k, j, (first, second)[k]).wait_send() for k in range(2) for j in range(4)] and None)
    by_parity(lambda first, second, source: [wz_copy(j, first).wait_send() for j in range(4)] and None)
    xs_copy.wait_send()

    shard_a = expert_number(1, 0)
    shard_b = expert_number(1, 1)
    shard_c = expert_number(0, 1)
    ends = jnp.logical_or(dp == 0, dp == 3)
    end_z = jnp.where(dp < 2, 0, 3)
    near_mid = (jnp.where(dp < 2, 1, 2), s, y)
    other_mid = (3 - dp, s, y)
    end_peer = (end_z, s, y)
    core_sends = [
        remote(win.at[shard_b], ra_hbm.at[0], ed_send.at[0], ed_recv.at[0], core_peer),
        remote(wout.at[shard_b], ra_hbm.at[1], ed_send.at[1], ed_recv.at[1], core_peer),
        remote(win.at[shard_c], ro_hbm.at[0], ed_send.at[2], ed_recv.at[2], core_peer),
        remote(wout.at[shard_c], ro_hbm.at[1], ed_send.at[3], ed_recv.at[3], core_peer),
    ]

    def weight_grads(f):
        acc[...] += dot_nn(hid[f], wout[f])
        wout[f] = dot_tn(hid[f], cs[...]).astype(BF16)
        win[f] = dot_tn(xs[...], gp[f]).astype(BF16)

    load_a = [
        pltpu.make_async_copy(ra_hbm.at[0], win.at[shard_b], local_sem.at[1]),
        pltpu.make_async_copy(ra_hbm.at[1], wout.at[shard_b], local_sem.at[2]),
    ]
    load_o = [
        pltpu.make_async_copy(ro_hbm.at[0], win.at[shard_c], local_sem.at[1]),
        pltpu.make_async_copy(ro_hbm.at[1], wout.at[shard_c], local_sem.at[2]),
    ]

    def piece(k):
        return pl.ds(pl.multiple_of(lax.rem(k, 4) * chunk, chunk), chunk)

    def add_to(target, first, second):
        target[...] = first[...] + second[...]

    def by_matrix(k, action):
        @pl.when(k < 4)
        def _():
            action(win, dwin_hbm)

        @pl.when(k >= 4)
        def _():
            action(wout, dwout_hbm)

    def x_grad(k, grads):
        return remote(grads.at[shard_a, piece(k)], grads.at[shard_c, piece(k)],
                      ex_send.at[k], ex_recv.at[k], x_peer)

    def end_grad(k, grads):
        return remote(grads.at[s, piece(k)], grads.at[shard_c, piece(k)], ee_send.at[k], ee_recv.at[k], near_mid)

    def mid_grad(k, grads):
        return remote(grads.at[s, piece(k)], grads.at[shard_a, piece(k)], em_send.at[k], em_recv.at[k], other_mid)

    def back_grad(k, grads, out):
        return remote(grads.at[shard_b, piece(k)], out.at[piece(k)], eb_send.at[k], eb_recv.at[k], end_peer)

    def out_grad(k, grads, out):
        return pltpu.make_async_copy(grads.at[shard_b, piece(k)], out.at[piece(k)], eo_sem.at[k])

    def send_x(k):
        pl.semaphore_wait(free_x, 1)
        by_matrix(k, lambda grads, out: x_grad(k, grads).start())

    def start_x():
        def step(k, carry):
            by_matrix(k, lambda grads, out: add_to(
                grads.at[shard_a, piece(k)], grads.at[shard_a, piece(k)], grads.at[shard_b, piece(k)]))
            pl.semaphore_signal(free_x, inc=1, device_id=x_peer, device_id_type=MESH)

            @pl.when(jnp.logical_and(k >= 1, k < 4))
            def _():
                send_x(k - 1)
            return carry

        lax.fori_loop(0, 8, step, 0)

    def service(t):
        @pl.when(t < 8)
        def _():
            def action(grads, out):
                x_grad(t, grads).wait()

                @pl.when(t < 5)
                def _():
                    send_x(t + 3)
                add_to(grads.at[s, piece(t)], grads.at[s, piece(t)], grads.at[shard_b, piece(t)])

                @pl.when(ends)
                def _():
                    @pl.when(t == 0)
                    def _():
                        pl.semaphore_wait(free_z, 1)
                    end_grad(t, grads).start()

                @pl.when(jnp.logical_not(ends))
                def _():
                    pl.semaphore_signal(free_m, inc=1, device_id=other_mid, device_id_type=MESH)
            by_matrix(t, action)

        @pl.when(jnp.logical_and(jnp.logical_not(ends), jnp.logical_and(t >= 1, t < 9)))
        def _():
            k = t - 1

            def action(grads, out):
                end_grad(k, grads).wait_recv()
                add_to(grads.at[s, piece(k)], grads.at[s, piece(k)], grads.at[shard_c, piece(k)])
                pl.semaphore_wait(free_m, 1)
                mid_grad(k, grads).start()
            by_matrix(k, action)

        @pl.when(jnp.logical_and(jnp.logical_not(ends), t >= 2))
        def _():
            k = t - 2

            def action(grads, out):
                mid_grad(k, grads).wait_recv()
                add_to(grads.at[shard_b, piece(k)], grads.at[s, piece(k)], grads.at[shard_a, piece(k)])
                out_grad(k, grads, out).start()
                back_grad(k, grads, out).start()
            by_matrix(k, action)

    def drain_chain():
        def step(k, carry):
            def action(grads, out):
                @pl.when(ends)
                def _():
                    end_grad(k, grads).wait_send()
                    back_grad(k, grads, out).wait_recv()

                @pl.when(jnp.logical_not(ends))
                def _():
                    mid_grad(k, grads).wait_send()
                    back_grad(k, grads, out).wait_send()
                    out_grad(k, grads, out).wait()
            by_matrix(k, action)
            return carry

        lax.fori_loop(0, 8, step, 0)

    half = width // 2
    my_lanes = pl.ds(pl.multiple_of(c * half, half), half)
    peer_lanes = pl.ds(pl.multiple_of((1 - c) * half, half), half)
    corner = 2 * x + y
    sums = [None] * 4
    orders = ["yzx", "yxz", "yxz", "yxz"]

    def sum_step(m, step):
        source, out = sums[m]

        stages = []
        start, size, held, number = 0, width, 0, 0
        for axis in orders[m]:
            place, count, peers = {
                "x": (x, 2, [x_peer]), "y": (y, 2, [y_peer]), "z": (dp, 4, z_peers)}[axis]
            size = size // count
            sends = []
            for k, peer in enumerate(peers):
                other = start + lax.rem(place + 1 + k, count) * size
                sends.append((pl.ds(pl.multiple_of(other, size), size), slice(held, held + size), number, peer))
                held += size
                number += 1
            start = start + place * size
            stages.append((pl.ds(pl.multiple_of(start, size), size), sends))

        def core_send():
            return remote(source.at[:, peer_lanes], recv_d, rd_send.at[m], rd_recv.at[m], core_peer)

        def scatters(n):
            return [
                remote(source.at[rows, my_lanes], recv_p.at[m, held], rp_send.at[m, k], rp_recv.at[m, k], peer)
                for rows, held, k, peer in stages[n][1]]

        def gathers(n):
            kept = (stages[n][0], my_lanes)
            origin = source if n == 2 else out
            return [
                remote(origin.at[kept], out.at[kept], rz_send.at[m, k], rz_recv.at[m, k], peer)
                for rows, held, k, peer in stages[n][1]]

        def own_store():
            kept = (stages[2][0], my_lanes)
            return pltpu.make_async_copy(source.at[kept], out.at[kept], own_sem.at[m])

        def core_gather():
            return remote(out.at[:, my_lanes], out.at[:, my_lanes], gd_send.at[m], gd_recv.at[m], core_peer)

        if step == 0:
            if m > 0:
                pl.semaphore_wait(free_d, 1)
            core_send().start()
        if step == 1:
            core_send().wait()
            add_to(source.at[:, my_lanes], source.at[:, my_lanes], recv_d)
            if m < 3:
                pl.semaphore_signal(free_d, inc=1, device_id=core_peer, device_id_type=MESH)
            for one in scatters(0):
                one.start()
        if 2 <= step <= 4:
            n = step - 2
            for one in scatters(n):
                one.wait()
            kept = (stages[n][0], my_lanes)
            total = source[kept].astype(F32)
            for rows, held, k, peer in stages[n][1]:
                total = total + recv_p[m, held].astype(F32)
            source[kept] = total.astype(BF16)
            if n < 2:
                for one in scatters(n + 1):
                    one.start()
            else:
                own_store().start()
                for one in gathers(2):
                    one.start()
        if 5 <= step <= 7:
            n = 7 - step
            if n == 2:
                own_store().wait()
            for one in gathers(n):
                one.wait()
            if n > 0:
                for one in gathers(n - 1):
                    one.start()
            else:
                core_gather().start()
        if step == 8:
            core_gather().wait()

    def grads_step(i, carry):
        weight_grads(expert_number(1 - i // 2, lax.rem(i + 1, 2)))

        @pl.when(i == 0)
        def _():
            core_sends[0].start()
            core_sends[1].start()

        @pl.when(i == 1)
        def _():
            for k in range(2):
                core_sends[k].wait()
                load_a[k].start()

        @pl.when(i == 2)
        def _():
            core_sends[2].start()
            core_sends[3].start()
            for k in range(2):
                load_a[k].wait()
            start_x()
        return carry

    lax.fori_loop(0, 4, grads_step, 0)
    eob[...] = acc[...].astype(BF16)
    out_copy.start()
    for k in range(2):
        core_sends[2 + k].wait()
        load_o[k].start()

    grad_copy.wait_recv()
    acc[...] = jnp.zeros_like(acc)
    gg_ref[...] = jnp.zeros_like(gg_ref)

    def take_back(r, own, returned):
        picked = pl.ds(pl.multiple_of(r * span, span), span)
        return dot_tn(route[0, :, picked], own) + dot_tn(route[1, :, picked], returned)

    def ffn_back(r, carry):
        rows = pl.ds(pl.multiple_of(r * span, span), span)
        grad = take_back(r, xgb[0:cap], gback[...])
        xhat, root = norm_parts(mid[r])
        gg_ref[0:1] += jnp.sum(grad * xhat, axis=0, keepdims=True)
        whole = cot_ref[rows].astype(F32) + norm_back(grad, gain_f, xhat, root)
        preg[r] = whole
        branch = whole.astype(BF16)
        att = oa[r]
        acc[...] += dot_nn(att.astype(BF16), branch)
        up = dot_nt(wo_ref[...], branch)
        up3 = up.reshape(H, HD, span)
        inner = jnp.sum(up3 * att.reshape(H, HD, span), axis=1, keepdims=True)
        for g in range(2):
            factor = facs[r, :, g]
            dl[r, :, g] = inner * factor
            flipped = (up3 * factor).reshape(width, span).astype(BF16)
            dot[g, r] = flipped
            do[g, r] = flipped.T
        oa[r] = jnp.zeros_like(oa[r])
        return carry

    lax.fori_loop(0, 2, ffn_back, 0)
    xs[...] = acc[...].astype(BF16)
    sums[0] = (xs, dwo_hbm)
    sum_step(0, 0)
    for k in range(2):
        load_o[k].wait()
    add_to(win.at[s], win.at[s], win.at[shard_c])
    add_to(wout.at[s], wout.at[s], wout.at[shard_c])

    @pl.when(jnp.logical_not(ends))
    def _():
        pl.semaphore_signal(free_z, inc=1, device_id=end_peer, device_id_type=MESH)

    service(jnp.int32(0))
    sum_step(0, 1)

    def attend_back(r, p, slot, g, parts, places):
        lanes = pair_lanes(p)
        q_pair = qs[r, :, lanes]
        do_pair = do[g, r, :, lanes]
        dot_pair = dot[g, r, lanes, :]
        for part, place in zip(parts, places):
            v_pair = vs[part, r, :, lanes]
            k_flipped = ks[part, r, :, lanes].T
            grad_k = 0.0
            grad_v = 0.0
            for hh in range(2):
                h = 2 * p + hh
                rows = head_rows(p, hh)
                weights = ebuf[slot, hh, place]
                grad_p = dot_nn(v_pair, only(dot_pair, first_rows, hh))
                grad_s = (weights.astype(F32) * (grad_p - dl[r, h, g])).astype(BF16)
                grad_v = grad_v + dot_nn(weights, only(do_pair, first_half, hh))
                grad_k = grad_k + dot_nn(grad_s, only(q_pair, first_half, hh))
                oa[r, rows, :] += dot_nn(k_flipped[hh * HD:(hh + 1) * HD], grad_s)
            place_rows = pl.ds(pl.multiple_of(r * span, span), span)
            hid[part, place_rows, lanes] = grad_k.astype(BF16)
            gp[part, place_rows, lanes] = grad_v.astype(BF16)

    def back_loop(g, parts, places, every, first):
        wide = len(parts) == 2

        def fetch(i):
            r, p, slot = i // 6, lax.rem(i, 6), lax.rem(i, 2)
            return e_near(r, p, slot, False, wide) if g == 0 else e_far(r, p, slot, False)

        fetch(0).start()

        def step(i, carry):
            @pl.when(i < 11)
            def _():
                fetch(i + 1).start()
            fetch(i).wait()
            attend_back(i // 6, lax.rem(i, 6), lax.rem(i, 2), g, parts, places)
            if every:
                @pl.when(lax.rem(i, every) == every // 2)
                def _():
                    service(first + i // every)
            return carry

        lax.fori_loop(0, 12, step, 0)

    def normed_grad(part):
        return dot_nt(hid[part, 0:local], wk_ref[...]) + dot_nt(gp[part, 0:local], wv_ref[...])

    far_core = remote(cs.at[0:local], dnr0, dn_send.at[0], dn_recv.at[0], core_peer)
    far_x = remote(cs.at[0:local], dnr0, dn_send.at[1], dn_recv.at[1], x_peer)
    near_core = remote(xgb.at[0:local], dnr1, dn_send.at[2], dn_recv.at[2], core_peer)

    @pl.when(x == 1)
    def _():
        back_loop(1, [0, 1], [0, 1], 4, 1)
        cs[0:local] = normed_grad(1 - c).astype(BF16)
        far_core.start()
        mine_far = normed_grad(c)
        far_core.wait()
        cs[0:local] = (mine_far + dnr0[...].astype(F32)).astype(BF16)
        far_x.start()
        sum_step(0, 2)

    grad_copy.wait_send()

    @pl.when(jnp.logical_and(x == 1, c == 0))
    def _():
        back_loop(0, [s], [1], 6, 4)

    @pl.when(jnp.logical_and(x == 1, c == 1))
    def _():
        back_loop(0, [s - 1, s], [0, 1], 6, 4)

    @pl.when(jnp.logical_and(x == 0, c == 0))
    def _():
        back_loop(0, [s], [1], 0, 0)

    @pl.when(jnp.logical_and(x == 0, c == 1))
    def _():
        back_loop(0, [s - 1, s], [0, 1], 0, 0)

    @pl.when(c == 1)
    def _():
        xgb[0:local] = normed_grad(s - 1).astype(BF16)
        near_core.start()

    @pl.when(x == 0)
    def _():
        def step(t, carry):
            service(t)
            return carry

        lax.fori_loop(1, 4, step, 0)
        sum_step(0, 2)
        lax.fori_loop(4, 6, step, 0)

    sum_step(0, 3)

    out_copy.wait()

    def out_add(r, carry):
        rows = pl.ds(pl.multiple_of(r * span, span), span)
        do[0, r] = (mid[r] + take_back(r, eob[0:cap], eback[...])).astype(BF16)
        return carry

    lax.fori_loop(0, 2, out_add, 0)
    out_done = pltpu.make_async_copy(do.at[0], out_hbm, local_sem.at[4])
    out_done.start()

    tokens_again = pltpu.make_async_copy(tokens_hbm, do.at[1], local_sem.at[0])
    tokens_again.start()
    for r in range(2):
        qs[r] = (oa[r] * (HD ** -0.5)).astype(BF16).T

    def all_parts(grads):
        acc[...] = jnp.zeros_like(acc)

        def step(part, carry):
            acc[...] += dot_tn(nb[part].reshape(local, width), grads[part, 0:local])
            return carry

        @pl.when(x == 1)
        def _():
            lax.fori_loop(0, 2, step, 0)

        @pl.when(c == 1)
        def _():
            step(s - 1, 0)

        step(s, 0)

    free = [lax.rem(s + k, 4) for k in range(1, 4)]
    all_parts(hid)
    hid[free[0]] = acc[...].astype(BF16)
    sums[1] = (hid.at[free[0]], dwk_hbm)
    sum_step(1, 0)
    service(jnp.int32(6))
    all_parts(gp)
    hid[free[1]] = acc[...].astype(BF16)
    sums[2] = (hid.at[free[1]], dwv_hbm)
    sum_step(1, 1)
    sum_step(2, 0)
    query_grads = qs[...].reshape(local, width)
    acc[...] = dot_tn(nb[s].reshape(local, width), query_grads)
    hid[free[2]] = acc[...].astype(BF16)
    sums[3] = (hid.at[free[2]], dwq_hbm)
    sum_step(2, 1)
    sum_step(3, 0)
    acc[0:local] = normed_grad(s) + dot_nt(query_grads, wq_ref[...])

    sum_step(3, 1)
    sum_step(1, 2)
    service(jnp.int32(7))
    sum_step(2, 2)
    sum_step(3, 2)
    @pl.when(c == 0)
    def _():
        near_core.wait_recv()
        acc[0:local] += dnr1[...].astype(F32)

    @pl.when(x == 0)
    def _():
        far_x.wait_recv()
        acc[0:local] += dnr0[...].astype(F32)

    tokens_again.wait()

    def first_back(r, carry):
        rows = pl.ds(pl.multiple_of(r * span, span), span)
        grad = acc[rows]
        xhat, root = norm_parts(do[1, r].astype(F32))
        gg_ref[1:2] += jnp.sum(grad * xhat, axis=0, keepdims=True)
        mid[r] = preg[r] + norm_back(grad, gain_a, xhat, root)
        return carry

    lax.fori_loop(0, 2, first_back, 0)
    ig_done = pltpu.make_async_copy(mid, ig_hbm, local_sem.at[0])
    ig_done.start()

    def gain_sum(first, mine, count, peers, sems):
        gsum[first + mine] = gg_ref[...]
        copies = [
            remote(gsum.at[first + mine], gsum.at[first + mine], gn_send.at[sems + k], gn_recv.at[sems + k], peer)
            for k, peer in enumerate(peers)]
        for one in copies:
            one.start()
        return copies

    def gain_total(first, count, copies):
        for one in copies:
            one.wait()
        total = gsum[first]
        for k in range(1, count):
            total = total + gsum[first + k]
        gg_ref[...] = total

    copies = gain_sum(0, c, 2, [core_peer], 0)
    sum_step(0, 4)
    service(jnp.int32(8))
    gain_total(0, 2, copies)
    copies = gain_sum(2, corner, 4, plane_peers, 1)
    for m in range(1, 4):
        sum_step(m, 3)
    sum_step(0, 5)
    service(jnp.int32(9))
    gain_total(2, 4, copies)
    copies = gain_sum(6, dp, 4, z_peers, 4)
    for step in range(4, 8):
        for m in range(1, 4):
            sum_step(m, step)
        if step < 6:
            sum_step(0, step + 2)
    gain_total(6, 4, copies)
    for m in range(4):
        sum_step(m, 8)
    drain_chain()
    ig_done.wait()
    out_done.wait()
    by_parity(lambda first, second, source: [wx_copy(j, first, source).wait_send() for j in range(4)] and None)

    @pl.when(x == 1)
    def _():
        far_x.wait_send()

    @pl.when(x == 0)
    def _():
        for r in range(2):
            token_copy(r).wait_send()

    @pl.when(c == 1)
    def _():
        near_core.wait_send()

    @pl.when(c == 0)
    def _():
        for r in range(2):
            core_copy(r).wait_send()


def block(tokens, cot, ids, table, lengths, gain_a, gain_f, wq, wk, wv, wo, w_in, w_out):
    rows, span, width = tokens.shape
    local = rows * span
    cap = 3 * local // 4
    vmem = pl.BlockSpec(memory_space=pltpu.VMEM)
    hbm = pl.BlockSpec(memory_space=pl.ANY)
    smem = pl.BlockSpec(memory_space=pltpu.SMEM)
    sem = pltpu.SemaphoreType.DMA
    signal = pltpu.SemaphoreType.REGULAR
    square = (width, width)
    blocks = (4, rows, span, width)
    flipped = (2, rows, width, span)
    shape = jax.ShapeDtypeStruct
    return pl.pallas_call(
        block_kernel,
        out_shape=(
            shape((rows, span, width), BF16),
            shape((rows, span, width), F32),
            shape(square, BF16), shape(square, BF16), shape(square, BF16), shape(square, BF16),
            shape(square, BF16), shape(square, BF16),
            shape((8, width), F32),
            shape((2, rows, 6, 2, 2, span, span), BF16),
            shape((2,) + square, BF16), shape((2,) + square, BF16),
        ),
        in_specs=[hbm, vmem, vmem, vmem, smem, vmem, vmem, vmem, vmem, vmem, vmem, hbm, hbm],
        out_specs=(hbm,) * 8 + (vmem, hbm, hbm, hbm),
        scratch_shapes=[
            pltpu.VMEM(blocks, BF16),
            pltpu.VMEM(square, BF16),
            pltpu.VMEM(square, BF16),
            pltpu.VMEM((rows, span, width), BF16),
            pltpu.VMEM(blocks, BF16),
            pltpu.VMEM(blocks, BF16),
            pltpu.VMEM(flipped, BF16),
            pltpu.VMEM((2, 2, 2, span, span), BF16),
            pltpu.VMEM((rows, width, span), F32),
            pltpu.VMEM((rows, H, 2, 1, span), F32),
            pltpu.VMEM((rows, H, 2, 1, span), F32),
            pltpu.VMEM((rows, H, 2, 1, span), F32),
            pltpu.VMEM((2, cap, local), BF16),
            pltpu.VMEM((2 * cap, width), BF16),
            pltpu.VMEM((2 * cap, width), BF16),
            pltpu.VMEM((2, rows, span, width), BF16),
            pltpu.VMEM((rows, span, width), F32),
            pltpu.VMEM((4,) + square, BF16),
            pltpu.VMEM((4,) + square, BF16),
            pltpu.VMEM((2 * cap, width), F32),
            pltpu.VMEM((rows, span, width), F32),
            pltpu.VMEM((4, 2 * cap, width), BF16),
            pltpu.VMEM((4, 2 * cap, width), BF16),
            pltpu.VMEM((cap, width), BF16),
            pltpu.VMEM((cap, width), BF16),
            pltpu.VMEM((local, width), BF16),
            pltpu.VMEM((local, width), BF16),
            sem((5,)), sem((2,)), sem((2,)), sem((2,)), sem((2,)), sem((2,)), sem((2,)), sem((2,)),
            sem((4,)), sem((4,)), sem((4,)), sem((4,)), sem((8,)), sem((8,)), sem((2,)), sem((2,)),
            sem((4,)), sem((4,)), sem((3,)), sem((3,)),
            pltpu.VMEM((width, width // 2), BF16),
            pltpu.VMEM((4, 15 * width // 16, width // 2), BF16),
            pltpu.VMEM((10, 8, width), F32),
            sem((4,)), sem((4,)), sem((8,)), sem((8,)), sem((8,)), sem((8,)), sem((8,)), sem((8,)), sem((8,)), sem((8,)),
            sem((8,)), signal, signal, signal, signal,
            sem((4,)), sem((4,)), sem((4, 5)), sem((4, 5)), sem((4, 5)), sem((4, 5)), sem((4,)), sem((4,)),
            sem((4,)), sem((7,)), sem((7,)),
        ],
        compiler_params=pltpu.CompilerParams(collective_id=1, has_side_effects=True, vmem_limit_bytes=62 << 20),
        name="block_step",
    )(tokens, cot, ids, table, lengths, gain_a, gain_f, wq, wk, wv, wo, w_in, w_out)


def finish_kernel(*refs):
    for source, target in zip(refs[:8], refs[8:]):
        target[...] = source[...].astype(target.dtype)


def finish(squares, output, input_grad):
    width = squares[0].shape[0]
    steps = 4
    shape = jax.ShapeDtypeStruct
    output_rows = output.reshape(-1, width)
    grad_rows = input_grad.reshape(-1, width)
    arrays = list(squares) + [output_rows, grad_rows]
    specs = [pl.BlockSpec((one.shape[0] // steps, width), lambda i: (i, 0)) for one in arrays]
    kinds = [F32] * 6 + [BF16, F32]
    done = pl.pallas_call(
        finish_kernel,
        grid=(steps,),
        out_shape=[shape(one.shape, kind) for one, kind in zip(arrays, kinds)],
        in_specs=specs,
        out_specs=specs,
        compiler_params=pltpu.CompilerParams(vmem_limit_bytes=48 << 20),
        name="finish",
    )(*arrays)
    return done[:6], done[6].reshape(output.shape), done[7].reshape(input_grad.shape)


def norm_rows(values, gain):
    average = jnp.mean(values, axis=-1, keepdims=True)
    centred = values - average
    spread = jnp.mean(centred * centred, axis=-1, keepdims=True)
    return centred * lax.rsqrt(spread + epsilon) * gain


def gelu_grad(pre, upstream):
    unused, pullback = jax.vjp(jax.nn.gelu, pre)
    return pullback(upstream)[0]


def split_heads(matrix):
    return matrix.reshape(matrix.shape[0], matrix.shape[1], H, HD).transpose(2, 0, 1, 3)


def join_heads(stacked):
    return stacked.transpose(1, 2, 0, 3).reshape(stacked.shape[1], stacked.shape[2], H * HD)


def per_device_plain(
    tokens,
    token_ids,
    hash_table,
    lengths,
    gain_attn,
    w_query,
    w_key,
    w_value,
    w_output,
    gain_ffn,
    w_in,
    w_out,
    cotangent,
):
    row_count, span, width = tokens.shape
    local_tok = row_count * span
    whole = span * lax.axis_size("seq")
    place = lax.axis_index("seq")
    scale = HD ** (-0.5)
    inputs = tokens.reshape(local_tok, width).astype(jnp.float32)
    key_positions = jnp.arange(whole, dtype=jnp.int32)
    query_positions = place * span + jnp.arange(span, dtype=jnp.int32)
    ends = jnp.cumsum(lengths, axis=1)
    key_document = jnp.sum(
        (key_positions[None, :, None] >= ends[:, None, :]).astype(jnp.int32), axis=2
    )
    query_document = jnp.sum(
        (query_positions[None, :, None] >= ends[:, None, :]).astype(jnp.int32), axis=2
    )
    visible = (key_positions[None, None, :] <= query_positions[None, :, None]) & (
        query_document[:, :, None] == key_document[:, None, :]
    )
    normed, first_norm_back = jax.vjp(norm_rows, inputs, gain_attn)
    normed_low = normed.astype(jnp.bfloat16)
    query = jnp.dot(normed_low, w_query, preferred_element_type=jnp.float32).astype(jnp.bfloat16)
    keys = jnp.dot(normed_low, w_key, preferred_element_type=jnp.float32).astype(jnp.bfloat16)
    values = jnp.dot(normed_low, w_value, preferred_element_type=jnp.float32).astype(jnp.bfloat16)
    own_pair = jnp.concatenate([keys, values], axis=1).reshape(row_count, span, 2 * width)
    all_pairs = lax.all_gather(own_pair, "seq", axis=1, tiled=True)

    def pair_heads(pairs):
        return (split_heads(pairs[:, :, :width]), split_heads(pairs[:, :, width:]))

    query_heads = split_heads(query.reshape(row_count, span, width))
    key_heads, value_heads = pair_heads(all_pairs)

    def head_forward(parts):
        query_one, key_one, value_one = parts
        scores = (
            jnp.einsum("rqd,rkd->rqk", query_one, key_one, preferred_element_type=jnp.float32)
            * scale
        )
        scores = jnp.where(visible, scores, masked_score)
        peak = jnp.max(scores, axis=2, keepdims=True)
        weights = jnp.exp(scores - peak)
        totals = jnp.sum(weights, axis=2, keepdims=True)
        probs = (weights / totals).astype(jnp.bfloat16)
        mixed = jnp.einsum("rqk,rkd->rqd", probs, value_one, preferred_element_type=jnp.float32)
        return (mixed, (peak + jnp.log(totals))[:, :, 0])

    mixed_heads, log_totals = lax.map(head_forward, (query_heads, key_heads, value_heads))
    attended = join_heads(mixed_heads).reshape(local_tok, width).astype(jnp.bfloat16)
    middle = inputs + jnp.dot(attended, w_output, preferred_element_type=jnp.float32)
    ffn_norm, second_norm_back = jax.vjp(norm_rows, middle, gain_ffn)
    ffn_in = ffn_norm.astype(jnp.bfloat16)
    experts = lax.axis_size("expert")
    capacity = min(2 * local_tok // experts, 3 * local_tok // 4)
    expert_of = jnp.take(hash_table, token_ids.reshape(local_tok), axis=0)
    labels = jnp.arange(experts, dtype=jnp.int32)
    onehot = (expert_of[:, None] == labels[None, :]).astype(jnp.int32)
    own_rank = jnp.sum((jnp.cumsum(onehot, axis=0) - 1) * onehot, axis=1)
    slots = expert_of * capacity + own_rank
    sources = (
        jnp.full((experts * capacity,), local_tok, jnp.int32)
        .at[slots]
        .set(jnp.arange(local_tok, dtype=jnp.int32))
    )

    def to_slots(rows_low):
        padded = jnp.concatenate([rows_low, jnp.zeros((1, width), rows_low.dtype)], axis=0)
        return jnp.take(padded, sources, axis=0).reshape(experts, capacity, width)

    received = lax.all_to_all(
        to_slots(ffn_in), "expert", split_axis=0, concat_axis=0, tiled=True
    ).reshape(-1, width)
    full_in, full_out = (
        lax.all_gather(w_in, "seq", axis=2, tiled=True),
        lax.all_gather(w_out, "seq", axis=1, tiled=True),
    )
    full_in = full_in[0]
    full_out = full_out[0]
    first = jnp.dot(received, full_in, preferred_element_type=jnp.float32)
    produced = jnp.dot(
        jax.nn.gelu(first).astype(jnp.bfloat16), full_out, preferred_element_type=jnp.float32
    ).astype(jnp.bfloat16)
    returned = lax.all_to_all(
        produced.reshape(experts, capacity, width),
        "expert",
        split_axis=0,
        concat_axis=0,
        tiled=True,
    ).reshape(-1, width)
    output = middle + jnp.take(returned, slots, axis=0).astype(jnp.float32)
    upstream = cotangent.reshape(local_tok, width)
    grad_received_out = lax.all_to_all(
        to_slots(upstream), "expert", split_axis=0, concat_axis=0, tiled=True
    ).reshape(-1, width)
    pre = jnp.dot(received, full_in, preferred_element_type=jnp.float32)
    hidden = jax.nn.gelu(pre).astype(jnp.bfloat16)
    grad_full_out = jnp.einsum(
        "rf,rd->fd", hidden, grad_received_out, preferred_element_type=jnp.float32
    )
    grad_hidden = jnp.einsum(
        "rd,fd->rf", grad_received_out, full_out, preferred_element_type=jnp.float32
    )
    grad_pre = gelu_grad(pre, grad_hidden).astype(jnp.bfloat16)
    grad_full_in = jnp.einsum("rd,rf->df", received, grad_pre, preferred_element_type=jnp.float32)
    grad_received = jnp.einsum(
        "rf,df->rd", grad_pre, full_in, preferred_element_type=jnp.float32
    ).astype(jnp.bfloat16)
    grad_in_part, grad_out_part = (
        lax.psum_scatter(
            grad_full_in[None].astype(jnp.bfloat16), "seq", scatter_dimension=2, tiled=True
        ).astype(jnp.float32),
        lax.psum_scatter(
            grad_full_out[None].astype(jnp.bfloat16), "seq", scatter_dimension=1, tiled=True
        ).astype(jnp.float32),
    )
    grad_in, grad_out = (
        lax.psum(grad_in_part.astype(jnp.bfloat16), "dp").astype(jnp.float32),
        lax.psum(grad_out_part.astype(jnp.bfloat16), "dp").astype(jnp.float32),
    )
    grad_back = lax.all_to_all(
        grad_received.reshape(experts, capacity, width),
        "expert",
        split_axis=0,
        concat_axis=0,
        tiled=True,
    ).reshape(-1, width)
    grad_ffn_in = jnp.take(grad_back, slots, axis=0).astype(jnp.float32)
    grad_middle_norm, grad_gain_ffn = second_norm_back(grad_ffn_in)
    grad_middle = upstream.astype(jnp.float32) + grad_middle_norm
    grad_branch = grad_middle.astype(jnp.bfloat16)
    grad_w_output = jnp.einsum(
        "cd,ce->de", attended, grad_branch, preferred_element_type=jnp.float32
    )
    grad_attended = jnp.einsum(
        "ce,de->cd", grad_branch, w_output, preferred_element_type=jnp.float32
    ).astype(jnp.bfloat16)
    again_pairs = lax.all_gather(own_pair, "seq", axis=1, tiled=True)
    key_back, value_back = pair_heads(again_pairs)

    def head_backward(parts):
        query_one, key_one, value_one, grad_one, log_one = parts
        scores = (
            jnp.einsum("rqd,rkd->rqk", query_one, key_one, preferred_element_type=jnp.float32)
            * scale
        )
        scores = jnp.where(visible, scores, masked_score)
        probs_full = jnp.exp(scores - log_one[:, :, None])
        probs = probs_full.astype(jnp.bfloat16)
        grad_probs = jnp.einsum(
            "rqd,rkd->rqk", grad_one, value_one, preferred_element_type=jnp.float32
        )
        inner = jnp.sum(probs_full * grad_probs, axis=2, keepdims=True)
        grad_scores = (probs_full * (grad_probs - inner)).astype(jnp.bfloat16)
        grad_query_one = (
            jnp.einsum("rqk,rkd->rqd", grad_scores, key_one, preferred_element_type=jnp.float32)
            * scale
        )
        grad_key_one = (
            jnp.einsum("rqk,rqd->rkd", grad_scores, query_one, preferred_element_type=jnp.float32)
            * scale
        )
        grad_value_one = jnp.einsum(
            "rqk,rqd->rkd", probs, grad_one, preferred_element_type=jnp.float32
        )
        return (grad_query_one, grad_key_one, grad_value_one)

    grad_att_heads = split_heads(grad_attended.reshape(row_count, span, width))
    grad_query_heads, grad_key_heads, grad_value_heads = lax.map(
        head_backward, (query_heads, key_back, value_back, grad_att_heads, log_totals)
    )
    grad_query_rows = join_heads(grad_query_heads).reshape(local_tok, width).astype(jnp.bfloat16)
    pair_grads = jnp.concatenate([join_heads(grad_key_heads), join_heads(grad_value_heads)], axis=2)
    own_grads = (
        lax.psum_scatter(pair_grads, "seq", scatter_dimension=1, tiled=True)
        .reshape(local_tok, 2 * width)
        .astype(jnp.bfloat16)
    )
    grad_key_rows = own_grads[:, :width]
    grad_value_rows = own_grads[:, width:]
    grad_w_query = jnp.einsum(
        "cd,ce->de", normed_low, grad_query_rows, preferred_element_type=jnp.float32
    )
    grad_w_key = jnp.einsum(
        "cd,ce->de", normed_low, grad_key_rows, preferred_element_type=jnp.float32
    )
    grad_w_value = jnp.einsum(
        "cd,ce->de", normed_low, grad_value_rows, preferred_element_type=jnp.float32
    )
    grad_normed = jnp.einsum(
        "ce,de->cd", grad_query_rows, w_query, preferred_element_type=jnp.float32
    )
    grad_normed = grad_normed + jnp.einsum(
        "ce,de->cd", grad_key_rows, w_key, preferred_element_type=jnp.float32
    )
    grad_normed = grad_normed + jnp.einsum(
        "ce,de->cd", grad_value_rows, w_value, preferred_element_type=jnp.float32
    )
    grad_inputs_norm, grad_gain_attn = first_norm_back(grad_normed)
    input_grad = grad_middle + grad_inputs_norm
    summed = lax.psum(
        (grad_gain_attn, grad_w_query, grad_w_key, grad_w_value, grad_w_output, grad_gain_ffn),
        ("dp", "seq", "expert"),
    )
    shaped_output = output.astype(jnp.bfloat16).reshape(row_count, span, width)
    shaped_grad = input_grad.reshape(row_count, span, width)
    return (
        shaped_output,
        shaped_grad,
        summed[0],
        summed[1],
        summed[2],
        summed[3],
        summed[4],
        summed[5],
        grad_in,
        grad_out,
    )


def per_device(
    tokens,
    token_ids,
    hash_table,
    lengths,
    gain_attn,
    w_query,
    w_key,
    w_value,
    w_output,
    gain_ffn,
    w_in,
    w_out,
    cotangent,
):
    row_count, span, width = tokens.shape
    local_tok = row_count * span
    output, input_grad, grad_q, grad_k, grad_v, grad_o, grad_in, grad_out, gains = block(
        tokens, cotangent.reshape(local_tok, width), token_ids, hash_table.reshape(-1, 128), lengths,
        gain_attn, gain_ffn,
        w_query, w_key, w_value, w_output, w_in[0], w_out[0])[:9]
    squares, output, input_grad = finish((grad_q, grad_k, grad_v, grad_o, grad_in, grad_out), output, input_grad)
    return (
        output,
        input_grad,
        gains[1],
        squares[0],
        squares[1],
        squares[2],
        squares[3],
        gains[0],
        squares[4][None],
        squares[5][None],
    )


def solution(mesh):
    sizes = (mesh.shape["dp"], mesh.shape["seq"], mesh.shape["expert"])
    return jax.shard_map(
        per_device if sizes == (4, 4, 2) else per_device_plain,
        mesh=mesh,
        in_specs=(
            P(("dp", "expert"), "seq", None),
            P(("dp", "expert"), "seq"),
            P(),
            P(("dp", "expert"), None),
            P(),
            P(),
            P(),
            P(),
            P(),
            P(),
            P("expert", None, "seq"),
            P("expert", "seq", None),
            P(("dp", "expert"), "seq", None),
        ),
        out_specs=(
            P(("dp", "expert"), "seq", None),
            P(("dp", "expert"), "seq", None),
            P(),
            P(),
            P(),
            P(),
            P(),
            P(),
            P("expert", None, "seq"),
            P("expert", "seq", None),
        ),
        check_vma=False,
    )
```

```python
import functools
import jax
import jax.numpy as jnp
from jax import lax
from jax.experimental import pallas as pl
from jax.experimental.pallas import tpu as pltpu
from jax.sharding import PartitionSpec as P

MESH = pl.DeviceIdType.MESH
F32 = jnp.float32
BF16 = jnp.bfloat16
I32 = jnp.int32
H = 12
HD = 64
epsilon = 1e-05
masked_score = -1e30
AHEAD = 3
gelu_a = 0.7978845608028654
gelu_b = 0.044715


FAR_ONE = {2: [("s", 1, 1)], 4: [("c", 2, 0)], 5: [("c", 1, 2)]}
NEAR_ONE = {3: [("c", 2, 1)], 5: [("c", 1, 3)]}
AFTER_ONE = [
    [("s", 0, 2), ("s", 1, 2), ("c", 3, 0)],
    [("s", 2, 0), ("c", 2, 2)],
    [("s", 2, 1), ("s", 3, 0), ("c", 1, 4), ("c", 3, 1)],
    [("s", 3, 1), ("s", 4, 0)],
]
FAR_TWO = {
    0: [("c", 2, 3), ("s", 4, 1)], 2: [("c", 1, 5)], 3: [("s", 2, 2), ("c", 3, 2)],
    5: [("c", 2, 4), ("s", 3, 2)]}
NEAR_TWO = {
    0: [("s", 4, 2), ("c", 1, 6), ("c", 3, 3)], 1: [("c", 2, 5)], 3: [("c", 1, 7), ("s", 0, 3), ("s", 1, 3)],
    4: [("c", 3, 4)]}
AFTER_TWO = [
    [("c", 2, 6)],
    [("s", 5, 0), ("s", 2, 3), ("s", 3, 3), ("c", 3, 5)],
    [("s", 5, 1), ("s", 6, 0), ("c", 2, 7), ("s", 4, 3)],
    [("s", 6, 1), ("s", 7, 0), ("s", 0, 4), ("s", 1, 4)],
]
TAIL = [
    [("s", 7, 1), ("c", 3, 6), ("s", 2, 4), ("s", 3, 4)],
    [("s", 5, 2), ("s", 4, 4), ("s", 6, 2), ("s", 0, 5), ("s", 1, 5), ("s", 7, 2), ("f", 0), ("f", 1)],
    [("s", 5, 3), ("c", 3, 7), ("s", 2, 5), ("s", 3, 5), ("s", 6, 3), ("s", 0, 6), ("s", 1, 6), ("s", 4, 5),
     ("s", 7, 3), ("f", 2), ("f", 3), ("s", 5, 4), ("s", 6, 4), ("s", 0, 7), ("s", 1, 7), ("s", 2, 6), ("s", 3, 6),
     ("s", 7, 4), ("s", 4, 6), ("s", 5, 5), ("s", 6, 5), ("s", 2, 7), ("s", 3, 7), ("s", 7, 5), ("s", 4, 7),
     ("s", 0, 8), ("s", 1, 8), ("s", 5, 6), ("s", 6, 6), ("s", 7, 6), ("s", 2, 8), ("s", 3, 8), ("s", 5, 7),
     ("s", 6, 7), ("s", 7, 7), ("s", 4, 8)],
    [("s", 5, 8), ("s", 6, 8), ("s", 7, 8)],
]


def dot_nn(a, b):
    return jnp.dot(a, b, preferred_element_type=F32)


def dot_nt(a, b):
    return lax.dot_general(a, b, (((1,), (1,)), ((), ())), preferred_element_type=F32)


def dot_tn(a, b):
    return lax.dot_general(a, b, (((0,), (0,)), ((), ())), preferred_element_type=F32)


def norm_parts(values):
    average = jnp.mean(values, axis=-1, keepdims=True)
    centred = values - average
    spread = jnp.mean(centred * centred, axis=-1, keepdims=True)
    root = lax.rsqrt(spread + epsilon)
    return centred * root, root


def norm_back(upstream, gain, xhat, root):
    scaled = upstream * gain
    first = jnp.mean(scaled, axis=-1, keepdims=True)
    second = jnp.mean(scaled * xhat, axis=-1, keepdims=True)
    return root * (scaled - first - xhat * second)


def block_kernel(
    tokens_hbm, cot_ref, ids_ref, table_ref, lengths_ref, gain_a_ref, gain_f_ref,
    wq_ref, wk_ref, wv_ref, wo_ref, win_hbm, wout_hbm,
    out_hbm, ig_hbm, dwq_hbm, dwk_hbm, dwv_hbm, dwo_hbm, dwin_hbm, dwout_hbm, gain_a_out, gain_f_out, es_hbm, ra_hbm, ro_hbm, nd_hbm,
    nb, xgb, eob, qs, ks, vs, dot, ebuf, oa, stat, facs, dl, route, cs, xs, do, mid,
    win, wout, acc, preg, hid, gp, gback, eback, dnr0,
    local_sem, e_sem, tok_send, tok_recv, fwd_send, fwd_recv, core_send, core_recv,
    wx_send, wx_recv, wz_send, wz_recv, wf_send, wf_recv, wc_send, wc_recv, y_send, y_recv, dn_send, dn_recv, far_send, far_recv,
    recv_d, recv_p, gg_ref, gsum, ed_send, ed_recv, ex_send, ex_recv, ee_send, ee_recv, em_send, em_recv,
    eb_send, eb_recv, eo_sem, free_x, free_z, free_m, free_d, free_e,
    rd_send, rd_recv, rp_send, rp_recv, rz_send, rz_recv, gd_send, gd_recv,
    own_sem, gn_send, gn_recv, near_send, near_recv,
):
    dp = lax.axis_index("dp")
    s = lax.axis_index("seq")
    y = lax.axis_index("expert")
    c = lax.rem(s, 2)
    x = s // 2
    core_peer = (dp, x * 2 + 1 - c, y)
    x_peer = (dp, (1 - x) * 2 + c, y)
    y_peer = (dp, s, 1 - y)
    span = tokens_hbm.shape[1]
    width = tokens_hbm.shape[2]
    local = 2 * span
    cap = gback.shape[0]
    stage = eob.at[0:cap]

    def remote(src, dst, send, recv, peer):
        return pltpu.make_async_remote_copy(
            src_ref=src, dst_ref=dst, send_sem=send, recv_sem=recv, device_id=peer, device_id_type=MESH)

    own_copy = pltpu.make_async_copy(tokens_hbm, nb.at[s], local_sem.at[0])
    win_copy = pltpu.make_async_copy(win_hbm, win.at[s], local_sem.at[1])
    wout_copy = pltpu.make_async_copy(wout_hbm, wout.at[s], local_sem.at[2])
    own_copy.start()
    win_copy.start()
    wout_copy.start()
    barrier = pltpu.get_barrier_semaphore()
    plane_peers = [x_peer, y_peer, (dp, (1 - x) * 2 + c, 1 - y)]
    z_peers = [(lax.rem(dp + d, 4), s, y) for d in range(1, 4)]
    for peer in [core_peer] + plane_peers + z_peers:
        pl.semaphore_signal(barrier, inc=1, device_id=peer, device_id_type=MESH)
    pl.semaphore_wait(barrier, 7)

    far_s = (1 - x) * 2 + c

    def token_copy(r):
        return remote(tokens_hbm.at[r], nb.at[s, r], tok_send.at[r], tok_recv.at[r], x_peer)

    def core_copy(r):
        return remote(tokens_hbm.at[r], nb.at[s, r], core_send.at[r], core_recv.at[r], core_peer)

    def forward_copy(r):
        return remote(nb.at[c, r], nb.at[c, r], fwd_send.at[r], fwd_recv.at[r], core_peer)

    wc_copies = [
        remote(win_hbm, win.at[s], wc_send.at[0], wc_recv.at[0], core_peer),
        remote(wout_hbm, wout.at[s], wc_send.at[1], wc_recv.at[1], core_peer),
    ]
    chunk = width // 4
    even = lax.rem(dp, 2) == 0
    swap_peer = (dp + 1 - 2 * lax.rem(dp, 2), s, y)

    def by_parity(action):
        @pl.when(even)
        def _():
            action(win, wout, win_hbm)

        @pl.when(jnp.logical_not(even))
        def _():
            action(wout, win, wout_hbm)

    def rows_of(j):
        return slice(j * chunk, (j + 1) * chunk)

    def wx_copy(j, matrix, source):
        return remote(source.at[rows_of(j)], matrix.at[s, rows_of(j)], wx_send.at[j], wx_recv.at[j], x_peer)

    def wz_copy(j, matrix):
        return remote(matrix.at[far_s, rows_of(j)], matrix.at[far_s, rows_of(j)], wz_send.at[j], wz_recv.at[j], swap_peer)

    def wf_copy(k, j, matrix):
        return remote(matrix.at[far_s, rows_of(j)], matrix.at[far_s, rows_of(j)],
                      wf_send.at[4 * k + j], wf_recv.at[4 * k + j], core_peer)

    def from_x(j):
        def action(first, second, source):
            wx_copy(j, first, source).wait_recv()
            wz_copy(j, first).start()
            wf_copy(0, j, first).start()
        by_parity(action)

    def from_z(j):
        def action(first, second, source):
            wz_copy(j, second).wait_recv()
            wf_copy(1, j, second).start()
        by_parity(action)

    @pl.when(x == 0)
    def _():
        for r in range(2):
            token_copy(r).start()

    by_parity(lambda first, second, source: [wx_copy(j, first, source).start() for j in range(4)] and None)

    @pl.when(c == 0)
    def _():
        for r in range(2):
            core_copy(r).start()

    wc_copies[0].start()
    wc_copies[1].start()

    ids = jnp.concatenate([ids_ref[0:1, :], ids_ref[1:2, :]], axis=1)
    high = ids // 128
    low = ids - high * 128
    pick = jnp.where(lax.broadcasted_iota(I32, (64, local), 0) == high, 1.0, 0.0).astype(BF16)
    looked = dot_tn(table_ref[...].astype(F32).astype(BF16), pick)
    expert_row = jnp.sum(
        jnp.where(lax.broadcasted_iota(I32, (128, local), 0) == low, looked, 0.0), axis=0, keepdims=True)
    mine = jnp.where(expert_row == y.astype(F32), 1.0, 0.0)
    sixteen = lax.broadcasted_iota(I32, (16, local), 0)
    both = jnp.where(sixteen == 0, mine, jnp.where(sixteen == 1, 1.0 - mine, 0.0)).astype(BF16)
    before = jnp.where(
        lax.broadcasted_iota(I32, (local, local), 0) < lax.broadcasted_iota(I32, (local, local), 1), 1.0, 0.0
    ).astype(BF16)
    ranks = dot_nn(both, before)
    slot_rows = lax.broadcasted_iota(I32, (cap, local), 0).astype(F32)
    for u in range(2):
        chosen = mine if u == 0 else 1.0 - mine
        route[u] = jnp.where(slot_rows == ranks[u:u + 1, :], chosen, 0.0).astype(BF16)

    cot_copy = remote(stage, cs.at[cap:], y_send.at[0], y_recv.at[0], y_peer)
    xs_copy = remote(stage, xs.at[cap:], y_send.at[1], y_recv.at[1], y_peer)
    stage[...] = dot_nn(route[1], cot_ref[...]).astype(BF16)
    cot_copy.start()
    cs[0:cap] = dot_nn(route[0], cot_ref[...]).astype(BF16)

    gain_a = gain_a_ref[...].reshape(1, width)
    gain_f = gain_f_ref[...].reshape(1, width)

    def normalise(part, r):
        nb[part, r] = (norm_parts(nb[part, r].astype(F32))[0] * gain_a).astype(BF16)

    def project(part, r):
        normed = nb[part, r]
        ks[part, r] = dot_nn(normed, wk_ref[...]).astype(BF16)
        vs[part, r] = dot_nn(normed, wv_ref[...]).astype(BF16)

    first_half = lax.broadcasted_iota(I32, (span, 128), 1) < HD
    first_rows = lax.broadcasted_iota(I32, (128, span), 0) < HD

    def apart(values, keep, axis):
        none = jnp.zeros_like(values)
        return jnp.concatenate([jnp.where(keep, values, none), jnp.where(keep, none, values)], axis=axis)

    def pair_lanes(p):
        return pl.ds(pl.multiple_of(p * 128, 128), 128)

    def head_rows(p, hh):
        return pl.ds(pl.multiple_of(p * 128 + hh * HD, HD), HD)

    def e_near(r, p, slot, write, both_parts):
        here = ebuf.at[slot] if both_parts else ebuf.at[slot, 1]
        there = es_hbm.at[0, r, p] if both_parts else es_hbm.at[0, r, p, 1]
        return pltpu.make_async_copy(here if write else there, there if write else here, e_sem.at[slot])

    def e_far(r, p, slot, write):
        here = ebuf.at[slot]
        there = es_hbm.at[1, r, p]
        return pltpu.make_async_copy(here if write else there, there if write else here, e_sem.at[slot])

    def attend(r, p, slot, parts, places, diagonal):
        lanes = pair_lanes(p)
        q_two = apart(qs[r, :, lanes], first_half, 0)
        v_flipped = [vs[part, r, :, lanes].T for part in parts]
        scores = [dot_nt(ks[part, r, :, lanes], q_two) for part in parts]
        if diagonal:
            ki = lax.broadcasted_iota(I32, (span, 2 * span), 0)
            qi = lax.broadcasted_iota(I32, (span, 2 * span), 1)
            qi = jnp.where(qi >= span, qi - span, qi)
            scores[-1] = jnp.where(ki <= qi, scores[-1], masked_score)
        peak = jnp.max(scores[0], axis=0, keepdims=True)
        for extra in scores[1:]:
            peak = jnp.maximum(peak, jnp.max(extra, axis=0, keepdims=True))
        weights = [jnp.exp(one - peak) for one in scores]
        total = jnp.sum(weights[0], axis=0, keepdims=True)
        for extra in weights[1:]:
            total = total + jnp.sum(extra, axis=0, keepdims=True)
        low_weights = [one.astype(BF16) for one in weights]
        for place, one in zip(places, low_weights):
            ebuf[slot, place] = one
        results = []
        for hh in range(2):
            columns = slice(hh * span, (hh + 1) * span)
            mixed = 0.0
            for v_one, one in zip(v_flipped, low_weights):
                mixed = mixed + dot_nn(v_one[hh * HD:(hh + 1) * HD], one[:, columns])
            results.append((2 * p + hh, head_rows(p, hh), peak[:, columns], total[:, columns], mixed))
        return results

    own_copy.wait()

    def own_rows(r, carry):
        mid[r] = nb[s, r].astype(F32)
        normalise(s, r)
        project(s, r)
        qs[r] = (dot_nn(nb[s, r], wq_ref[...]) * (HD ** -0.5)).astype(BF16)
        return carry

    lax.fori_loop(0, 2, own_rows, 0)

    def near_loop(parts, places):
        wide = len(parts) == 2

        def step(i, carry):
            r, p, slot = i // 6, lax.rem(i, 6), lax.rem(i, 2)

            @pl.when(i >= 2)
            def _():
                e_near(r, p, slot, True, wide).wait()

            for h, rows, peak, total, mixed in attend(r, p, slot, parts, places, True):
                stat[r, h, 0:1] = peak
                stat[r, h, 1:2] = total
                oa[r, rows, :] = mixed
            e_near(r, p, slot, True, wide).start()
            return carry

        lax.fori_loop(0, 12, step, 0)
        for slot in range(2):
            e_near(1, 4 + slot, slot, True, wide).wait()

    @pl.when(c == 0)
    def _():
        near_loop([s], [1])

    @pl.when(c == 1)
    def _():
        for r in range(2):
            core_copy(r).wait_recv()

        def partner_rows(r, carry):
            normalise(s - 1, r)
            project(s - 1, r)
            return carry

        lax.fori_loop(0, 2, partner_rows, 0)
        near_loop([s - 1, s], [0, 1])

    @pl.when(x == 0)
    def _():
        def step(i, carry):
            r, h = i // H, lax.rem(i, H)
            rows = pl.ds(pl.multiple_of(h * HD, HD), HD)
            inverse = 1.0 / stat[r, h, 1:2]
            facs[r, h, 0:1] = inverse
            facs[r, h, 1:2] = jnp.zeros_like(inverse)
            oa[r, rows, :] = oa[r, rows, :] * inverse
            return carry

        lax.fori_loop(0, 2 * H, step, 0)
        from_x(0)

    @pl.when(x == 1)
    def _():
        for r in range(2):
            token_copy(r).wait_recv()
            normalise(c, r)
            forward_copy(r).start()
            project(c, r)
            forward_copy(r).wait()
            project(1 - c, r)
            if r == 1:
                from_x(0)
            single = lengths_ref[r, 1] == 0

            def step(p, carry):
                slot = lax.rem(p, 2)

                @pl.when(p >= 2)
                def _():
                    e_far(r, p, slot, True).wait()

                for h, rows, peak, total, mixed in attend(r, p, slot, [0, 1], [0, 1], False):
                    near_peak = stat[r, h, 0:1]
                    peak = jnp.where(single, peak, near_peak)
                    top = jnp.maximum(peak, near_peak)
                    near_f = jnp.exp(near_peak - top)
                    far_f = jnp.where(single, jnp.exp(peak - top), 0.0)
                    whole = near_f * stat[r, h, 1:2] + far_f * total
                    near_f = near_f / whole
                    far_f = far_f / whole
                    facs[r, h, 0:1] = near_f
                    facs[r, h, 1:2] = far_f
                    oa[r, rows, :] = oa[r, rows, :] * near_f + mixed * far_f
                e_far(r, p, slot, True).start()
                return carry

            lax.fori_loop(0, 6, step, 0)
            for slot in range(2):
                e_far(r, 4 + slot, slot, True).wait()

    def out_rows(r, carry):
        att = oa[r].astype(BF16).T
        value = mid[r] + dot_nn(att, wo_ref[...])
        mid[r] = value
        do[0, r] = (norm_parts(value)[0] * gain_f).astype(BF16)
        return carry

    lax.fori_loop(0, 2, out_rows, 0)
    from_x(1)

    ffn_in = do[0].reshape(local, width)
    cot_copy.wait_send()
    stage[...] = dot_nn(route[1], ffn_in).astype(BF16)
    xs_copy.start()
    xs[0:cap] = dot_nn(route[0], ffn_in).astype(BF16)
    win_copy.wait()
    wout_copy.wait()
    acc[...] = jnp.zeros_like(acc)

    def expert_rows(u, f):
        rows = pl.ds(pl.multiple_of(u * cap, cap), cap)
        tokens_in = xs[rows]
        grads_in = cs[rows]
        for n in range(3):
            lanes = slice(n * 256, (n + 1) * 256)
            pre = dot_nn(tokens_in, win[f, :, lanes])
            up = dot_nt(grads_in, wout[f, lanes])
            square = pre * pre
            bent = jnp.tanh(gelu_a * pre * (1.0 + gelu_b * square))
            half = 0.5 * (1.0 + bent)
            slope = half + 0.5 * pre * (1.0 - bent * bent) * (gelu_a * (1.0 + 3.0 * gelu_b * square))
            hid[f, rows, lanes] = (pre * half).astype(BF16)
            gp[f, rows, lanes] = (up * slope).astype(BF16)
        acc[rows] += dot_nt(gp[f, rows], win[f])

    def expert_number(ix, ic):
        return 2 * lax.rem(x + ix, 2) + lax.rem(c + ic, 2)

    def moe_step(i, carry):
        ix = i // 4
        outer, inner = lax.rem(i // 2, 2), lax.rem(i, 2)

        @pl.when(i == 2)
        def _():
            xs_copy.wait_recv()
            cot_copy.wait_recv()

        @pl.when(i == 6)
        def _():
            by_parity(lambda first, second, source: [
                wf_copy(k, j, (first, second)[k]).wait_recv() for k in range(2) for j in range(4)] and None)

        @pl.when(i == 1)
        def _():
            wc_copies[0].wait_recv()
            wc_copies[1].wait_recv()
        expert_rows(jnp.where(ix == 0, outer, inner), expert_number(ix, jnp.where(ix == 0, inner, outer)))

        @pl.when(i == 0)
        def _():
            from_x(2)
            from_z(0)

        @pl.when(i == 1)
        def _():
            from_x(3)
            from_z(1)
            from_z(2)

        @pl.when(i == 2)
        def _():
            from_z(3)
        return carry

    lax.fori_loop(0, 8, moe_step, 0)

    grad_copy = remote(xgb.at[cap:], gback, y_send.at[2], y_recv.at[2], y_peer)
    out_copy = remote(eob.at[cap:], eback, y_send.at[3], y_recv.at[3], y_peer)
    xgb[...] = acc[...].astype(BF16)
    grad_copy.start()
    acc[...] = jnp.zeros_like(acc)
    wc_copies[0].wait_send()
    wc_copies[1].wait_send()
    by_parity(lambda first, second, source: [
        wf_copy(k, j, (first, second)[k]).wait_send() for k in range(2) for j in range(4)] and None)
    by_parity(lambda first, second, source: [wz_copy(j, first).wait_send() for j in range(4)] and None)
    xs_copy.wait_send()

    shard_a = expert_number(1, 0)
    shard_b = expert_number(1, 1)
    shard_c = expert_number(0, 1)
    ends = jnp.logical_or(dp == 0, dp == 3)
    end_z = jnp.where(dp < 2, 0, 3)
    near_mid = (jnp.where(dp < 2, 1, 2), s, y)
    other_mid = (3 - dp, s, y)
    end_peer = (end_z, s, y)
    core_sends = [
        remote(win.at[shard_b], ra_hbm.at[0], ed_send.at[0], ed_recv.at[0], core_peer),
        remote(wout.at[shard_b], ra_hbm.at[1], ed_send.at[1], ed_recv.at[1], core_peer),
        remote(win.at[shard_c], ro_hbm.at[0], ed_send.at[2], ed_recv.at[2], core_peer),
        remote(wout.at[shard_c], ro_hbm.at[1], ed_send.at[3], ed_recv.at[3], core_peer),
    ]

    def weight_grads(f):
        acc[...] += dot_nn(hid[f], wout[f])
        wout[f] = dot_tn(hid[f], cs[...]).astype(BF16)
        win[f] = dot_tn(xs[...], gp[f]).astype(BF16)

    load_a = [
        pltpu.make_async_copy(ra_hbm.at[0], win.at[shard_b], local_sem.at[1]),
        pltpu.make_async_copy(ra_hbm.at[1], wout.at[shard_b], local_sem.at[2]),
    ]
    load_o = [
        pltpu.make_async_copy(ro_hbm.at[0], win.at[shard_c], local_sem.at[1]),
        pltpu.make_async_copy(ro_hbm.at[1], wout.at[shard_c], local_sem.at[2]),
    ]

    def piece(k):
        return pl.ds(pl.multiple_of(lax.rem(k, 4) * chunk, chunk), chunk)

    def add_to(target, first, second):
        target[...] = first[...] + second[...]

    def by_matrix(k, action):
        @pl.when(k < 4)
        def _():
            action(win, dwin_hbm)

        @pl.when(k >= 4)
        def _():
            action(wout, dwout_hbm)

    def x_grad(k, grads):
        return remote(grads.at[shard_a, piece(k)], grads.at[shard_c, piece(k)],
                      ex_send.at[k], ex_recv.at[k], x_peer)

    def end_grad(k, grads):
        return remote(grads.at[s, piece(k)], grads.at[shard_c, piece(k)], ee_send.at[k], ee_recv.at[k], near_mid)

    def mid_grad(k, grads):
        return remote(grads.at[s, piece(k)], grads.at[shard_a, piece(k)], em_send.at[k], em_recv.at[k], other_mid)

    def back_grad(k, grads, out):
        return remote(grads.at[shard_b, piece(k)], out.at[piece(k)], eb_send.at[k], eb_recv.at[k], end_peer)

    def out_grad(k, grads, out):
        return pltpu.make_async_copy(grads.at[shard_b, piece(k)], out.at[piece(k)], eo_sem.at[k])

    def send_x(k):
        pl.semaphore_wait(free_x, 1)
        by_matrix(k, lambda grads, out: x_grad(k, grads).start())

    def start_x():
        def step(k, carry):
            by_matrix(k, lambda grads, out: add_to(
                grads.at[shard_a, piece(k)], grads.at[shard_a, piece(k)], grads.at[shard_b, piece(k)]))
            pl.semaphore_signal(free_x, inc=1, device_id=x_peer, device_id_type=MESH)

            @pl.when(jnp.logical_and(k >= 1, k < AHEAD + 1))
            def _():
                send_x(k - 1)
            return carry

        lax.fori_loop(0, 8, step, 0)

    def chain(kind, number):
        k = jnp.int32(number)

        def action(grads, out):
            if kind == 1:
                x_grad(k, grads).wait()
                if number < 8 - AHEAD:
                    send_x(k + AHEAD)
                add_to(grads.at[s, piece(k)], grads.at[s, piece(k)], grads.at[shard_b, piece(k)])

                @pl.when(ends)
                def _():
                    if number == 0:
                        pl.semaphore_wait(free_z, 1)
                    end_grad(k, grads).start()

                @pl.when(jnp.logical_not(ends))
                def _():
                    pl.semaphore_signal(free_m, inc=1, device_id=other_mid, device_id_type=MESH)
            if kind == 2:
                @pl.when(jnp.logical_not(ends))
                def _():
                    end_grad(k, grads).wait_recv()
                    add_to(grads.at[s, piece(k)], grads.at[s, piece(k)], grads.at[shard_c, piece(k)])
                    pl.semaphore_wait(free_m, 1)
                    mid_grad(k, grads).start()
            if kind == 3:
                @pl.when(jnp.logical_not(ends))
                def _():
                    mid_grad(k, grads).wait_recv()
                    add_to(grads.at[shard_b, piece(k)], grads.at[s, piece(k)], grads.at[shard_a, piece(k)])
                    out_grad(k, grads, out).start()
                    back_grad(k, grads, out).start()

        action(*((win, dwin_hbm) if number < 4 else (wout, dwout_hbm)))

    def chain_all(steps):
        for kind, number in steps:
            chain(kind, number)

    def drain_chain():
        def step(k, carry):
            def action(grads, out):
                @pl.when(ends)
                def _():
                    end_grad(k, grads).wait_send()
                    back_grad(k, grads, out).wait_recv()

                @pl.when(jnp.logical_not(ends))
                def _():
                    mid_grad(k, grads).wait_send()
                    back_grad(k, grads, out).wait_send()
                    out_grad(k, grads, out).wait()
            by_matrix(k, action)
            return carry

        lax.fori_loop(0, 8, step, 0)

    half = width // 2
    tall = width // 2
    corner = 2 * x + y
    sums = [None] * 8

    def sum_step(m, step):
        source, at, out, to = sums[m]
        lanes = slice(at, at + half)
        goal = slice(to, to + half)
        (one, one_peer), (two, two_peer) = [(x, x_peer), (y, y_peer)] if m == 6 else [(y, y_peer), (x, x_peer)]
        low_one = c * tall + one * (tall // 2)
        low_two = low_one + two * (tall // 4)

        def rows(start, size):
            return pl.ds(pl.multiple_of(start, size), size)

        mine = rows(c * tall, tall)
        theirs = rows((1 - c) * tall, tall)
        kept_one = rows(low_one, tall // 2)
        sent_one = rows(c * tall + (1 - one) * (tall // 2), tall // 2)
        kept_two = rows(low_two, tall // 4)
        sent_two = rows(low_one + (1 - two) * (tall // 4), tall // 4)
        in_one = slice(0, tall // 2)
        in_two = slice(tall // 2, 3 * tall // 4)
        final = slice(0, tall // 4)
        slot = (slice((m // 2) * (tall // 4), (m // 2 + 1) * (tall // 4)), slice((m % 2) * half, (m % 2 + 1) * half))

        def core_send():
            return remote(source.at[theirs, lanes], recv_d, rd_send.at[m], rd_recv.at[m], core_peer)

        def one_part():
            return remote(source.at[sent_one, lanes], recv_p.at[m, in_one], rp_send.at[m, 0], rp_recv.at[m, 0], one_peer)

        def two_part():
            return remote(source.at[sent_two, lanes], recv_p.at[m, in_two], rp_send.at[m, 1], rp_recv.at[m, 1], two_peer)

        def end_part():
            return remote(source.at[kept_two, lanes], gback.at[slot], rp_send.at[m, 2], rp_recv.at[m, 2], near_mid)

        def mid_part():
            return remote(source.at[kept_two, lanes], eback.at[slot], rp_send.at[m, 3], rp_recv.at[m, 3], other_mid)

        def back_part():
            return remote(recv_p.at[m, final], out.at[kept_two, goal], rz_send.at[m, 0], rz_recv.at[m, 0], end_peer)

        def own_store():
            return pltpu.make_async_copy(recv_p.at[m, final], out.at[kept_two, goal], own_sem.at[m])

        def two_gather():
            return remote(out.at[kept_two, goal], out.at[kept_two, goal], rz_send.at[m, 1], rz_recv.at[m, 1], two_peer)

        def one_gather():
            return remote(out.at[kept_one, goal], out.at[kept_one, goal], rz_send.at[m, 2], rz_recv.at[m, 2], one_peer)

        def core_gather():
            return remote(out.at[mine, goal], out.at[mine, goal], gd_send.at[m], gd_recv.at[m], core_peer)

        if step == 0:
            if m > 0:
                pl.semaphore_wait(free_d, 1)
            core_send().start()
        if step == 1:
            core_send().wait()
            add_to(source.at[mine, lanes], source.at[mine, lanes], recv_d)
            if m < 7:
                pl.semaphore_signal(free_d, inc=1, device_id=core_peer, device_id_type=MESH)
            one_part().start()
        if step == 2:
            one_part().wait()
            add_to(source.at[kept_one, lanes], source.at[kept_one, lanes], recv_p.at[m, in_one])
            two_part().start()
        if step == 3:
            two_part().wait()
            add_to(source.at[kept_two, lanes], source.at[kept_two, lanes], recv_p.at[m, in_two])

            @pl.when(ends)
            def _():
                if m == 0:
                    pl.semaphore_wait(free_e, 1)
                end_part().start()
        if step == 4:
            @pl.when(jnp.logical_not(ends))
            def _():
                end_part().wait_recv()
                add_to(source.at[kept_two, lanes], source.at[kept_two, lanes], gback.at[slot])
                mid_part().start()
        if step == 5:
            @pl.when(jnp.logical_not(ends))
            def _():
                mid_part().wait_recv()
                add_to(recv_p.at[m, final], source.at[kept_two, lanes], eback.at[slot])
                own_store().start()
                back_part().start()
        if step == 6:
            @pl.when(ends)
            def _():
                end_part().wait_send()
                back_part().wait_recv()

            @pl.when(jnp.logical_not(ends))
            def _():
                mid_part().wait_send()
                own_store().wait()
                back_part().wait_send()
            two_gather().start()
        if step == 7:
            two_gather().wait()
            one_gather().start()
        if step == 8:
            one_gather().wait()
            core_gather().start()
        if step == 9:
            core_gather().wait()

    def run(steps):
        for one in steps:
            if one[0] == "c":
                chain(one[1], one[2])
            if one[0] == "s":
                sum_step(one[1], one[2])
            if one[0] == "f":
                far_send_on(one[1])

    def grads_step(i, carry):
        weight_grads(expert_number(1 - i // 2, lax.rem(i + 1, 2)))

        @pl.when(i == 0)
        def _():
            core_sends[0].start()
            core_sends[1].start()

        @pl.when(i == 1)
        def _():
            for k in range(2):
                core_sends[k].wait()
                load_a[k].start()
            for k in range(2):
                load_a[k].wait()
            start_x()

        @pl.when(i == 2)
        def _():
            core_sends[2].start()
            core_sends[3].start()
        return carry

    lax.fori_loop(0, 4, grads_step, 0)
    eob[...] = acc[...].astype(BF16)
    out_copy.start()
    for k in range(2):
        core_sends[2 + k].wait()
        load_o[k].start()

    for k in range(2):
        load_o[k].wait()
    add_to(win.at[s], win.at[s], win.at[shard_c])
    add_to(wout.at[s], wout.at[s], wout.at[shard_c])

    @pl.when(jnp.logical_not(ends))
    def _():
        pl.semaphore_signal(free_z, inc=1, device_id=end_peer, device_id_type=MESH)

    grad_copy.wait_recv()
    acc[...] = jnp.zeros_like(acc)
    gg_ref[...] = jnp.zeros_like(gg_ref)

    def take_back(r, own, returned):
        picked = pl.ds(pl.multiple_of(r * span, span), span)
        return dot_tn(route[0, :, picked], own) + dot_tn(route[1, :, picked], returned)

    def ffn_back(r, carry):
        rows = pl.ds(pl.multiple_of(r * span, span), span)
        grad = take_back(r, xgb[0:cap], gback[...])
        xhat, root = norm_parts(mid[r])
        gg_ref[0:1] += jnp.sum(grad * xhat, axis=0, keepdims=True)
        whole = cot_ref[rows].astype(F32) + norm_back(grad, gain_f, xhat, root)
        preg[r] = whole
        branch = whole.astype(BF16)
        att = oa[r]
        acc[...] += dot_nn(att.astype(BF16), branch)
        up = dot_nt(wo_ref[...], branch)
        up3 = up.reshape(H, HD, span)
        inner = jnp.sum(up3 * att.reshape(H, HD, span), axis=1, keepdims=True)
        for g in range(2):
            factor = facs[r, :, g:g + 1]
            dl[r, :, g:g + 1] = inner * factor
            flipped = (up3 * factor).reshape(width, span).astype(BF16)
            dot[g, r] = flipped
            do[g, r] = flipped.T
        oa[r] = jnp.zeros_like(oa[r])
        return carry

    chain(1, 0)
    lax.fori_loop(0, 2, ffn_back, 0)

    @pl.when(jnp.logical_not(ends))
    def _():
        pl.semaphore_signal(free_e, inc=1, device_id=end_peer, device_id_type=MESH)

    xs[...] = acc[...].astype(BF16)
    sums[0] = (xs, 0, dwo_hbm, 0)
    sums[1] = (xs, half, dwo_hbm, half)
    sum_step(0, 0)
    run([("s", 0, 1), ("c", 1, 1), ("s", 1, 0)])

    def attend_back(r, p, slot, g, parts, places):
        lanes = pair_lanes(p)
        q_two = apart(qs[r, :, lanes], first_half, 0)
        do_two = apart(do[g, r, :, lanes], first_half, 0)
        dot_two = apart(dot[g, r, lanes, :], first_rows, 1)
        inner = jnp.concatenate([dl[r, 2 * p, g:g + 1], dl[r, 2 * p + 1, g:g + 1]], axis=1)
        grad_q = [0.0, 0.0]
        for part, place in zip(parts, places):
            weights = ebuf[slot, place]
            k_flipped = ks[part, r, :, lanes].T
            grad_p = dot_nn(vs[part, r, :, lanes], dot_two)
            grad_s = (weights.astype(F32) * (grad_p - inner)).astype(BF16)
            place_rows = pl.ds(pl.multiple_of(r * span, span), span)
            hid[part, place_rows, lanes] = dot_nn(grad_s, q_two).astype(BF16)
            gp[part, place_rows, lanes] = dot_nn(weights, do_two).astype(BF16)
            for hh in range(2):
                columns = slice(hh * span, (hh + 1) * span)
                grad_q[hh] = grad_q[hh] + dot_nn(k_flipped[hh * HD:(hh + 1) * HD], grad_s[:, columns])
        for hh in range(2):
            oa[r, head_rows(p, hh), :] += grad_q[hh]

    def back_loop(g, parts, places, hf, extra):
        wide = len(parts) == 2

        def fetch(i):
            r, p, slot = i // 3, 3 * hf + lax.rem(i, 3), lax.rem(i, 2)
            return e_near(r, p, slot, False, wide) if g == 0 else e_far(r, p, slot, False)

        fetch(0).start()

        def step(i, carry):
            @pl.when(i < 5)
            def _():
                fetch(i + 1).start()
            fetch(i).wait()
            attend_back(i // 3, 3 * hf + lax.rem(i, 3), lax.rem(i, 2), g, parts, places)
            for at, steps in extra.items():
                @pl.when(jnp.logical_and(i == at, x == 1))
                def _():
                    run(steps)
            return carry

        lax.fori_loop(0, 6, step, 0)

    def gain_part(part, grad):
        gg_ref[1:2] += jnp.sum(grad * nb[part].reshape(local, width).astype(F32), axis=0, keepdims=True)

    def normed_grad(part):
        grad = dot_nt(hid[part, 0:local], wk_ref[...]) + dot_nt(gp[part, 0:local], wv_ref[...])
        gain_part(part, grad)
        return grad

    far_core = remote(cs.at[0:local], dnr0, dn_send.at[0], dn_recv.at[0], core_peer)
    def far_x(k):
        rows = slice(k * span // 2, (k + 1) * span // 2)
        return remote(cs.at[rows], dnr0.at[rows], far_send.at[k], far_recv.at[k], x_peer)

    def far_send_on(k):
        @pl.when(x == 1)
        def _():
            far_x(k).start()

    near_core = [
        remote(hid.at[r, local:local + span], nd_hbm.at[r], near_send.at[r], near_recv.at[r], core_peer) for r in range(2)]

    out_done = [
        pltpu.make_async_copy(cs.at[r * span:(r + 1) * span], out_hbm.at[r], local_sem.at[4 + r]) for r in range(2)]

    def out_add(r, carry):
        rows = pl.ds(pl.multiple_of(r * span, span), span)
        cs[rows] = (mid[r] + take_back(r, eob[0:cap], eback[...])).astype(BF16)
        return carry

    def near_both(hf, extra):
        @pl.when(c == 0)
        def _():
            back_loop(0, [s], [1], hf, extra)

        @pl.when(c == 1)
        def _():
            back_loop(0, [s - 1, s], [0, 1], hf, extra)

    def late(*lists):
        @pl.when(x == 0)
        def _():
            for extra in lists:
                for at in sorted(extra):
                    run(extra[at])

    def all_parts(grads, hf):
        columns = slice(hf * half, (hf + 1) * half)
        acc[:, 0:half] = jnp.zeros_like(acc[:, 0:half])

        def step(part, carry):
            acc[:, 0:half] += dot_tn(nb[part].reshape(local, width), grads[part, 0:local, columns])
            return carry

        @pl.when(x == 1)
        def _():
            lax.fori_loop(0, 2, step, 0)

        @pl.when(c == 1)
        def _():
            step(s - 1, 0)

        step(s, 0)
        return acc[:, 0:half].astype(BF16)

    def query_part(hf):
        columns = slice(hf * half, (hf + 1) * half)
        for r in range(2):
            qs[r, :, columns] = (oa[r, columns, :] * (HD ** -0.5)).astype(BF16).T
        return dot_tn(nb[s].reshape(local, width), qs[:, :, columns].reshape(local, half)).astype(BF16)

    @pl.when(x == 1)
    def _():
        back_loop(1, [0, 1], [0, 1], 0, FAR_ONE)
    grad_copy.wait_send()
    near_both(0, NEAR_ONE)
    late(FAR_ONE, NEAR_ONE)
    out_copy.wait()
    lax.fori_loop(0, 2, out_add, 0)
    for r in range(2):
        out_done[r].start()
    run(AFTER_ONE[0])
    xgb[:, 0:half] = all_parts(hid, 0)
    sums[2] = (xgb, 0, dwk_hbm, 0)
    run(AFTER_ONE[1])
    xgb[:, half:width] = all_parts(gp, 0)
    sums[3] = (xgb, half, dwv_hbm, 0)
    run(AFTER_ONE[2])
    eob[:, 0:half] = query_part(0)
    sums[4] = (eob, 0, dwq_hbm, 0)
    run(AFTER_ONE[3])
    for r in range(2):
        out_done[r].wait()

    @pl.when(x == 1)
    def _():
        back_loop(1, [0, 1], [0, 1], 1, FAR_TWO)
        cs[0:local] = normed_grad(1 - c).astype(BF16)
        far_core.start()
        mine_far = normed_grad(c)
        far_core.wait()
        cs[0:local] = (mine_far + dnr0[...].astype(F32)).astype(BF16)

    near_both(1, NEAR_TWO)
    late(FAR_TWO, NEAR_TWO)

    @pl.when(c == 1)
    def _():
        behind = normed_grad(s - 1).astype(BF16)
        for r in range(2):
            hid[r, local:local + span] = behind[r * span:(r + 1) * span]
            near_core[r].start()

    tokens_again = pltpu.make_async_copy(tokens_hbm, do.at[1], local_sem.at[0])
    tokens_again.start()
    run(AFTER_TWO[0])
    key_part = all_parts(hid, 1)
    eob[:, half:width] = key_part
    sums[5] = (eob, half, dwk_hbm, half)
    run(AFTER_TWO[1])
    values_part = all_parts(gp, 1)
    late_sums = gp.at[lax.rem(s + 1, 4)]
    late_sums[:, 0:half] = values_part
    sums[6] = (late_sums, 0, dwv_hbm, half)
    run(AFTER_TWO[2])
    late_sums[:, half:width] = query_part(1)
    sums[7] = (late_sums, half, dwq_hbm, half)
    run(AFTER_TWO[3])
    from_query = dot_nt(qs[...].reshape(local, width), wq_ref[...])
    gain_part(s, from_query)
    acc[0:local] = normed_grad(s) + from_query
    gg_ref[1:2] = gg_ref[1:2] / gain_a

    def gain_sum(first, mine, count, peers, sems):
        gsum[first + mine] = gg_ref[...]
        copies = [
            remote(gsum.at[first + mine], gsum.at[first + mine], gn_send.at[sems + k], gn_recv.at[sems + k], peer)
            for k, peer in enumerate(peers)]
        for one in copies:
            one.start()
        return copies

    def gain_total(first, count, copies):
        for one in copies:
            one.wait()
        total = gsum[first]
        for k in range(1, count):
            total = total + gsum[first + k]
        gg_ref[...] = total

    copies = gain_sum(0, c, 2, [core_peer], 0)
    run(TAIL[0])
    gain_total(0, 2, copies)
    copies = gain_sum(2, corner, 4, plane_peers, 1)
    run(TAIL[1])
    gain_total(2, 4, copies)
    copies = gain_sum(6, dp, 4, z_peers, 4)
    run(TAIL[2])
    @pl.when(c == 0)
    def _():
        for r in range(2):
            near_core[r].wait_recv()
        loaded = pltpu.make_async_copy(nd_hbm, do.at[0], local_sem.at[3])
        loaded.start()
        loaded.wait()
        acc[0:local] += do[0].reshape(local, width).astype(F32)

    @pl.when(x == 0)
    def _():
        for k in range(4):
            far_x(k).wait_recv()
        acc[0:local] += dnr0[...].astype(F32)

    tokens_again.wait()

    def first_back(r, carry):
        rows = pl.ds(pl.multiple_of(r * span, span), span)
        grad = acc[rows]
        xhat, root = norm_parts(do[1, r].astype(F32))
        mid[r] = preg[r] + norm_back(grad, gain_a, xhat, root)
        return carry

    lax.fori_loop(0, 2, first_back, 0)
    ig_done = pltpu.make_async_copy(mid, ig_hbm, local_sem.at[0])
    ig_done.start()

    run(TAIL[3])
    gain_total(6, 4, copies)
    gain_a_out[...] = gg_ref[1:2].reshape(width)
    gain_f_out[...] = gg_ref[0:1].reshape(width)
    for m in range(8):
        sum_step(m, 9)
    drain_chain()
    ig_done.wait()
    by_parity(lambda first, second, source: [wx_copy(j, first, source).wait_send() for j in range(4)] and None)

    @pl.when(x == 1)
    def _():
        for k in range(4):
            far_x(k).wait_send()

    @pl.when(x == 0)
    def _():
        for r in range(2):
            token_copy(r).wait_send()

    @pl.when(c == 1)
    def _():
        for r in range(2):
            near_core[r].wait_send()

    @pl.when(c == 0)
    def _():
        for r in range(2):
            core_copy(r).wait_send()


def block(tokens, cot, ids, table, lengths, gain_a, gain_f, wq, wk, wv, wo, w_in, w_out):
    rows, span, width = tokens.shape
    local = rows * span
    cap = 3 * local // 4
    vmem = pl.BlockSpec(memory_space=pltpu.VMEM)
    hbm = pl.BlockSpec(memory_space=pl.ANY)
    smem = pl.BlockSpec(memory_space=pltpu.SMEM)
    sem = pltpu.SemaphoreType.DMA
    signal = pltpu.SemaphoreType.REGULAR
    square = (width, width)
    blocks = (4, rows, span, width)
    flipped = (2, rows, width, span)
    shape = jax.ShapeDtypeStruct
    return pl.pallas_call(
        block_kernel,
        out_shape=(
            shape((rows, span, width), BF16),
            shape((rows, span, width), F32),
            shape(square, BF16), shape(square, BF16), shape(square, BF16), shape(square, BF16),
            shape(square, BF16), shape(square, BF16),
            shape((width,), F32), shape((width,), F32),
            shape((2, rows, 6, 2, span, 2 * span), BF16),
            shape((2,) + square, BF16), shape((2,) + square, BF16), shape((rows, span, width), BF16),
        ),
        in_specs=[hbm, vmem, vmem, vmem, smem, vmem, vmem, vmem, vmem, vmem, vmem, hbm, hbm],
        out_specs=(hbm,) * 8 + (vmem, vmem, hbm, hbm, hbm, hbm),
        scratch_shapes=[
            pltpu.VMEM(blocks, BF16),
            pltpu.VMEM(square, BF16),
            pltpu.VMEM(square, BF16),
            pltpu.VMEM((rows, span, width), BF16),
            pltpu.VMEM(blocks, BF16),
            pltpu.VMEM(blocks, BF16),
            pltpu.VMEM(flipped, BF16),
            pltpu.VMEM((2, 2, span, 2 * span), BF16),
            pltpu.VMEM((rows, width, span), F32),
            pltpu.VMEM((rows, H, 2, span), F32),
            pltpu.VMEM((rows, H, 2, span), F32),
            pltpu.VMEM((rows, H, 2, span), F32),
            pltpu.VMEM((2, cap, local), BF16),
            pltpu.VMEM((2 * cap, width), BF16),
            pltpu.VMEM((2 * cap, width), BF16),
            pltpu.VMEM((2, rows, span, width), BF16),
            pltpu.VMEM((rows, span, width), F32),
            pltpu.VMEM((4,) + square, BF16),
            pltpu.VMEM((4,) + square, BF16),
            pltpu.VMEM((2 * cap, width), F32),
            pltpu.VMEM((rows, span, width), F32),
            pltpu.VMEM((4, 2 * cap, width), BF16),
            pltpu.VMEM((4, 2 * cap, width), BF16),
            pltpu.VMEM((cap, width), BF16),
            pltpu.VMEM((cap, width), BF16),
            pltpu.VMEM((local, width), BF16),
            sem((6,)), sem((2,)), sem((2,)), sem((2,)), sem((2,)), sem((2,)), sem((2,)), sem((2,)),
            sem((4,)), sem((4,)), sem((4,)), sem((4,)), sem((8,)), sem((8,)), sem((2,)), sem((2,)),
            sem((4,)), sem((4,)), sem((3,)), sem((3,)), sem((4,)), sem((4,)),
            pltpu.VMEM((width // 2, width // 2), BF16),
            pltpu.VMEM((8, 3 * width // 8, width // 2), BF16),
            pltpu.VMEM((8, width), F32),
            pltpu.VMEM((10, 8, width), F32),
            sem((4,)), sem((4,)), sem((8,)), sem((8,)), sem((8,)), sem((8,)), sem((8,)), sem((8,)), sem((8,)), sem((8,)),
            sem((8,)), signal, signal, signal, signal, signal,
            sem((8,)), sem((8,)), sem((8, 4)), sem((8, 4)), sem((8, 3)), sem((8, 3)), sem((8,)), sem((8,)),
            sem((8,)), sem((7,)), sem((7,)), sem((2,)), sem((2,)),
        ],
        compiler_params=pltpu.CompilerParams(collective_id=1, has_side_effects=True, vmem_limit_bytes=62 << 20),
        name="block_step",
    )(tokens, cot, ids, table, lengths, gain_a, gain_f, wq, wk, wv, wo, w_in, w_out)


def finish_kernel(*refs):
    for source, target in zip(refs[:10], refs[10:]):
        target[...] = source[...].astype(target.dtype)


def finish(squares, output, input_grad, gains):
    width = squares[0].shape[0]
    steps = 8
    shape = jax.ShapeDtypeStruct
    output_rows = output.reshape(-1, width)
    grad_rows = input_grad.reshape(-1, width)
    arrays = list(squares) + [output_rows, grad_rows] + list(gains)
    specs = [pl.BlockSpec((one.shape[0] // steps, width), lambda i: (i, 0)) for one in arrays[:8]]
    specs += [pl.BlockSpec((width,), lambda i: (0,))] * 2
    kinds = [F32] * 6 + [BF16, F32, F32, F32]
    done = pl.pallas_call(
        finish_kernel,
        grid=(steps,),
        out_shape=[shape(one.shape, kind) for one, kind in zip(arrays, kinds)],
        in_specs=specs,
        out_specs=specs,
        compiler_params=pltpu.CompilerParams(vmem_limit_bytes=62 << 20),
        name="finish",
    )(*arrays)
    return done[:6], done[6].reshape(output.shape), done[7].reshape(input_grad.shape), done[8:]


def norm_rows(values, gain):
    average = jnp.mean(values, axis=-1, keepdims=True)
    centred = values - average
    spread = jnp.mean(centred * centred, axis=-1, keepdims=True)
    return centred * lax.rsqrt(spread + epsilon) * gain


def gelu_grad(pre, upstream):
    unused, pullback = jax.vjp(jax.nn.gelu, pre)
    return pullback(upstream)[0]


def split_heads(matrix):
    return matrix.reshape(matrix.shape[0], matrix.shape[1], H, HD).transpose(2, 0, 1, 3)


def join_heads(stacked):
    return stacked.transpose(1, 2, 0, 3).reshape(stacked.shape[1], stacked.shape[2], H * HD)


def per_device_plain(
    tokens,
    token_ids,
    hash_table,
    lengths,
    gain_attn,
    w_query,
    w_key,
    w_value,
    w_output,
    gain_ffn,
    w_in,
    w_out,
    cotangent,
):
    row_count, span, width = tokens.shape
    local_tok = row_count * span
    whole = span * lax.axis_size("seq")
    place = lax.axis_index("seq")
    scale = HD ** (-0.5)
    inputs = tokens.reshape(local_tok, width).astype(jnp.float32)
    key_positions = jnp.arange(whole, dtype=jnp.int32)
    query_positions = place * span + jnp.arange(span, dtype=jnp.int32)
    ends = jnp.cumsum(lengths, axis=1)
    key_document = jnp.sum(
        (key_positions[None, :, None] >= ends[:, None, :]).astype(jnp.int32), axis=2
    )
    query_document = jnp.sum(
        (query_positions[None, :, None] >= ends[:, None, :]).astype(jnp.int32), axis=2
    )
    visible = (key_positions[None, None, :] <= query_positions[None, :, None]) & (
        query_document[:, :, None] == key_document[:, None, :]
    )
    normed, first_norm_back = jax.vjp(norm_rows, inputs, gain_attn)
    normed_low = normed.astype(jnp.bfloat16)
    query = jnp.dot(normed_low, w_query, preferred_element_type=jnp.float32).astype(jnp.bfloat16)
    keys = jnp.dot(normed_low, w_key, preferred_element_type=jnp.float32).astype(jnp.bfloat16)
    values = jnp.dot(normed_low, w_value, preferred_element_type=jnp.float32).astype(jnp.bfloat16)
    own_pair = jnp.concatenate([keys, values], axis=1).reshape(row_count, span, 2 * width)
    all_pairs = lax.all_gather(own_pair, "seq", axis=1, tiled=True)

    def pair_heads(pairs):
        return (split_heads(pairs[:, :, :width]), split_heads(pairs[:, :, width:]))

    query_heads = split_heads(query.reshape(row_count, span, width))
    key_heads, value_heads = pair_heads(all_pairs)

    def head_forward(parts):
        query_one, key_one, value_one = parts
        scores = (
            jnp.einsum("rqd,rkd->rqk", query_one, key_one, preferred_element_type=jnp.float32)
            * scale
        )
        scores = jnp.where(visible, scores, masked_score)
        peak = jnp.max(scores, axis=2, keepdims=True)
        weights = jnp.exp(scores - peak)
        totals = jnp.sum(weights, axis=2, keepdims=True)
        probs = (weights / totals).astype(jnp.bfloat16)
        mixed = jnp.einsum("rqk,rkd->rqd", probs, value_one, preferred_element_type=jnp.float32)
        return (mixed, (peak + jnp.log(totals))[:, :, 0])

    mixed_heads, log_totals = lax.map(head_forward, (query_heads, key_heads, value_heads))
    attended = join_heads(mixed_heads).reshape(local_tok, width).astype(jnp.bfloat16)
    middle = inputs + jnp.dot(attended, w_output, preferred_element_type=jnp.float32)
    ffn_norm, second_norm_back = jax.vjp(norm_rows, middle, gain_ffn)
    ffn_in = ffn_norm.astype(jnp.bfloat16)
    experts = lax.axis_size("expert")
    capacity = min(2 * local_tok // experts, 3 * local_tok // 4)
    expert_of = jnp.take(hash_table, token_ids.reshape(local_tok), axis=0)
    labels = jnp.arange(experts, dtype=jnp.int32)
    onehot = (expert_of[:, None] == labels[None, :]).astype(jnp.int32)
    own_rank = jnp.sum((jnp.cumsum(onehot, axis=0) - 1) * onehot, axis=1)
    slots = expert_of * capacity + own_rank
    sources = (
        jnp.full((experts * capacity,), local_tok, jnp.int32)
        .at[slots]
        .set(jnp.arange(local_tok, dtype=jnp.int32))
    )

    def to_slots(rows_low):
        padded = jnp.concatenate([rows_low, jnp.zeros((1, width), rows_low.dtype)], axis=0)
        return jnp.take(padded, sources, axis=0).reshape(experts, capacity, width)

    received = lax.all_to_all(
        to_slots(ffn_in), "expert", split_axis=0, concat_axis=0, tiled=True
    ).reshape(-1, width)
    full_in, full_out = (
        lax.all_gather(w_in, "seq", axis=2, tiled=True),
        lax.all_gather(w_out, "seq", axis=1, tiled=True),
    )
    full_in = full_in[0]
    full_out = full_out[0]
    first = jnp.dot(received, full_in, preferred_element_type=jnp.float32)
    produced = jnp.dot(
        jax.nn.gelu(first).astype(jnp.bfloat16), full_out, preferred_element_type=jnp.float32
    ).astype(jnp.bfloat16)
    returned = lax.all_to_all(
        produced.reshape(experts, capacity, width),
        "expert",
        split_axis=0,
        concat_axis=0,
        tiled=True,
    ).reshape(-1, width)
    output = middle + jnp.take(returned, slots, axis=0).astype(jnp.float32)
    upstream = cotangent.reshape(local_tok, width)
    grad_received_out = lax.all_to_all(
        to_slots(upstream), "expert", split_axis=0, concat_axis=0, tiled=True
    ).reshape(-1, width)
    pre = jnp.dot(received, full_in, preferred_element_type=jnp.float32)
    hidden = jax.nn.gelu(pre).astype(jnp.bfloat16)
    grad_full_out = jnp.einsum(
        "rf,rd->fd", hidden, grad_received_out, preferred_element_type=jnp.float32
    )
    grad_hidden = jnp.einsum(
        "rd,fd->rf", grad_received_out, full_out, preferred_element_type=jnp.float32
    )
    grad_pre = gelu_grad(pre, grad_hidden).astype(jnp.bfloat16)
    grad_full_in = jnp.einsum("rd,rf->df", received, grad_pre, preferred_element_type=jnp.float32)
    grad_received = jnp.einsum(
        "rf,df->rd", grad_pre, full_in, preferred_element_type=jnp.float32
    ).astype(jnp.bfloat16)
    grad_in_part, grad_out_part = (
        lax.psum_scatter(
            grad_full_in[None].astype(jnp.bfloat16), "seq", scatter_dimension=2, tiled=True
        ).astype(jnp.float32),
        lax.psum_scatter(
            grad_full_out[None].astype(jnp.bfloat16), "seq", scatter_dimension=1, tiled=True
        ).astype(jnp.float32),
    )
    grad_in, grad_out = (
        lax.psum(grad_in_part.astype(jnp.bfloat16), "dp").astype(jnp.float32),
        lax.psum(grad_out_part.astype(jnp.bfloat16), "dp").astype(jnp.float32),
    )
    grad_back = lax.all_to_all(
        grad_received.reshape(experts, capacity, width),
        "expert",
        split_axis=0,
        concat_axis=0,
        tiled=True,
    ).reshape(-1, width)
    grad_ffn_in = jnp.take(grad_back, slots, axis=0).astype(jnp.float32)
    grad_middle_norm, grad_gain_ffn = second_norm_back(grad_ffn_in)
    grad_middle = upstream.astype(jnp.float32) + grad_middle_norm
    grad_branch = grad_middle.astype(jnp.bfloat16)
    grad_w_output = jnp.einsum(
        "cd,ce->de", attended, grad_branch, preferred_element_type=jnp.float32
    )
    grad_attended = jnp.einsum(
        "ce,de->cd", grad_branch, w_output, preferred_element_type=jnp.float32
    ).astype(jnp.bfloat16)
    again_pairs = lax.all_gather(own_pair, "seq", axis=1, tiled=True)
    key_back, value_back = pair_heads(again_pairs)

    def head_backward(parts):
        query_one, key_one, value_one, grad_one, log_one = parts
        scores = (
            jnp.einsum("rqd,rkd->rqk", query_one, key_one, preferred_element_type=jnp.float32)
            * scale
        )
        scores = jnp.where(visible, scores, masked_score)
        probs_full = jnp.exp(scores - log_one[:, :, None])
        probs = probs_full.astype(jnp.bfloat16)
        grad_probs = jnp.einsum(
            "rqd,rkd->rqk", grad_one, value_one, preferred_element_type=jnp.float32
        )
        inner = jnp.sum(probs_full * grad_probs, axis=2, keepdims=True)
        grad_scores = (probs_full * (grad_probs - inner)).astype(jnp.bfloat16)
        grad_query_one = (
            jnp.einsum("rqk,rkd->rqd", grad_scores, key_one, preferred_element_type=jnp.float32)
            * scale
        )
        grad_key_one = (
            jnp.einsum("rqk,rqd->rkd", grad_scores, query_one, preferred_element_type=jnp.float32)
            * scale
        )
        grad_value_one = jnp.einsum(
            "rqk,rqd->rkd", probs, grad_one, preferred_element_type=jnp.float32
        )
        return (grad_query_one, grad_key_one, grad_value_one)

    grad_att_heads = split_heads(grad_attended.reshape(row_count, span, width))
    grad_query_heads, grad_key_heads, grad_value_heads = lax.map(
        head_backward, (query_heads, key_back, value_back, grad_att_heads, log_totals)
    )
    grad_query_rows = join_heads(grad_query_heads).reshape(local_tok, width).astype(jnp.bfloat16)
    pair_grads = jnp.concatenate([join_heads(grad_key_heads), join_heads(grad_value_heads)], axis=2)
    own_grads = (
        lax.psum_scatter(pair_grads, "seq", scatter_dimension=1, tiled=True)
        .reshape(local_tok, 2 * width)
        .astype(jnp.bfloat16)
    )
    grad_key_rows = own_grads[:, :width]
    grad_value_rows = own_grads[:, width:]
    grad_w_query = jnp.einsum(
        "cd,ce->de", normed_low, grad_query_rows, preferred_element_type=jnp.float32
    )
    grad_w_key = jnp.einsum(
        "cd,ce->de", normed_low, grad_key_rows, preferred_element_type=jnp.float32
    )
    grad_w_value = jnp.einsum(
        "cd,ce->de", normed_low, grad_value_rows, preferred_element_type=jnp.float32
    )
    grad_normed = jnp.einsum(
        "ce,de->cd", grad_query_rows, w_query, preferred_element_type=jnp.float32
    )
    grad_normed = grad_normed + jnp.einsum(
        "ce,de->cd", grad_key_rows, w_key, preferred_element_type=jnp.float32
    )
    grad_normed = grad_normed + jnp.einsum(
        "ce,de->cd", grad_value_rows, w_value, preferred_element_type=jnp.float32
    )
    grad_inputs_norm, grad_gain_attn = first_norm_back(grad_normed)
    input_grad = grad_middle + grad_inputs_norm
    summed = lax.psum(
        (grad_gain_attn, grad_w_query, grad_w_key, grad_w_value, grad_w_output, grad_gain_ffn),
        ("dp", "seq", "expert"),
    )
    shaped_output = output.astype(jnp.bfloat16).reshape(row_count, span, width)
    shaped_grad = input_grad.reshape(row_count, span, width)
    return (
        shaped_output,
        shaped_grad,
        summed[0],
        summed[1],
        summed[2],
        summed[3],
        summed[4],
        summed[5],
        grad_in,
        grad_out,
    )


def per_device(
    tokens,
    token_ids,
    hash_table,
    lengths,
    gain_attn,
    w_query,
    w_key,
    w_value,
    w_output,
    gain_ffn,
    w_in,
    w_out,
    cotangent,
):
    row_count, span, width = tokens.shape
    local_tok = row_count * span
    output, input_grad, grad_q, grad_k, grad_v, grad_o, grad_in, grad_out, grad_gain_a, grad_gain_f = block(
        tokens, cotangent.reshape(local_tok, width), token_ids, hash_table.reshape(-1, 128), lengths,
        gain_attn, gain_ffn,
        w_query, w_key, w_value, w_output, w_in[0], w_out[0])[:10]
    squares, output, input_grad, gains = finish(
        (grad_q, grad_k, grad_v, grad_o, grad_in, grad_out), output, input_grad, (grad_gain_a, grad_gain_f))
    return (
        output,
        input_grad,
        gains[0],
        squares[0],
        squares[1],
        squares[2],
        squares[3],
        gains[1],
        squares[4][None],
        squares[5][None],
    )


def solution(mesh):
    sizes = (mesh.shape["dp"], mesh.shape["seq"], mesh.shape["expert"])
    return jax.shard_map(
        per_device if sizes == (4, 4, 2) else per_device_plain,
        mesh=mesh,
        in_specs=(
            P(("dp", "expert"), "seq", None),
            P(("dp", "expert"), "seq"),
            P(),
            P(("dp", "expert"), None),
            P(),
            P(),
            P(),
            P(),
            P(),
            P(),
            P("expert", None, "seq"),
            P("expert", "seq", None),
            P(("dp", "expert"), "seq", None),
        ),
        out_specs=(
            P(("dp", "expert"), "seq", None),
            P(("dp", "expert"), "seq", None),
            P(),
            P(),
            P(),
            P(),
            P(),
            P(),
            P("expert", None, "seq"),
            P("expert", "seq", None),
        ),
        check_vma=False,
    )
```

```python
import functools
import jax
import jax.numpy as jnp
from jax import lax
from jax.experimental import pallas as pl
from jax.experimental.pallas import tpu as pltpu
from jax.sharding import PartitionSpec as P

MESH = pl.DeviceIdType.MESH
F32 = jnp.float32
BF16 = jnp.bfloat16
I32 = jnp.int32
H = 12
HD = 64
epsilon = 1e-05
masked_score = -1e30
gelu_a = 0.7978845608028654
gelu_b = 0.044715


FAR_ONE = {2: [('s', 1, 1)], 4: [('c', 2, 0)], 5: [('c', 1, 2)]}
NEAR_ONE = {3: [('c', 2, 1)], 5: [('c', 1, 3)]}
AFTER_ONE = [[('s', 0, 2), ('s', 1, 2), ('c', 3, 0)], [('s', 2, 0), ('c', 2, 2)], [('s', 2, 1), ('s', 3, 0), ('c', 1, 4), ('c', 3, 1)], [('s', 3, 1), ('s', 4, 0)]]
FAR_TWO = {0: [('c', 2, 3), ('s', 4, 1)], 2: [('c', 1, 5), ('x', 6)], 3: [('s', 2, 2), ('c', 3, 2)], 5: [('s', 3, 2), ('x', 7), ('c', 2, 4)]}
NEAR_TWO = {0: [('s', 4, 2), ('f', 0), ('f', 1), ('f', 2), ('f', 3), ('c', 3, 3)], 2: [('s', 0, 3), ('s', 1, 3), ('s', 2, 3)], 3: [('c', 2, 5), ('s', 3, 3)], 5: [('c', 3, 4)]}
AFTER_TWO = [[('s', 4, 3), ('s', 0, 4), ('s', 1, 4)], [('s', 5, 0), ('s', 2, 4), ('s', 3, 4)], [('s', 5, 1), ('s', 6, 0), ('s', 4, 4), ('c', 3, 5), ('c', 1, 6)], [('s', 6, 1), ('s', 7, 0), ('s', 0, 5), ('s', 1, 5)]]
TAIL = [[('s', 7, 1), ('s', 5, 2), ('s', 2, 5), ('s', 3, 5)], [('s', 6, 2), ('s', 4, 5), ('s', 5, 3), ('c', 2, 6), ('s', 0, 6), ('s', 1, 6), ('s', 7, 2)], [('s', 6, 3), ('s', 2, 6), ('s', 0, 7), ('s', 3, 6), ('s', 1, 7), ('s', 5, 4), ('s', 7, 3), ('f', 4), ('c', 1, 7), ('s', 4, 6), ('s', 6, 4), ('s', 2, 7), ('s', 3, 7), ('f', 5), ('s', 5, 5), ('s', 7, 4), ('s', 6, 5), ('s', 4, 7), ('f', 6), ('s', 0, 8), ('s', 5, 6), ('s', 7, 5), ('s', 1, 8), ('s', 6, 6), ('c', 2, 7), ('c', 3, 6), ('s', 5, 7), ('s', 7, 6), ('f', 7), ('s', 6, 7), ('s', 2, 8), ('s', 3, 8), ('s', 7, 7), ('c', 3, 7), ('s', 4, 8)], [('s', 5, 8), ('s', 6, 8), ('s', 7, 8)]]


def dot_nn(a, b):
    return jnp.dot(a, b, preferred_element_type=F32)


def dot_nt(a, b):
    return lax.dot_general(a, b, (((1,), (1,)), ((), ())), preferred_element_type=F32)


def dot_tn(a, b):
    return lax.dot_general(a, b, (((0,), (0,)), ((), ())), preferred_element_type=F32)


def norm_parts(values):
    average = jnp.mean(values, axis=-1, keepdims=True)
    centred = values - average
    spread = jnp.mean(centred * centred, axis=-1, keepdims=True)
    root = lax.rsqrt(spread + epsilon)
    return centred * root, root


def norm_back(upstream, gain, xhat, root):
    scaled = upstream * gain
    first = jnp.mean(scaled, axis=-1, keepdims=True)
    second = jnp.mean(scaled * xhat, axis=-1, keepdims=True)
    return root * (scaled - first - xhat * second)


def block_kernel(
    tokens_hbm, cot_ref, ids_ref, table_ref, lengths_ref, gain_a_ref, gain_f_ref,
    wq_ref, wk_ref, wv_ref, wo_ref, win_hbm, wout_hbm,
    out_hbm, ig_hbm, dwq_hbm, dwk_hbm, dwv_hbm, dwo_hbm, dwin_hbm, dwout_hbm, gain_a_out, gain_f_out, es_hbm, ra_hbm, ro_hbm, nd_hbm,
    nb, xgb, eob, qs, ks, vs, dot, ebuf, oa, stat, facs, dl, route, cs, xs, do, mid,
    win, wout, acc, preg, hid, gp, gback, eback, dnr0,
    local_sem, e_sem, tok_send, tok_recv, fwd_send, fwd_recv, core_send, core_recv,
    wx_send, wx_recv, wz_send, wz_recv, wf_send, wf_recv, wc_send, wc_recv, y_send, y_recv, dn_send, dn_recv, far_send, far_recv,
    recv_d, recv_p, gg_ref, gsum, ed_send, ed_recv, ex_send, ex_recv, ee_send, ee_recv, em_send, em_recv,
    eb_send, eb_recv, eo_sem, free_x, free_z, free_m, free_d, free_e,
    rd_send, rd_recv, rp_send, rp_recv, rz_send, rz_recv, gd_send, gd_recv,
    own_sem, gn_send, gn_recv, near_send, near_recv,
):
    dp = lax.axis_index("dp")
    s = lax.axis_index("seq")
    y = lax.axis_index("expert")
    c = lax.rem(s, 2)
    x = s // 2
    core_peer = (dp, x * 2 + 1 - c, y)
    x_peer = (dp, (1 - x) * 2 + c, y)
    y_peer = (dp, s, 1 - y)
    span = tokens_hbm.shape[1]
    width = tokens_hbm.shape[2]
    local = 2 * span
    cap = gback.shape[0]
    stage = eob.at[0:cap]

    def remote(src, dst, send, recv, peer):
        return pltpu.make_async_remote_copy(
            src_ref=src, dst_ref=dst, send_sem=send, recv_sem=recv, device_id=peer, device_id_type=MESH)

    own_copy = pltpu.make_async_copy(tokens_hbm, nb.at[s], local_sem.at[0])
    win_copy = pltpu.make_async_copy(win_hbm, win.at[s], local_sem.at[1])
    wout_copy = pltpu.make_async_copy(wout_hbm, wout.at[s], local_sem.at[2])
    own_copy.start()
    win_copy.start()
    wout_copy.start()
    barrier = pltpu.get_barrier_semaphore()
    plane_peers = [x_peer, y_peer, (dp, (1 - x) * 2 + c, 1 - y)]
    z_peers = [(lax.rem(dp + d, 4), s, y) for d in range(1, 4)]
    for peer in [core_peer] + plane_peers + z_peers:
        pl.semaphore_signal(barrier, inc=1, device_id=peer, device_id_type=MESH)
    pl.semaphore_wait(barrier, 7)

    far_s = (1 - x) * 2 + c

    def token_copy(r):
        return remote(tokens_hbm.at[r], nb.at[s, r], tok_send.at[r], tok_recv.at[r], x_peer)

    def core_copy(r):
        return remote(tokens_hbm.at[r], nb.at[s, r], core_send.at[r], core_recv.at[r], core_peer)

    def forward_copy(r):
        return remote(nb.at[c, r], nb.at[c, r], fwd_send.at[r], fwd_recv.at[r], core_peer)

    wc_copies = [
        remote(win_hbm, win.at[s], wc_send.at[0], wc_recv.at[0], core_peer),
        remote(wout_hbm, wout.at[s], wc_send.at[1], wc_recv.at[1], core_peer),
    ]
    chunk = width // 4
    even = lax.rem(dp, 2) == 0
    swap_peer = (dp + 1 - 2 * lax.rem(dp, 2), s, y)

    def by_parity(action):
        @pl.when(even)
        def _():
            action(win, wout, win_hbm)

        @pl.when(jnp.logical_not(even))
        def _():
            action(wout, win, wout_hbm)

    def rows_of(j):
        return slice(j * chunk, (j + 1) * chunk)

    def wx_copy(j, matrix, source):
        return remote(source.at[rows_of(j)], matrix.at[s, rows_of(j)], wx_send.at[j], wx_recv.at[j], x_peer)

    def wz_copy(j, matrix):
        return remote(matrix.at[far_s, rows_of(j)], matrix.at[far_s, rows_of(j)], wz_send.at[j], wz_recv.at[j], swap_peer)

    def wf_copy(k, j, matrix):
        return remote(matrix.at[far_s, rows_of(j)], matrix.at[far_s, rows_of(j)],
                      wf_send.at[4 * k + j], wf_recv.at[4 * k + j], core_peer)

    def from_x(j):
        def action(first, second, source):
            wx_copy(j, first, source).wait_recv()
            wz_copy(j, first).start()
            wf_copy(0, j, first).start()
        by_parity(action)

    def from_z(j):
        def action(first, second, source):
            wz_copy(j, second).wait_recv()
            wf_copy(1, j, second).start()
        by_parity(action)

    @pl.when(x == 0)
    def _():
        for r in range(2):
            token_copy(r).start()

    by_parity(lambda first, second, source: [wx_copy(j, first, source).start() for j in range(4)] and None)

    @pl.when(c == 0)
    def _():
        for r in range(2):
            core_copy(r).start()

    wc_copies[0].start()
    wc_copies[1].start()

    ids = jnp.concatenate([ids_ref[0:1, :], ids_ref[1:2, :]], axis=1)
    high = ids // 128
    low = ids - high * 128
    pick = jnp.where(lax.broadcasted_iota(I32, (64, local), 0) == high, 1.0, 0.0).astype(BF16)
    looked = dot_tn(table_ref[...].astype(F32).astype(BF16), pick)
    expert_row = jnp.sum(
        jnp.where(lax.broadcasted_iota(I32, (128, local), 0) == low, looked, 0.0), axis=0, keepdims=True)
    mine = jnp.where(expert_row == y.astype(F32), 1.0, 0.0)
    sixteen = lax.broadcasted_iota(I32, (16, local), 0)
    both = jnp.where(sixteen == 0, mine, jnp.where(sixteen == 1, 1.0 - mine, 0.0)).astype(BF16)
    before = jnp.where(
        lax.broadcasted_iota(I32, (local, local), 0) < lax.broadcasted_iota(I32, (local, local), 1), 1.0, 0.0
    ).astype(BF16)
    ranks = dot_nn(both, before)
    slot_rows = lax.broadcasted_iota(I32, (cap, local), 0).astype(F32)
    for u in range(2):
        chosen = mine if u == 0 else 1.0 - mine
        route[u] = jnp.where(slot_rows == ranks[u:u + 1, :], chosen, 0.0).astype(BF16)

    cot_copy = remote(stage, cs.at[cap:], y_send.at[0], y_recv.at[0], y_peer)
    xs_copy = remote(stage, xs.at[cap:], y_send.at[1], y_recv.at[1], y_peer)
    stage[...] = dot_nn(route[1], cot_ref[...]).astype(BF16)
    cot_copy.start()
    cs[0:cap] = dot_nn(route[0], cot_ref[...]).astype(BF16)

    gain_a = gain_a_ref[...].reshape(1, width)
    gain_f = gain_f_ref[...].reshape(1, width)

    def normalise(part, r):
        nb[part, r] = (norm_parts(nb[part, r].astype(F32))[0] * gain_a).astype(BF16)

    def project(part, r):
        normed = nb[part, r]
        ks[part, r] = dot_nn(normed, wk_ref[...]).astype(BF16)
        vs[part, r] = dot_nn(normed, wv_ref[...]).astype(BF16)

    first_half = lax.broadcasted_iota(I32, (span, 128), 1) < HD
    first_rows = lax.broadcasted_iota(I32, (128, span), 0) < HD

    def apart(values, keep, axis):
        none = jnp.zeros_like(values)
        return jnp.concatenate([jnp.where(keep, values, none), jnp.where(keep, none, values)], axis=axis)

    def pair_lanes(p):
        return pl.ds(pl.multiple_of(p * 128, 128), 128)

    def head_rows(p, hh):
        return pl.ds(pl.multiple_of(p * 128 + hh * HD, HD), HD)

    def e_near(r, p, slot, write, both_parts):
        here = ebuf.at[slot] if both_parts else ebuf.at[slot, 1]
        there = es_hbm.at[0, r, p] if both_parts else es_hbm.at[0, r, p, 1]
        return pltpu.make_async_copy(here if write else there, there if write else here, e_sem.at[slot])

    def e_far(r, p, slot, write):
        here = ebuf.at[slot]
        there = es_hbm.at[1, r, p]
        return pltpu.make_async_copy(here if write else there, there if write else here, e_sem.at[slot])

    def attend(r, p, slot, parts, places, diagonal):
        lanes = pair_lanes(p)
        q_two = apart(qs[r, :, lanes], first_half, 0)
        v_flipped = [vs[part, r, :, lanes].T for part in parts]
        scores = [dot_nt(ks[part, r, :, lanes], q_two) for part in parts]
        if diagonal:
            ki = lax.broadcasted_iota(I32, (span, 2 * span), 0)
            qi = lax.broadcasted_iota(I32, (span, 2 * span), 1)
            qi = jnp.where(qi >= span, qi - span, qi)
            scores[-1] = jnp.where(ki <= qi, scores[-1], masked_score)
        peak = jnp.max(scores[0], axis=0, keepdims=True)
        for extra in scores[1:]:
            peak = jnp.maximum(peak, jnp.max(extra, axis=0, keepdims=True))
        weights = [jnp.exp(one - peak) for one in scores]
        total = jnp.sum(weights[0], axis=0, keepdims=True)
        for extra in weights[1:]:
            total = total + jnp.sum(extra, axis=0, keepdims=True)
        low_weights = [one.astype(BF16) for one in weights]
        for place, one in zip(places, low_weights):
            ebuf[slot, place] = one
        results = []
        for hh in range(2):
            columns = slice(hh * span, (hh + 1) * span)
            mixed = 0.0
            for v_one, one in zip(v_flipped, low_weights):
                mixed = mixed + dot_nn(v_one[hh * HD:(hh + 1) * HD], one[:, columns])
            results.append((2 * p + hh, head_rows(p, hh), peak[:, columns], total[:, columns], mixed))
        return results

    own_copy.wait()

    def own_rows(r, carry):
        mid[r] = nb[s, r].astype(F32)
        normalise(s, r)
        project(s, r)
        qs[r] = (dot_nn(nb[s, r], wq_ref[...]) * (HD ** -0.5)).astype(BF16)
        return carry

    lax.fori_loop(0, 2, own_rows, 0)

    def near_loop(parts, places):
        wide = len(parts) == 2

        def step(i, carry):
            r, p, slot = i // 6, lax.rem(i, 6), lax.rem(i, 2)

            @pl.when(i >= 2)
            def _():
                e_near(r, p, slot, True, wide).wait()

            for h, rows, peak, total, mixed in attend(r, p, slot, parts, places, True):
                stat[r, h, 0:1] = peak
                stat[r, h, 1:2] = total
                oa[r, rows, :] = mixed
            e_near(r, p, slot, True, wide).start()
            return carry

        lax.fori_loop(0, 12, step, 0)
        for slot in range(2):
            e_near(1, 4 + slot, slot, True, wide).wait()

    @pl.when(c == 0)
    def _():
        near_loop([s], [1])

    @pl.when(c == 1)
    def _():
        for r in range(2):
            core_copy(r).wait_recv()

        def partner_rows(r, carry):
            normalise(s - 1, r)
            project(s - 1, r)
            return carry

        lax.fori_loop(0, 2, partner_rows, 0)
        near_loop([s - 1, s], [0, 1])

    @pl.when(x == 0)
    def _():
        def step(i, carry):
            r, h = i // H, lax.rem(i, H)
            rows = pl.ds(pl.multiple_of(h * HD, HD), HD)
            inverse = 1.0 / stat[r, h, 1:2]
            facs[r, h, 0:1] = inverse
            facs[r, h, 1:2] = jnp.zeros_like(inverse)
            oa[r, rows, :] = oa[r, rows, :] * inverse
            return carry

        lax.fori_loop(0, 2 * H, step, 0)
        from_x(0)

    @pl.when(x == 1)
    def _():
        for r in range(2):
            token_copy(r).wait_recv()
            normalise(c, r)
            forward_copy(r).start()
            project(c, r)
            forward_copy(r).wait()
            project(1 - c, r)
            if r == 1:
                from_x(0)
            single = lengths_ref[r, 1] == 0

            def step(p, carry):
                slot = lax.rem(p, 2)

                @pl.when(p >= 2)
                def _():
                    e_far(r, p, slot, True).wait()

                for h, rows, peak, total, mixed in attend(r, p, slot, [0, 1], [0, 1], False):
                    near_peak = stat[r, h, 0:1]
                    peak = jnp.where(single, peak, near_peak)
                    top = jnp.maximum(peak, near_peak)
                    near_f = jnp.exp(near_peak - top)
                    far_f = jnp.where(single, jnp.exp(peak - top), 0.0)
                    whole = near_f * stat[r, h, 1:2] + far_f * total
                    near_f = near_f / whole
                    far_f = far_f / whole
                    facs[r, h, 0:1] = near_f
                    facs[r, h, 1:2] = far_f
                    oa[r, rows, :] = oa[r, rows, :] * near_f + mixed * far_f
                e_far(r, p, slot, True).start()
                return carry

            lax.fori_loop(0, 6, step, 0)
            for slot in range(2):
                e_far(r, 4 + slot, slot, True).wait()

    def out_rows(r, carry):
        att = oa[r].astype(BF16).T
        value = mid[r] + dot_nn(att, wo_ref[...])
        mid[r] = value
        do[0, r] = (norm_parts(value)[0] * gain_f).astype(BF16)
        return carry

    lax.fori_loop(0, 2, out_rows, 0)
    from_x(1)

    ffn_in = do[0].reshape(local, width)
    cot_copy.wait_send()
    stage[...] = dot_nn(route[1], ffn_in).astype(BF16)
    xs_copy.start()
    xs[0:cap] = dot_nn(route[0], ffn_in).astype(BF16)
    win_copy.wait()
    wout_copy.wait()
    acc[...] = jnp.zeros_like(acc)

    def expert_rows(u, f):
        rows = pl.ds(pl.multiple_of(u * cap, cap), cap)
        tokens_in = xs[rows]
        grads_in = cs[rows]
        for n in range(3):
            lanes = slice(n * 256, (n + 1) * 256)
            pre = dot_nn(tokens_in, win[f, :, lanes])
            up = dot_nt(grads_in, wout[f, lanes])
            square = pre * pre
            bent = jnp.tanh(gelu_a * pre * (1.0 + gelu_b * square))
            half = 0.5 * (1.0 + bent)
            slope = half + 0.5 * pre * (1.0 - bent * bent) * (gelu_a * (1.0 + 3.0 * gelu_b * square))
            hid[f, rows, lanes] = (pre * half).astype(BF16)
            gp[f, rows, lanes] = (up * slope).astype(BF16)
        acc[rows] += dot_nt(gp[f, rows], win[f])

    def expert_number(ix, ic):
        return 2 * lax.rem(x + ix, 2) + lax.rem(c + ic, 2)

    def moe_step(i, carry):
        ix = i // 4
        outer, inner = lax.rem(i // 2, 2), lax.rem(i, 2)

        @pl.when(i == 2)
        def _():
            xs_copy.wait_recv()
            cot_copy.wait_recv()

        @pl.when(i == 6)
        def _():
            by_parity(lambda first, second, source: [
                wf_copy(k, j, (first, second)[k]).wait_recv() for k in range(2) for j in range(4)] and None)

        @pl.when(i == 1)
        def _():
            wc_copies[0].wait_recv()
            wc_copies[1].wait_recv()
        expert_rows(jnp.where(ix == 0, outer, inner), expert_number(ix, jnp.where(ix == 0, inner, outer)))

        @pl.when(i == 0)
        def _():
            from_x(2)
            from_z(0)

        @pl.when(i == 1)
        def _():
            from_x(3)
            from_z(1)
            from_z(2)

        @pl.when(i == 3)
        def _():
            from_z(3)
        return carry

    lax.fori_loop(0, 8, moe_step, 0)

    grad_copy = remote(xgb.at[cap:], gback, y_send.at[2], y_recv.at[2], y_peer)
    out_copy = remote(eob.at[cap:], eback, y_send.at[3], y_recv.at[3], y_peer)
    xgb[...] = acc[...].astype(BF16)
    grad_copy.start()
    acc[...] = jnp.zeros_like(acc)
    wc_copies[0].wait_send()
    wc_copies[1].wait_send()
    by_parity(lambda first, second, source: [
        wf_copy(k, j, (first, second)[k]).wait_send() for k in range(2) for j in range(4)] and None)
    by_parity(lambda first, second, source: [wz_copy(j, first).wait_send() for j in range(4)] and None)
    xs_copy.wait_send()

    shard_a = expert_number(1, 0)
    shard_b = expert_number(1, 1)
    shard_c = expert_number(0, 1)
    ends = jnp.logical_or(dp == 0, dp == 3)
    end_z = jnp.where(dp < 2, 0, 3)
    near_mid = (jnp.where(dp < 2, 1, 2), s, y)
    other_mid = (3 - dp, s, y)
    end_peer = (end_z, s, y)
    core_sends = [
        remote(win.at[shard_b], ra_hbm.at[0], ed_send.at[0], ed_recv.at[0], core_peer),
        remote(wout.at[shard_b], ra_hbm.at[1], ed_send.at[1], ed_recv.at[1], core_peer),
        remote(win.at[shard_c], ro_hbm.at[0], ed_send.at[2], ed_recv.at[2], core_peer),
        remote(wout.at[shard_c], ro_hbm.at[1], ed_send.at[3], ed_recv.at[3], core_peer),
    ]

    def weight_grads(i):
        f = expert_number(1 - i // 2, lax.rem(i + 1, 2))
        win[f] = dot_tn(xs[...], gp[f]).astype(BF16)

        @pl.when(i == 0)
        def _():
            core_sends[0].start()

        @pl.when(i == 2)
        def _():
            core_sends[2].start()
        acc[...] += dot_nn(hid[f], wout[f])
        wout[f] = dot_tn(hid[f], cs[...]).astype(BF16)

    load_a = [
        pltpu.make_async_copy(ra_hbm.at[0], win.at[shard_b], local_sem.at[1]),
        pltpu.make_async_copy(ra_hbm.at[1], wout.at[shard_b], local_sem.at[2]),
    ]
    load_o = [
        pltpu.make_async_copy(ro_hbm.at[0], win.at[shard_c], local_sem.at[1]),
        pltpu.make_async_copy(ro_hbm.at[1], wout.at[shard_c], local_sem.at[2]),
    ]

    def piece(k):
        return pl.ds(pl.multiple_of(lax.rem(k, 4) * chunk, chunk), chunk)

    def add_to(target, first, second):
        target[...] = first[...] + second[...]

    def by_matrix(k, action):
        @pl.when(k < 4)
        def _():
            action(win, dwin_hbm)

        @pl.when(k >= 4)
        def _():
            action(wout, dwout_hbm)

    def x_grad(k, grads):
        return remote(grads.at[shard_a, piece(k)], grads.at[shard_c, piece(k)],
                      ex_send.at[k], ex_recv.at[k], x_peer)

    def end_grad(k, grads):
        return remote(grads.at[s, piece(k)], grads.at[shard_c, piece(k)], ee_send.at[k], ee_recv.at[k], near_mid)

    def mid_grad(k, grads):
        return remote(grads.at[s, piece(k)], grads.at[shard_a, piece(k)], em_send.at[k], em_recv.at[k], other_mid)

    def back_grad(k, grads, out):
        return remote(grads.at[shard_b, piece(k)], out.at[piece(k)], eb_send.at[k], eb_recv.at[k], end_peer)

    def out_grad(k, grads, out):
        return pltpu.make_async_copy(grads.at[shard_b, piece(k)], out.at[piece(k)], eo_sem.at[k])

    def send_x(k):
        pl.semaphore_wait(free_x, 1)
        by_matrix(k, lambda grads, out: x_grad(k, grads).start())

    def start_x():
        def step(k, carry):
            by_matrix(k, lambda grads, out: add_to(
                grads.at[shard_a, piece(k)], grads.at[shard_a, piece(k)], grads.at[shard_b, piece(k)]))
            pl.semaphore_signal(free_x, inc=1, device_id=x_peer, device_id_type=MESH)

            @pl.when(jnp.logical_and(k >= 1, k < 4))
            def _():
                send_x(k - 1)
            return carry

        lax.fori_loop(0, 8, step, 0)

    def chain(kind, number):
        k = jnp.int32(number)

        def action(grads, out):
            if kind == 1:
                x_grad(k, grads).wait()
                if number < 3:
                    send_x(k + 3)
                add_to(grads.at[s, piece(k)], grads.at[s, piece(k)], grads.at[shard_b, piece(k)])

                @pl.when(ends)
                def _():
                    if number == 0:
                        pl.semaphore_wait(free_z, 1)
                    end_grad(k, grads).start()

                @pl.when(jnp.logical_not(ends))
                def _():
                    pl.semaphore_signal(free_m, inc=1, device_id=other_mid, device_id_type=MESH)
            if kind == 2:
                @pl.when(jnp.logical_not(ends))
                def _():
                    end_grad(k, grads).wait_recv()
                    add_to(grads.at[s, piece(k)], grads.at[s, piece(k)], grads.at[shard_c, piece(k)])
                    pl.semaphore_wait(free_m, 1)
                    mid_grad(k, grads).start()
            if kind == 3:
                @pl.when(jnp.logical_not(ends))
                def _():
                    mid_grad(k, grads).wait_recv()
                    add_to(grads.at[shard_b, piece(k)], grads.at[s, piece(k)], grads.at[shard_a, piece(k)])
                    out_grad(k, grads, out).start()
                    back_grad(k, grads, out).start()

        action(*((win, dwin_hbm) if number < 4 else (wout, dwout_hbm)))

    def chain_all(steps):
        for kind, number in steps:
            chain(kind, number)

    def drain_chain():
        def step(k, carry):
            def action(grads, out):
                @pl.when(ends)
                def _():
                    end_grad(k, grads).wait_send()
                    back_grad(k, grads, out).wait_recv()

                @pl.when(jnp.logical_not(ends))
                def _():
                    mid_grad(k, grads).wait_send()
                    back_grad(k, grads, out).wait_send()
                    out_grad(k, grads, out).wait()
            by_matrix(k, action)
            return carry

        lax.fori_loop(0, 8, step, 0)

    half = width // 2
    tall = width // 2
    corner = 2 * x + y
    sums = [None] * 8

    def sum_step(m, step):
        source, at, out, to = sums[m]
        lanes = slice(at, at + half)
        goal = slice(to, to + half)
        (one, one_peer), (two, two_peer) = [(x, x_peer), (y, y_peer)] if m == 6 else [(y, y_peer), (x, x_peer)]
        low_one = c * tall + one * (tall // 2)
        low_two = low_one + two * (tall // 4)

        def rows(start, size):
            return pl.ds(pl.multiple_of(start, size), size)

        mine = rows(c * tall, tall)
        theirs = rows((1 - c) * tall, tall)
        kept_one = rows(low_one, tall // 2)
        sent_one = rows(c * tall + (1 - one) * (tall // 2), tall // 2)
        kept_two = rows(low_two, tall // 4)
        sent_two = rows(low_one + (1 - two) * (tall // 4), tall // 4)
        in_one = slice(0, tall // 2)
        in_two = slice(tall // 2, 3 * tall // 4)
        final = slice(0, tall // 4)
        slot = (slice((m // 2) * (tall // 4), (m // 2 + 1) * (tall // 4)), slice((m % 2) * half, (m % 2 + 1) * half))

        def core_send():
            return remote(source.at[theirs, lanes], recv_d, rd_send.at[m], rd_recv.at[m], core_peer)

        def one_part():
            return remote(source.at[sent_one, lanes], recv_p.at[m, in_one], rp_send.at[m, 0], rp_recv.at[m, 0], one_peer)

        def two_part():
            return remote(source.at[sent_two, lanes], recv_p.at[m, in_two], rp_send.at[m, 1], rp_recv.at[m, 1], two_peer)

        def end_part():
            return remote(source.at[kept_two, lanes], gback.at[slot], rp_send.at[m, 2], rp_recv.at[m, 2], near_mid)

        def mid_part():
            return remote(source.at[kept_two, lanes], eback.at[slot], rp_send.at[m, 3], rp_recv.at[m, 3], other_mid)

        def back_part():
            return remote(recv_p.at[m, final], out.at[kept_two, goal], rz_send.at[m, 0], rz_recv.at[m, 0], end_peer)

        def own_store():
            return pltpu.make_async_copy(recv_p.at[m, final], out.at[kept_two, goal], own_sem.at[m])

        def two_gather():
            return remote(out.at[kept_two, goal], out.at[kept_two, goal], rz_send.at[m, 1], rz_recv.at[m, 1], two_peer)

        def one_gather():
            return remote(out.at[kept_one, goal], out.at[kept_one, goal], rz_send.at[m, 2], rz_recv.at[m, 2], one_peer)

        def core_gather():
            return remote(out.at[mine, goal], out.at[mine, goal], gd_send.at[m], gd_recv.at[m], core_peer)

        if step == 0:
            if m > 0:
                pl.semaphore_wait(free_d, 1)
            core_send().start()
        if step == 1:
            core_send().wait()
            add_to(source.at[mine, lanes], source.at[mine, lanes], recv_d)
            if m < 7:
                pl.semaphore_signal(free_d, inc=1, device_id=core_peer, device_id_type=MESH)
            one_part().start()
        if step == 2:
            one_part().wait()
            add_to(source.at[kept_one, lanes], source.at[kept_one, lanes], recv_p.at[m, in_one])
            two_part().start()
        if step == 3:
            two_part().wait()
            add_to(source.at[kept_two, lanes], source.at[kept_two, lanes], recv_p.at[m, in_two])

            @pl.when(ends)
            def _():
                if m == 0:
                    pl.semaphore_wait(free_e, 1)
                end_part().start()
        if step == 4:
            @pl.when(jnp.logical_not(ends))
            def _():
                end_part().wait_recv()
                add_to(source.at[kept_two, lanes], source.at[kept_two, lanes], gback.at[slot])
                mid_part().start()
        if step == 5:
            @pl.when(jnp.logical_not(ends))
            def _():
                mid_part().wait_recv()
                add_to(recv_p.at[m, final], source.at[kept_two, lanes], eback.at[slot])
                own_store().start()
                back_part().start()
        if step == 6:
            @pl.when(ends)
            def _():
                end_part().wait_send()
                back_part().wait_recv()

            @pl.when(jnp.logical_not(ends))
            def _():
                mid_part().wait_send()
                own_store().wait()
                back_part().wait_send()
            two_gather().start()
        if step == 7:
            two_gather().wait()
            one_gather().start()
        if step == 8:
            one_gather().wait()
            core_gather().start()
        if step == 9:
            core_gather().wait()

    def run(steps):
        for one in steps:
            if one[0] == "c":
                chain(one[1], one[2])
            if one[0] == "s":
                sum_step(one[1], one[2])
            if one[0] == "x":
                send_x(jnp.int32(one[1]))
            if one[0] == "f":
                far_send_on(one[1])

    def grads_step(i, carry):
        weight_grads(i)

        @pl.when(i == 0)
        def _():
            core_sends[1].start()

        @pl.when(i == 1)
        def _():
            for k in range(2):
                core_sends[k].wait()
                load_a[k].start()
            for k in range(2):
                load_a[k].wait()
            start_x()

        @pl.when(i == 2)
        def _():
            core_sends[3].start()
        return carry

    lax.fori_loop(0, 4, grads_step, 0)
    eob[...] = acc[...].astype(BF16)
    out_copy.start()
    for k in range(2):
        core_sends[2 + k].wait()
        load_o[k].start()

    for k in range(2):
        load_o[k].wait()
    add_to(win.at[s], win.at[s], win.at[shard_c])
    add_to(wout.at[s], wout.at[s], wout.at[shard_c])

    @pl.when(jnp.logical_not(ends))
    def _():
        pl.semaphore_signal(free_z, inc=1, device_id=end_peer, device_id_type=MESH)

    grad_copy.wait_recv()
    acc[...] = jnp.zeros_like(acc)
    gg_ref[...] = jnp.zeros_like(gg_ref)

    def take_back(r, own, returned):
        picked = pl.ds(pl.multiple_of(r * span, span), span)
        return dot_tn(route[0, :, picked], own) + dot_tn(route[1, :, picked], returned)

    def ffn_back(r, carry):
        rows = pl.ds(pl.multiple_of(r * span, span), span)
        grad = take_back(r, xgb[0:cap], gback[...])
        xhat, root = norm_parts(mid[r])
        gg_ref[0:1] += jnp.sum(grad * xhat, axis=0, keepdims=True)
        whole = cot_ref[rows].astype(F32) + norm_back(grad, gain_f, xhat, root)
        preg[r] = whole
        branch = whole.astype(BF16)
        att = oa[r]
        acc[...] += dot_nn(att.astype(BF16), branch)
        up = dot_nt(wo_ref[...], branch)
        up3 = up.reshape(H, HD, span)
        inner = jnp.sum(up3 * att.reshape(H, HD, span), axis=1, keepdims=True)
        for g in range(2):
            factor = facs[r, :, g:g + 1]
            dl[r, :, g:g + 1] = inner * factor
            flipped = (up3 * factor).reshape(width, span).astype(BF16)
            dot[g, r] = flipped
            do[g, r] = flipped.T
        oa[r] = jnp.zeros_like(oa[r])
        return carry

    chain(1, 0)
    lax.fori_loop(0, 2, ffn_back, 0)

    @pl.when(jnp.logical_not(ends))
    def _():
        pl.semaphore_signal(free_e, inc=1, device_id=end_peer, device_id_type=MESH)

    xs[...] = acc[...].astype(BF16)
    sums[0] = (xs, 0, dwo_hbm, 0)
    sums[1] = (xs, half, dwo_hbm, half)
    sum_step(0, 0)
    run([("s", 0, 1), ("c", 1, 1), ("s", 1, 0)])

    def attend_back(r, p, slot, g, parts, places):
        lanes = pair_lanes(p)
        q_two = apart(qs[r, :, lanes], first_half, 0)
        do_two = apart(do[g, r, :, lanes], first_half, 0)
        dot_two = apart(dot[g, r, lanes, :], first_rows, 1)
        inner = jnp.concatenate([dl[r, 2 * p, g:g + 1], dl[r, 2 * p + 1, g:g + 1]], axis=1)
        grad_q = [0.0, 0.0]
        for part, place in zip(parts, places):
            weights = ebuf[slot, place]
            k_flipped = ks[part, r, :, lanes].T
            grad_p = dot_nn(vs[part, r, :, lanes], dot_two)
            grad_s = (weights.astype(F32) * (grad_p - inner)).astype(BF16)
            place_rows = pl.ds(pl.multiple_of(r * span, span), span)
            hid[part, place_rows, lanes] = dot_nn(grad_s, q_two).astype(BF16)
            gp[part, place_rows, lanes] = dot_nn(weights, do_two).astype(BF16)
            for hh in range(2):
                columns = slice(hh * span, (hh + 1) * span)
                grad_q[hh] = grad_q[hh] + dot_nn(k_flipped[hh * HD:(hh + 1) * HD], grad_s[:, columns])
        for hh in range(2):
            oa[r, head_rows(p, hh), :] += grad_q[hh]

    def back_loop(g, parts, places, hf, extra):
        wide = len(parts) == 2

        def fetch(i):
            r, p, slot = i // 3, 3 * hf + lax.rem(i, 3), lax.rem(i, 2)
            return e_near(r, p, slot, False, wide) if g == 0 else e_far(r, p, slot, False)

        fetch(0).start()

        def step(i, carry):
            @pl.when(i < 5)
            def _():
                fetch(i + 1).start()
            fetch(i).wait()
            attend_back(i // 3, 3 * hf + lax.rem(i, 3), lax.rem(i, 2), g, parts, places)
            for at, steps in extra.items():
                @pl.when(jnp.logical_and(i == at, x == 1))
                def _():
                    run(steps)
            return carry

        lax.fori_loop(0, 6, step, 0)

    def gain_part(part, grad):
        gg_ref[1:2] += jnp.sum(grad * nb[part].reshape(local, width).astype(F32), axis=0, keepdims=True)

    def normed_grad(part):
        grad = dot_nt(hid[part, 0:local], wk_ref[...]) + dot_nt(gp[part, 0:local], wv_ref[...])
        gain_part(part, grad)
        return grad

    far_core = remote(cs.at[0:local], dnr0, dn_send.at[0], dn_recv.at[0], core_peer)
    def far_x(k):
        rows = slice(k * span // 4, (k + 1) * span // 4)
        return remote(cs.at[rows], dnr0.at[rows], far_send.at[k], far_recv.at[k], x_peer)

    def far_send_on(k):
        @pl.when(x == 1)
        def _():
            far_x(k).start()

    near_core = [
        remote(hid.at[r, local:local + span], nd_hbm.at[r], near_send.at[r], near_recv.at[r], core_peer) for r in range(2)]

    out_done = [
        pltpu.make_async_copy(cs.at[r * span:(r + 1) * span], out_hbm.at[r], local_sem.at[4 + r]) for r in range(2)]

    def out_add(r, carry):
        rows = pl.ds(pl.multiple_of(r * span, span), span)
        cs[rows] = (mid[r] + take_back(r, eob[0:cap], eback[...])).astype(BF16)
        return carry

    def near_both(hf, extra):
        @pl.when(c == 0)
        def _():
            back_loop(0, [s], [1], hf, extra)

        @pl.when(c == 1)
        def _():
            back_loop(0, [s - 1, s], [0, 1], hf, extra)

    def late(*lists):
        @pl.when(x == 0)
        def _():
            for extra in lists:
                for at in sorted(extra):
                    run(extra[at])

    def all_parts(grads, hf):
        columns = slice(hf * half, (hf + 1) * half)
        acc[:, 0:half] = jnp.zeros_like(acc[:, 0:half])

        def step(part, carry):
            acc[:, 0:half] += dot_tn(nb[part].reshape(local, width), grads[part, 0:local, columns])
            return carry

        @pl.when(x == 1)
        def _():
            lax.fori_loop(0, 2, step, 0)

        @pl.when(c == 1)
        def _():
            step(s - 1, 0)

        step(s, 0)
        return acc[:, 0:half].astype(BF16)

    def query_part(hf):
        columns = slice(hf * half, (hf + 1) * half)
        for r in range(2):
            qs[r, :, columns] = (oa[r, columns, :] * (HD ** -0.5)).astype(BF16).T
        return dot_tn(nb[s].reshape(local, width), qs[:, :, columns].reshape(local, half)).astype(BF16)

    @pl.when(x == 1)
    def _():
        back_loop(1, [0, 1], [0, 1], 0, FAR_ONE)
    grad_copy.wait_send()
    near_both(0, NEAR_ONE)
    late(FAR_ONE, NEAR_ONE)
    out_copy.wait()
    lax.fori_loop(0, 2, out_add, 0)
    for r in range(2):
        out_done[r].start()
    run(AFTER_ONE[0])
    xgb[:, 0:half] = all_parts(hid, 0)
    sums[2] = (xgb, 0, dwk_hbm, 0)
    run(AFTER_ONE[1])
    xgb[:, half:width] = all_parts(gp, 0)
    sums[3] = (xgb, half, dwv_hbm, 0)
    run(AFTER_ONE[2])
    eob[:, 0:half] = query_part(0)
    sums[4] = (eob, 0, dwq_hbm, 0)
    run(AFTER_ONE[3])
    for r in range(2):
        out_done[r].wait()

    @pl.when(x == 1)
    def _():
        back_loop(1, [0, 1], [0, 1], 1, FAR_TWO)
        cs[0:local] = normed_grad(1 - c).astype(BF16)
        far_core.start()
        mine_far = normed_grad(c)
        far_core.wait()
        cs[0:local] = (mine_far + dnr0[...].astype(F32)).astype(BF16)

    near_both(1, NEAR_TWO)
    late(FAR_TWO, NEAR_TWO)

    @pl.when(c == 1)
    def _():
        behind = normed_grad(s - 1).astype(BF16)
        for r in range(2):
            hid[r, local:local + span] = behind[r * span:(r + 1) * span]
            near_core[r].start()

    tokens_again = pltpu.make_async_copy(tokens_hbm, do.at[1], local_sem.at[0])
    tokens_again.start()
    run(AFTER_TWO[0])
    key_part = all_parts(hid, 1)
    eob[:, half:width] = key_part
    sums[5] = (eob, half, dwk_hbm, half)
    run(AFTER_TWO[1])
    values_part = all_parts(gp, 1)
    late_sums = gp.at[lax.rem(s + 1, 4)]
    late_sums[:, 0:half] = values_part
    sums[6] = (late_sums, 0, dwv_hbm, half)
    run(AFTER_TWO[2])
    late_sums[:, half:width] = query_part(1)
    sums[7] = (late_sums, half, dwq_hbm, half)
    run(AFTER_TWO[3])
    from_query = dot_nt(qs[...].reshape(local, width), wq_ref[...])
    gain_part(s, from_query)
    acc[0:local] = normed_grad(s) + from_query
    gg_ref[1:2] = gg_ref[1:2] / gain_a

    def gain_sum(first, mine, count, peers, sems):
        gsum[first + mine] = gg_ref[...]
        copies = [
            remote(gsum.at[first + mine], gsum.at[first + mine], gn_send.at[sems + k], gn_recv.at[sems + k], peer)
            for k, peer in enumerate(peers)]
        for one in copies:
            one.start()
        return copies

    def gain_total(first, count, copies):
        for one in copies:
            one.wait()
        total = gsum[first]
        for k in range(1, count):
            total = total + gsum[first + k]
        gg_ref[...] = total

    copies = gain_sum(0, c, 2, [core_peer], 0)
    run(TAIL[0])
    gain_total(0, 2, copies)
    copies = gain_sum(2, corner, 4, plane_peers, 1)
    run(TAIL[1])
    gain_total(2, 4, copies)
    copies = gain_sum(6, dp, 4, z_peers, 4)
    run(TAIL[2])
    @pl.when(c == 0)
    def _():
        for r in range(2):
            near_core[r].wait_recv()
        loaded = pltpu.make_async_copy(nd_hbm, do.at[0], local_sem.at[3])
        loaded.start()
        loaded.wait()
        acc[0:local] += do[0].reshape(local, width).astype(F32)

    @pl.when(x == 0)
    def _():
        for k in range(8):
            far_x(k).wait_recv()
        acc[0:local] += dnr0[...].astype(F32)

    tokens_again.wait()

    def first_back(r, carry):
        rows = pl.ds(pl.multiple_of(r * span, span), span)
        grad = acc[rows]
        xhat, root = norm_parts(do[1, r].astype(F32))
        mid[r] = preg[r] + norm_back(grad, gain_a, xhat, root)
        return carry

    lax.fori_loop(0, 2, first_back, 0)
    ig_done = pltpu.make_async_copy(mid, ig_hbm, local_sem.at[0])
    ig_done.start()

    run(TAIL[3])
    gain_total(6, 4, copies)
    gain_a_out[...] = gg_ref[1:2].reshape(width)
    gain_f_out[...] = gg_ref[0:1].reshape(width)
    for m in range(8):
        sum_step(m, 9)
    drain_chain()
    ig_done.wait()
    by_parity(lambda first, second, source: [wx_copy(j, first, source).wait_send() for j in range(4)] and None)

    @pl.when(x == 1)
    def _():
        for k in range(8):
            far_x(k).wait_send()

    @pl.when(x == 0)
    def _():
        for r in range(2):
            token_copy(r).wait_send()

    @pl.when(c == 1)
    def _():
        for r in range(2):
            near_core[r].wait_send()

    @pl.when(c == 0)
    def _():
        for r in range(2):
            core_copy(r).wait_send()


def block(tokens, cot, ids, table, lengths, gain_a, gain_f, wq, wk, wv, wo, w_in, w_out):
    rows, span, width = tokens.shape
    local = rows * span
    cap = 3 * local // 4
    vmem = pl.BlockSpec(memory_space=pltpu.VMEM)
    hbm = pl.BlockSpec(memory_space=pl.ANY)
    smem = pl.BlockSpec(memory_space=pltpu.SMEM)
    sem = pltpu.SemaphoreType.DMA
    signal = pltpu.SemaphoreType.REGULAR
    square = (width, width)
    blocks = (4, rows, span, width)
    flipped = (2, rows, width, span)
    shape = jax.ShapeDtypeStruct
    return pl.pallas_call(
        block_kernel,
        out_shape=(
            shape((rows, span, width), BF16),
            shape((rows, span, width), F32),
            shape(square, BF16), shape(square, BF16), shape(square, BF16), shape(square, BF16),
            shape(square, BF16), shape(square, BF16),
            shape((width,), F32), shape((width,), F32),
            shape((2, rows, 6, 2, span, 2 * span), BF16),
            shape((2,) + square, BF16), shape((2,) + square, BF16), shape((rows, span, width), BF16),
        ),
        in_specs=[hbm, vmem, vmem, vmem, smem, vmem, vmem, vmem, vmem, vmem, vmem, hbm, hbm],
        out_specs=(hbm,) * 8 + (vmem, vmem, hbm, hbm, hbm, hbm),
        scratch_shapes=[
            pltpu.VMEM(blocks, BF16),
            pltpu.VMEM(square, BF16),
            pltpu.VMEM(square, BF16),
            pltpu.VMEM((rows, span, width), BF16),
            pltpu.VMEM(blocks, BF16),
            pltpu.VMEM(blocks, BF16),
            pltpu.VMEM(flipped, BF16),
            pltpu.VMEM((2, 2, span, 2 * span), BF16),
            pltpu.VMEM((rows, width, span), F32),
            pltpu.VMEM((rows, H, 2, span), F32),
            pltpu.VMEM((rows, H, 2, span), F32),
            pltpu.VMEM((rows, H, 2, span), F32),
            pltpu.VMEM((2, cap, local), BF16),
            pltpu.VMEM((2 * cap, width), BF16),
            pltpu.VMEM((2 * cap, width), BF16),
            pltpu.VMEM((2, rows, span, width), BF16),
            pltpu.VMEM((rows, span, width), F32),
            pltpu.VMEM((4,) + square, BF16),
            pltpu.VMEM((4,) + square, BF16),
            pltpu.VMEM((2 * cap, width), F32),
            pltpu.VMEM((rows, span, width), F32),
            pltpu.VMEM((4, 2 * cap, width), BF16),
            pltpu.VMEM((4, 2 * cap, width), BF16),
            pltpu.VMEM((cap, width), BF16),
            pltpu.VMEM((cap, width), BF16),
            pltpu.VMEM((local, width), BF16),
            sem((6,)), sem((2,)), sem((2,)), sem((2,)), sem((2,)), sem((2,)), sem((2,)), sem((2,)),
            sem((4,)), sem((4,)), sem((4,)), sem((4,)), sem((8,)), sem((8,)), sem((2,)), sem((2,)),
            sem((4,)), sem((4,)), sem((3,)), sem((3,)), sem((8,)), sem((8,)),
            pltpu.VMEM((width // 2, width // 2), BF16),
            pltpu.VMEM((8, 3 * width // 8, width // 2), BF16),
            pltpu.VMEM((8, width), F32),
            pltpu.VMEM((10, 8, width), F32),
            sem((4,)), sem((4,)), sem((8,)), sem((8,)), sem((8,)), sem((8,)), sem((8,)), sem((8,)), sem((8,)), sem((8,)),
            sem((8,)), signal, signal, signal, signal, signal,
            sem((8,)), sem((8,)), sem((8, 4)), sem((8, 4)), sem((8, 3)), sem((8, 3)), sem((8,)), sem((8,)),
            sem((8,)), sem((7,)), sem((7,)), sem((2,)), sem((2,)),
        ],
        compiler_params=pltpu.CompilerParams(collective_id=1, has_side_effects=True, vmem_limit_bytes=62 << 20),
        name="block_step",
    )(tokens, cot, ids, table, lengths, gain_a, gain_f, wq, wk, wv, wo, w_in, w_out)


def finish_kernel(*refs):
    sources, targets = refs[:10], refs[10:20]
    low, wide, kept_low, kept_wide, in_sem, out_sem = refs[20:]
    loads = [pltpu.make_async_copy(sources[k], low.at[k], in_sem.at[k]) for k in range(6)]
    kept = [kept_low, kept_wide]
    loads += [pltpu.make_async_copy(sources[6 + k], kept[k], in_sem.at[6 + k]) for k in range(2)]
    stores = [pltpu.make_async_copy(wide.at[k], targets[k], out_sem.at[k]) for k in range(6)]
    stores += [pltpu.make_async_copy(kept[k], targets[6 + k], out_sem.at[6 + k]) for k in range(2)]
    for one in loads:
        one.start()
    for k in range(8, 10):
        targets[k][...] = sources[k][...]
    for k in range(6):
        loads[k].wait()
        wide[k] = low[k].astype(F32)
        stores[k].start()
    for k in range(6, 8):
        loads[k].wait()
        stores[k].start()
    for one in stores:
        one.wait()


def finish(squares, output, input_grad, gains):
    width = squares[0].shape[0]
    shape = jax.ShapeDtypeStruct
    arrays = list(squares) + [output, input_grad] + list(gains)
    hbm = pl.BlockSpec(memory_space=pl.ANY)
    vmem = pl.BlockSpec(memory_space=pltpu.VMEM)
    kinds = [F32] * 6 + [BF16, F32, F32, F32]
    done = pl.pallas_call(
        finish_kernel,
        out_shape=[shape(one.shape, kind) for one, kind in zip(arrays, kinds)],
        in_specs=[hbm] * 8 + [vmem] * 2,
        out_specs=[hbm] * 8 + [vmem] * 2,
        scratch_shapes=[
            pltpu.VMEM((6, width, width), BF16),
            pltpu.VMEM((6, width, width), F32),
            pltpu.VMEM(output.shape, BF16),
            pltpu.VMEM(input_grad.shape, F32),
            pltpu.SemaphoreType.DMA((8,)),
            pltpu.SemaphoreType.DMA((8,)),
        ],
        compiler_params=pltpu.CompilerParams(vmem_limit_bytes=62 << 20),
        name="finish",
    )(*arrays)
    return done[:6], done[6], done[7], done[8:]


def norm_rows(values, gain):
    average = jnp.mean(values, axis=-1, keepdims=True)
    centred = values - average
    spread = jnp.mean(centred * centred, axis=-1, keepdims=True)
    return centred * lax.rsqrt(spread + epsilon) * gain


def gelu_grad(pre, upstream):
    unused, pullback = jax.vjp(jax.nn.gelu, pre)
    return pullback(upstream)[0]


def split_heads(matrix):
    return matrix.reshape(matrix.shape[0], matrix.shape[1], H, HD).transpose(2, 0, 1, 3)


def join_heads(stacked):
    return stacked.transpose(1, 2, 0, 3).reshape(stacked.shape[1], stacked.shape[2], H * HD)


def per_device_plain(
    tokens,
    token_ids,
    hash_table,
    lengths,
    gain_attn,
    w_query,
    w_key,
    w_value,
    w_output,
    gain_ffn,
    w_in,
    w_out,
    cotangent,
):
    row_count, span, width = tokens.shape
    local_tok = row_count * span
    whole = span * lax.axis_size("seq")
    place = lax.axis_index("seq")
    scale = HD ** (-0.5)
    inputs = tokens.reshape(local_tok, width).astype(jnp.float32)
    key_positions = jnp.arange(whole, dtype=jnp.int32)
    query_positions = place * span + jnp.arange(span, dtype=jnp.int32)
    ends = jnp.cumsum(lengths, axis=1)
    key_document = jnp.sum(
        (key_positions[None, :, None] >= ends[:, None, :]).astype(jnp.int32), axis=2
    )
    query_document = jnp.sum(
        (query_positions[None, :, None] >= ends[:, None, :]).astype(jnp.int32), axis=2
    )
    visible = (key_positions[None, None, :] <= query_positions[None, :, None]) & (
        query_document[:, :, None] == key_document[:, None, :]
    )
    normed, first_norm_back = jax.vjp(norm_rows, inputs, gain_attn)
    normed_low = normed.astype(jnp.bfloat16)
    query = jnp.dot(normed_low, w_query, preferred_element_type=jnp.float32).astype(jnp.bfloat16)
    keys = jnp.dot(normed_low, w_key, preferred_element_type=jnp.float32).astype(jnp.bfloat16)
    values = jnp.dot(normed_low, w_value, preferred_element_type=jnp.float32).astype(jnp.bfloat16)
    own_pair = jnp.concatenate([keys, values], axis=1).reshape(row_count, span, 2 * width)
    all_pairs = lax.all_gather(own_pair, "seq", axis=1, tiled=True)

    def pair_heads(pairs):
        return (split_heads(pairs[:, :, :width]), split_heads(pairs[:, :, width:]))

    query_heads = split_heads(query.reshape(row_count, span, width))
    key_heads, value_heads = pair_heads(all_pairs)

    def head_forward(parts):
        query_one, key_one, value_one = parts
        scores = (
            jnp.einsum("rqd,rkd->rqk", query_one, key_one, preferred_element_type=jnp.float32)
            * scale
        )
        scores = jnp.where(visible, scores, masked_score)
        peak = jnp.max(scores, axis=2, keepdims=True)
        weights = jnp.exp(scores - peak)
        totals = jnp.sum(weights, axis=2, keepdims=True)
        probs = (weights / totals).astype(jnp.bfloat16)
        mixed = jnp.einsum("rqk,rkd->rqd", probs, value_one, preferred_element_type=jnp.float32)
        return (mixed, (peak + jnp.log(totals))[:, :, 0])

    mixed_heads, log_totals = lax.map(head_forward, (query_heads, key_heads, value_heads))
    attended = join_heads(mixed_heads).reshape(local_tok, width).astype(jnp.bfloat16)
    middle = inputs + jnp.dot(attended, w_output, preferred_element_type=jnp.float32)
    ffn_norm, second_norm_back = jax.vjp(norm_rows, middle, gain_ffn)
    ffn_in = ffn_norm.astype(jnp.bfloat16)
    experts = lax.axis_size("expert")
    capacity = min(2 * local_tok // experts, 3 * local_tok // 4)
    expert_of = jnp.take(hash_table, token_ids.reshape(local_tok), axis=0)
    labels = jnp.arange(experts, dtype=jnp.int32)
    onehot = (expert_of[:, None] == labels[None, :]).astype(jnp.int32)
    own_rank = jnp.sum((jnp.cumsum(onehot, axis=0) - 1) * onehot, axis=1)
    slots = expert_of * capacity + own_rank
    sources = (
        jnp.full((experts * capacity,), local_tok, jnp.int32)
        .at[slots]
        .set(jnp.arange(local_tok, dtype=jnp.int32))
    )

    def to_slots(rows_low):
        padded = jnp.concatenate([rows_low, jnp.zeros((1, width), rows_low.dtype)], axis=0)
        return jnp.take(padded, sources, axis=0).reshape(experts, capacity, width)

    received = lax.all_to_all(
        to_slots(ffn_in), "expert", split_axis=0, concat_axis=0, tiled=True
    ).reshape(-1, width)
    full_in, full_out = (
        lax.all_gather(w_in, "seq", axis=2, tiled=True),
        lax.all_gather(w_out, "seq", axis=1, tiled=True),
    )
    full_in = full_in[0]
    full_out = full_out[0]
    first = jnp.dot(received, full_in, preferred_element_type=jnp.float32)
    produced = jnp.dot(
        jax.nn.gelu(first).astype(jnp.bfloat16), full_out, preferred_element_type=jnp.float32
    ).astype(jnp.bfloat16)
    returned = lax.all_to_all(
        produced.reshape(experts, capacity, width),
        "expert",
        split_axis=0,
        concat_axis=0,
        tiled=True,
    ).reshape(-1, width)
    output = middle + jnp.take(returned, slots, axis=0).astype(jnp.float32)
    upstream = cotangent.reshape(local_tok, width)
    grad_received_out = lax.all_to_all(
        to_slots(upstream), "expert", split_axis=0, concat_axis=0, tiled=True
    ).reshape(-1, width)
    pre = jnp.dot(received, full_in, preferred_element_type=jnp.float32)
    hidden = jax.nn.gelu(pre).astype(jnp.bfloat16)
    grad_full_out = jnp.einsum(
        "rf,rd->fd", hidden, grad_received_out, preferred_element_type=jnp.float32
    )
    grad_hidden = jnp.einsum(
        "rd,fd->rf", grad_received_out, full_out, preferred_element_type=jnp.float32
    )
    grad_pre = gelu_grad(pre, grad_hidden).astype(jnp.bfloat16)
    grad_full_in = jnp.einsum("rd,rf->df", received, grad_pre, preferred_element_type=jnp.float32)
    grad_received = jnp.einsum(
        "rf,df->rd", grad_pre, full_in, preferred_element_type=jnp.float32
    ).astype(jnp.bfloat16)
    grad_in_part, grad_out_part = (
        lax.psum_scatter(
            grad_full_in[None].astype(jnp.bfloat16), "seq", scatter_dimension=2, tiled=True
        ).astype(jnp.float32),
        lax.psum_scatter(
            grad_full_out[None].astype(jnp.bfloat16), "seq", scatter_dimension=1, tiled=True
        ).astype(jnp.float32),
    )
    grad_in, grad_out = (
        lax.psum(grad_in_part.astype(jnp.bfloat16), "dp").astype(jnp.float32),
        lax.psum(grad_out_part.astype(jnp.bfloat16), "dp").astype(jnp.float32),
    )
    grad_back = lax.all_to_all(
        grad_received.reshape(experts, capacity, width),
        "expert",
        split_axis=0,
        concat_axis=0,
        tiled=True,
    ).reshape(-1, width)
    grad_ffn_in = jnp.take(grad_back, slots, axis=0).astype(jnp.float32)
    grad_middle_norm, grad_gain_ffn = second_norm_back(grad_ffn_in)
    grad_middle = upstream.astype(jnp.float32) + grad_middle_norm
    grad_branch = grad_middle.astype(jnp.bfloat16)
    grad_w_output = jnp.einsum(
        "cd,ce->de", attended, grad_branch, preferred_element_type=jnp.float32
    )
    grad_attended = jnp.einsum(
        "ce,de->cd", grad_branch, w_output, preferred_element_type=jnp.float32
    ).astype(jnp.bfloat16)
    again_pairs = lax.all_gather(own_pair, "seq", axis=1, tiled=True)
    key_back, value_back = pair_heads(again_pairs)

    def head_backward(parts):
        query_one, key_one, value_one, grad_one, log_one = parts
        scores = (
            jnp.einsum("rqd,rkd->rqk", query_one, key_one, preferred_element_type=jnp.float32)
            * scale
        )
        scores = jnp.where(visible, scores, masked_score)
        probs_full = jnp.exp(scores - log_one[:, :, None])
        probs = probs_full.astype(jnp.bfloat16)
        grad_probs = jnp.einsum(
            "rqd,rkd->rqk", grad_one, value_one, preferred_element_type=jnp.float32
        )
        inner = jnp.sum(probs_full * grad_probs, axis=2, keepdims=True)
        grad_scores = (probs_full * (grad_probs - inner)).astype(jnp.bfloat16)
        grad_query_one = (
            jnp.einsum("rqk,rkd->rqd", grad_scores, key_one, preferred_element_type=jnp.float32)
            * scale
        )
        grad_key_one = (
            jnp.einsum("rqk,rqd->rkd", grad_scores, query_one, preferred_element_type=jnp.float32)
            * scale
        )
        grad_value_one = jnp.einsum(
            "rqk,rqd->rkd", probs, grad_one, preferred_element_type=jnp.float32
        )
        return (grad_query_one, grad_key_one, grad_value_one)

    grad_att_heads = split_heads(grad_attended.reshape(row_count, span, width))
    grad_query_heads, grad_key_heads, grad_value_heads = lax.map(
        head_backward, (query_heads, key_back, value_back, grad_att_heads, log_totals)
    )
    grad_query_rows = join_heads(grad_query_heads).reshape(local_tok, width).astype(jnp.bfloat16)
    pair_grads = jnp.concatenate([join_heads(grad_key_heads), join_heads(grad_value_heads)], axis=2)
    own_grads = (
        lax.psum_scatter(pair_grads, "seq", scatter_dimension=1, tiled=True)
        .reshape(local_tok, 2 * width)
        .astype(jnp.bfloat16)
    )
    grad_key_rows = own_grads[:, :width]
    grad_value_rows = own_grads[:, width:]
    grad_w_query = jnp.einsum(
        "cd,ce->de", normed_low, grad_query_rows, preferred_element_type=jnp.float32
    )
    grad_w_key = jnp.einsum(
        "cd,ce->de", normed_low, grad_key_rows, preferred_element_type=jnp.float32
    )
    grad_w_value = jnp.einsum(
        "cd,ce->de", normed_low, grad_value_rows, preferred_element_type=jnp.float32
    )
    grad_normed = jnp.einsum(
        "ce,de->cd", grad_query_rows, w_query, preferred_element_type=jnp.float32
    )
    grad_normed = grad_normed + jnp.einsum(
        "ce,de->cd", grad_key_rows, w_key, preferred_element_type=jnp.float32
    )
    grad_normed = grad_normed + jnp.einsum(
        "ce,de->cd", grad_value_rows, w_value, preferred_element_type=jnp.float32
    )
    grad_inputs_norm, grad_gain_attn = first_norm_back(grad_normed)
    input_grad = grad_middle + grad_inputs_norm
    summed = lax.psum(
        (grad_gain_attn, grad_w_query, grad_w_key, grad_w_value, grad_w_output, grad_gain_ffn),
        ("dp", "seq", "expert"),
    )
    shaped_output = output.astype(jnp.bfloat16).reshape(row_count, span, width)
    shaped_grad = input_grad.reshape(row_count, span, width)
    return (
        shaped_output,
        shaped_grad,
        summed[0],
        summed[1],
        summed[2],
        summed[3],
        summed[4],
        summed[5],
        grad_in,
        grad_out,
    )


def per_device(
    tokens,
    token_ids,
    hash_table,
    lengths,
    gain_attn,
    w_query,
    w_key,
    w_value,
    w_output,
    gain_ffn,
    w_in,
    w_out,
    cotangent,
):
    row_count, span, width = tokens.shape
    local_tok = row_count * span
    output, input_grad, grad_q, grad_k, grad_v, grad_o, grad_in, grad_out, grad_gain_a, grad_gain_f = block(
        tokens, cotangent.reshape(local_tok, width), token_ids, hash_table.reshape(-1, 128), lengths,
        gain_attn, gain_ffn,
        w_query, w_key, w_value, w_output, w_in[0], w_out[0])[:10]
    squares, output, input_grad, gains = finish(
        (grad_q, grad_k, grad_v, grad_o, grad_in, grad_out), output, input_grad, (grad_gain_a, grad_gain_f))
    return (
        output,
        input_grad,
        gains[0],
        squares[0],
        squares[1],
        squares[2],
        squares[3],
        gains[1],
        squares[4][None],
        squares[5][None],
    )


def solution(mesh):
    sizes = (mesh.shape["dp"], mesh.shape["seq"], mesh.shape["expert"])
    return jax.shard_map(
        per_device if sizes == (4, 4, 2) else per_device_plain,
        mesh=mesh,
        in_specs=(
            P(("dp", "expert"), "seq", None),
            P(("dp", "expert"), "seq"),
            P(),
            P(("dp", "expert"), None),
            P(),
            P(),
            P(),
            P(),
            P(),
            P(),
            P("expert", None, "seq"),
            P("expert", "seq", None),
            P(("dp", "expert"), "seq", None),
        ),
        out_specs=(
            P(("dp", "expert"), "seq", None),
            P(("dp", "expert"), "seq", None),
            P(),
            P(),
            P(),
            P(),
            P(),
            P(),
            P("expert", None, "seq"),
            P("expert", "seq", None),
        ),
        check_vma=False,
    )
```

```python
import functools
import jax
import jax.numpy as jnp
from jax import lax
from jax.experimental import pallas as pl
from jax.experimental.pallas import tpu as pltpu
from jax.sharding import PartitionSpec as P

MESH = pl.DeviceIdType.MESH
F32 = jnp.float32
BF16 = jnp.bfloat16
I32 = jnp.int32
H = 12
HD = 64
epsilon = 1e-05
masked_score = -1e30
gelu_a = 0.7978845608028654
gelu_b = 0.044715


FAR_ONE = {1: [('s', 0, 1), ('s', 1, 0)], 3: [('s', 1, 1)], 4: [('c', 2, 0)], 5: [('c', 1, 2)]}
NEAR_ONE = {3: [('c', 2, 1)], 5: [('c', 1, 3)]}
AFTER_ONE = [[('s', 0, 2), ('s', 1, 2), ('c', 3, 0)], [('s', 2, 0), ('c', 2, 2)], [('s', 2, 1), ('s', 3, 0), ('c', 1, 4), ('c', 3, 1)], [('s', 3, 1), ('s', 4, 0)]]
FAR_TWO = {0: [('c', 2, 3), ('s', 4, 1)], 2: [('c', 1, 5), ('x', 6)], 3: [('s', 2, 2), ('c', 3, 2)], 5: [('s', 3, 2), ('x', 7), ('c', 2, 4)]}
NEAR_TWO = {0: [('s', 4, 2), ('f', 0), ('f', 1), ('f', 2), ('f', 3), ('c', 3, 3)], 2: [('s', 0, 3), ('s', 1, 3), ('s', 2, 3)], 3: [('c', 2, 5), ('s', 3, 3)], 5: [('c', 3, 4)]}
AFTER_TWO = [[('s', 0, 4), ('s', 1, 4)], [('s', 5, 0), ('s', 2, 4), ('s', 3, 4)], [('s', 5, 1), ('s', 6, 0), ('s', 4, 3), ('c', 3, 5), ('c', 1, 6)], [('s', 6, 1), ('s', 7, 0), ('s', 0, 5), ('s', 1, 5)]]
TAIL = [[('s', 7, 1), ('s', 4, 4), ('s', 5, 2), ('s', 2, 5), ('s', 3, 5)], [('s', 6, 2), ('s', 4, 5), ('s', 5, 3), ('c', 2, 6), ('s', 0, 6), ('s', 1, 6), ('s', 7, 2)], [('s', 6, 3), ('s', 2, 6), ('s', 0, 7), ('s', 3, 6), ('s', 1, 7), ('s', 5, 4), ('s', 7, 3), ('f', 4), ('c', 1, 7), ('s', 4, 6), ('s', 6, 4), ('s', 2, 7), ('s', 3, 7), ('f', 5), ('s', 5, 5), ('s', 7, 4), ('s', 6, 5), ('s', 4, 7), ('f', 6), ('s', 0, 8), ('s', 5, 6), ('s', 7, 5), ('s', 1, 8), ('s', 6, 6), ('c', 2, 7), ('c', 3, 6), ('s', 5, 7), ('s', 7, 6), ('f', 7), ('s', 6, 7), ('s', 2, 8), ('s', 3, 8), ('s', 7, 7), ('c', 3, 7), ('s', 4, 8)], [('s', 5, 8), ('s', 6, 8), ('s', 7, 8)]]


def dot_nn(a, b):
    return jnp.dot(a, b, preferred_element_type=F32)


def dot_nt(a, b):
    return lax.dot_general(a, b, (((1,), (1,)), ((), ())), preferred_element_type=F32)


def dot_tn(a, b):
    return lax.dot_general(a, b, (((0,), (0,)), ((), ())), preferred_element_type=F32)


def norm_parts(values):
    average = jnp.mean(values, axis=-1, keepdims=True)
    centred = values - average
    spread = jnp.mean(centred * centred, axis=-1, keepdims=True)
    root = lax.rsqrt(spread + epsilon)
    return centred * root, root


def norm_back(upstream, gain, xhat, root):
    scaled = upstream * gain
    first = jnp.mean(scaled, axis=-1, keepdims=True)
    second = jnp.mean(scaled * xhat, axis=-1, keepdims=True)
    return root * (scaled - first - xhat * second)


def block_kernel(
    tokens_hbm, cot_ref, ids_ref, table_ref, lengths_ref, gain_a_ref, gain_f_ref,
    wq_ref, wk_ref, wv_ref, wo_ref, win_hbm, wout_hbm,
    out_hbm, ig_hbm, dwq_hbm, dwk_hbm, dwv_hbm, dwo_hbm, dwin_hbm, dwout_hbm, gain_a_out, gain_f_out, es_hbm, ra_hbm, ro_hbm, nd_hbm,
    nb, xgb, eob, qs, ks, vs, dot, ebuf, oa, stat, facs, dl, route, cs, xs, do, mid,
    win, wout, acc, preg, hid, gp, gback, eback, dnr0,
    local_sem, e_sem, tok_send, tok_recv, fwd_send, fwd_recv, core_send, core_recv,
    wx_send, wx_recv, wz_send, wz_recv, wf_send, wf_recv, wc_send, wc_recv, y_send, y_recv, dn_send, dn_recv, far_send, far_recv,
    recv_d, recv_p, gg_ref, gsum, ed_send, ed_recv, ex_send, ex_recv, ee_send, ee_recv, em_send, em_recv,
    eb_send, eb_recv, eo_sem, free_x, free_z, free_m, free_d, free_e,
    rd_send, rd_recv, rp_send, rp_recv, rz_send, rz_recv, gd_send, gd_recv,
    own_sem, gn_send, gn_recv, near_send, near_recv,
):
    dp = lax.axis_index("dp")
    s = lax.axis_index("seq")
    y = lax.axis_index("expert")
    c = lax.rem(s, 2)
    x = s // 2
    core_peer = (dp, x * 2 + 1 - c, y)
    x_peer = (dp, (1 - x) * 2 + c, y)
    y_peer = (dp, s, 1 - y)
    span = tokens_hbm.shape[1]
    width = tokens_hbm.shape[2]
    local = 2 * span
    cap = gback.shape[0]
    stage = eob.at[0:cap]

    def remote(src, dst, send, recv, peer):
        return pltpu.make_async_remote_copy(
            src_ref=src, dst_ref=dst, send_sem=send, recv_sem=recv, device_id=peer, device_id_type=MESH)

    own_copy = pltpu.make_async_copy(tokens_hbm, nb.at[s], local_sem.at[0])
    win_copy = pltpu.make_async_copy(win_hbm, win.at[s], local_sem.at[1])
    wout_copy = pltpu.make_async_copy(wout_hbm, wout.at[s], local_sem.at[2])
    own_copy.start()
    win_copy.start()
    wout_copy.start()
    barrier = pltpu.get_barrier_semaphore()
    plane_peers = [x_peer, y_peer, (dp, (1 - x) * 2 + c, 1 - y)]
    z_peers = [(lax.rem(dp + d, 4), s, y) for d in range(1, 4)]
    for peer in [core_peer] + plane_peers + z_peers:
        pl.semaphore_signal(barrier, inc=1, device_id=peer, device_id_type=MESH)
    pl.semaphore_wait(barrier, 7)

    far_s = (1 - x) * 2 + c

    def token_copy(r):
        return remote(tokens_hbm.at[r], nb.at[s, r], tok_send.at[r], tok_recv.at[r], x_peer)

    def core_copy(r):
        return remote(tokens_hbm.at[r], nb.at[s, r], core_send.at[r], core_recv.at[r], core_peer)

    def forward_copy(r):
        return remote(nb.at[c, r], nb.at[c, r], fwd_send.at[r], fwd_recv.at[r], core_peer)

    wc_copies = [
        remote(win_hbm, win.at[s], wc_send.at[0], wc_recv.at[0], core_peer),
        remote(wout_hbm, wout.at[s], wc_send.at[1], wc_recv.at[1], core_peer),
    ]
    chunk = width // 4
    even = lax.rem(dp, 2) == 0
    swap_peer = (dp + 1 - 2 * lax.rem(dp, 2), s, y)

    def by_parity(action):
        @pl.when(even)
        def _():
            action(win, wout, win_hbm)

        @pl.when(jnp.logical_not(even))
        def _():
            action(wout, win, wout_hbm)

    def rows_of(j):
        return slice(j * chunk, (j + 1) * chunk)

    def wx_copy(j, matrix, source):
        return remote(source.at[rows_of(j)], matrix.at[s, rows_of(j)], wx_send.at[j], wx_recv.at[j], x_peer)

    def wz_copy(j, matrix):
        return remote(matrix.at[far_s, rows_of(j)], matrix.at[far_s, rows_of(j)], wz_send.at[j], wz_recv.at[j], swap_peer)

    def wf_copy(k, j, matrix):
        return remote(matrix.at[far_s, rows_of(j)], matrix.at[far_s, rows_of(j)],
                      wf_send.at[4 * k + j], wf_recv.at[4 * k + j], core_peer)

    def from_x(j):
        def action(first, second, source):
            wx_copy(j, first, source).wait_recv()
            wz_copy(j, first).start()
            wf_copy(0, j, first).start()
        by_parity(action)

    def from_z(j):
        def action(first, second, source):
            wz_copy(j, second).wait_recv()
            wf_copy(1, j, second).start()
        by_parity(action)

    @pl.when(x == 0)
    def _():
        for r in range(2):
            token_copy(r).start()

    by_parity(lambda first, second, source: [wx_copy(j, first, source).start() for j in range(4)] and None)

    @pl.when(c == 0)
    def _():
        for r in range(2):
            core_copy(r).start()

    wc_copies[0].start()
    wc_copies[1].start()

    ids = jnp.concatenate([ids_ref[0:1, :], ids_ref[1:2, :]], axis=1)
    high = ids // 128
    low = ids - high * 128
    pick = jnp.where(lax.broadcasted_iota(I32, (64, local), 0) == high, 1.0, 0.0).astype(BF16)
    looked = dot_tn(table_ref[...].astype(F32).astype(BF16), pick)
    expert_row = jnp.sum(
        jnp.where(lax.broadcasted_iota(I32, (128, local), 0) == low, looked, 0.0), axis=0, keepdims=True)
    mine = jnp.where(expert_row == y.astype(F32), 1.0, 0.0)
    sixteen = lax.broadcasted_iota(I32, (16, local), 0)
    both = jnp.where(sixteen == 0, mine, jnp.where(sixteen == 1, 1.0 - mine, 0.0)).astype(BF16)
    before = jnp.where(
        lax.broadcasted_iota(I32, (local, local), 0) < lax.broadcasted_iota(I32, (local, local), 1), 1.0, 0.0
    ).astype(BF16)
    ranks = dot_nn(both, before)
    slot_rows = lax.broadcasted_iota(I32, (cap, local), 0).astype(F32)
    for u in range(2):
        chosen = mine if u == 0 else 1.0 - mine
        route[u] = jnp.where(slot_rows == ranks[u:u + 1, :], chosen, 0.0).astype(BF16)

    cot_copy = remote(stage, cs.at[cap:], y_send.at[0], y_recv.at[0], y_peer)
    xs_copy = remote(stage, xs.at[cap:], y_send.at[1], y_recv.at[1], y_peer)
    stage[...] = dot_nn(route[1], cot_ref[...]).astype(BF16)
    cot_copy.start()
    cs[0:cap] = dot_nn(route[0], cot_ref[...]).astype(BF16)

    gain_a = gain_a_ref[...].reshape(1, width)
    gain_f = gain_f_ref[...].reshape(1, width)

    def normalise(part, r):
        nb[part, r] = (norm_parts(nb[part, r].astype(F32))[0] * gain_a).astype(BF16)

    def project(part, r):
        normed = nb[part, r]
        ks[part, r] = dot_nn(normed, wk_ref[...]).astype(BF16)
        vs[part, r] = dot_nn(normed, wv_ref[...]).astype(BF16)

    first_half = lax.broadcasted_iota(I32, (span, 128), 1) < HD
    first_rows = lax.broadcasted_iota(I32, (128, span), 0) < HD

    def apart(values, keep, axis):
        none = jnp.zeros_like(values)
        return jnp.concatenate([jnp.where(keep, values, none), jnp.where(keep, none, values)], axis=axis)

    def pair_lanes(p):
        return pl.ds(pl.multiple_of(p * 128, 128), 128)

    def head_rows(p, hh):
        return pl.ds(pl.multiple_of(p * 128 + hh * HD, HD), HD)

    def e_near(r, p, slot, write, both_parts):
        here = ebuf.at[slot] if both_parts else ebuf.at[slot, 1]
        there = es_hbm.at[0, r, p] if both_parts else es_hbm.at[0, r, p, 1]
        return pltpu.make_async_copy(here if write else there, there if write else here, e_sem.at[slot])

    def e_far(r, p, slot, write):
        here = ebuf.at[slot]
        there = es_hbm.at[1, r, p]
        return pltpu.make_async_copy(here if write else there, there if write else here, e_sem.at[slot])

    def attend(r, p, slot, parts, places, diagonal):
        lanes = pair_lanes(p)
        q_two = apart(qs[r, :, lanes], first_half, 0)
        v_flipped = [vs[part, r, :, lanes].T for part in parts]
        scores = [dot_nt(ks[part, r, :, lanes], q_two) for part in parts]
        if diagonal:
            ki = lax.broadcasted_iota(I32, (span, 2 * span), 0)
            qi = lax.broadcasted_iota(I32, (span, 2 * span), 1)
            qi = jnp.where(qi >= span, qi - span, qi)
            scores[-1] = jnp.where(ki <= qi, scores[-1], masked_score)
        peak = jnp.max(scores[0], axis=0, keepdims=True)
        for extra in scores[1:]:
            peak = jnp.maximum(peak, jnp.max(extra, axis=0, keepdims=True))
        weights = [jnp.exp(one - peak) for one in scores]
        total = jnp.sum(weights[0], axis=0, keepdims=True)
        for extra in weights[1:]:
            total = total + jnp.sum(extra, axis=0, keepdims=True)
        low_weights = [one.astype(BF16) for one in weights]
        for place, one in zip(places, low_weights):
            ebuf[slot, place] = one
        results = []
        for hh in range(2):
            columns = slice(hh * span, (hh + 1) * span)
            mixed = 0.0
            for v_one, one in zip(v_flipped, low_weights):
                mixed = mixed + dot_nn(v_one[hh * HD:(hh + 1) * HD], one[:, columns])
            results.append((2 * p + hh, head_rows(p, hh), peak[:, columns], total[:, columns], mixed))
        return results

    own_copy.wait()

    def own_rows(r, carry):
        mid[r] = nb[s, r].astype(F32)
        normalise(s, r)
        project(s, r)
        qs[r] = (dot_nn(nb[s, r], wq_ref[...]) * (HD ** -0.5)).astype(BF16)
        return carry

    lax.fori_loop(0, 2, own_rows, 0)

    def near_loop(parts, places):
        wide = len(parts) == 2

        def step(i, carry):
            r, p, slot = i // 6, lax.rem(i, 6), lax.rem(i, 2)

            @pl.when(i >= 2)
            def _():
                e_near(r, p, slot, True, wide).wait()

            for h, rows, peak, total, mixed in attend(r, p, slot, parts, places, True):
                stat[r, h, 0:1] = peak
                stat[r, h, 1:2] = total
                oa[r, rows, :] = mixed
            e_near(r, p, slot, True, wide).start()
            return carry

        lax.fori_loop(0, 12, step, 0)
        for slot in range(2):
            e_near(1, 4 + slot, slot, True, wide).wait()

    @pl.when(c == 0)
    def _():
        near_loop([s], [1])

    @pl.when(c == 1)
    def _():
        for r in range(2):
            core_copy(r).wait_recv()

        def partner_rows(r, carry):
            normalise(s - 1, r)
            project(s - 1, r)
            return carry

        lax.fori_loop(0, 2, partner_rows, 0)
        near_loop([s - 1, s], [0, 1])

    @pl.when(x == 0)
    def _():
        def step(i, carry):
            r, h = i // H, lax.rem(i, H)
            rows = pl.ds(pl.multiple_of(h * HD, HD), HD)
            inverse = 1.0 / stat[r, h, 1:2]
            facs[r, h, 0:1] = inverse
            facs[r, h, 1:2] = jnp.zeros_like(inverse)
            oa[r, rows, :] = oa[r, rows, :] * inverse
            return carry

        lax.fori_loop(0, 2 * H, step, 0)
        from_x(0)

    @pl.when(x == 1)
    def _():
        for r in range(2):
            token_copy(r).wait_recv()
            normalise(c, r)
            forward_copy(r).start()
            project(c, r)
            forward_copy(r).wait()
            project(1 - c, r)
            if r == 1:
                from_x(0)
            single = lengths_ref[r, 1] == 0

            def step(p, carry):
                slot = lax.rem(p, 2)

                @pl.when(p >= 2)
                def _():
                    e_far(r, p, slot, True).wait()

                for h, rows, peak, total, mixed in attend(r, p, slot, [0, 1], [0, 1], False):
                    near_peak = stat[r, h, 0:1]
                    peak = jnp.where(single, peak, near_peak)
                    top = jnp.maximum(peak, near_peak)
                    near_f = jnp.exp(near_peak - top)
                    far_f = jnp.where(single, jnp.exp(peak - top), 0.0)
                    whole = near_f * stat[r, h, 1:2] + far_f * total
                    near_f = near_f / whole
                    far_f = far_f / whole
                    facs[r, h, 0:1] = near_f
                    facs[r, h, 1:2] = far_f
                    oa[r, rows, :] = oa[r, rows, :] * near_f + mixed * far_f
                e_far(r, p, slot, True).start()
                return carry

            lax.fori_loop(0, 6, step, 0)
            for slot in range(2):
                e_far(r, 4 + slot, slot, True).wait()

    def out_rows(r, carry):
        att = oa[r].astype(BF16).T
        value = mid[r] + dot_nn(att, wo_ref[...])
        mid[r] = value
        do[0, r] = (norm_parts(value)[0] * gain_f).astype(BF16)
        return carry

    lax.fori_loop(0, 2, out_rows, 0)
    from_x(1)

    ffn_in = do[0].reshape(local, width)
    cot_copy.wait_send()
    stage[...] = dot_nn(route[1], ffn_in).astype(BF16)
    xs_copy.start()
    xs[0:cap] = dot_nn(route[0], ffn_in).astype(BF16)
    win_copy.wait()
    wout_copy.wait()
    acc[...] = jnp.zeros_like(acc)

    def expert_rows(u, f):
        rows = pl.ds(pl.multiple_of(u * cap, cap), cap)
        tokens_in = xs[rows]
        grads_in = cs[rows]
        for n in range(3):
            lanes = slice(n * 256, (n + 1) * 256)
            pre = dot_nn(tokens_in, win[f, :, lanes])
            up = dot_nt(grads_in, wout[f, lanes])
            square = pre * pre
            bent = jnp.tanh(gelu_a * pre * (1.0 + gelu_b * square))
            half = 0.5 * (1.0 + bent)
            slope = half + 0.5 * pre * (1.0 - bent * bent) * (gelu_a * (1.0 + 3.0 * gelu_b * square))
            hid[f, rows, lanes] = (pre * half).astype(BF16)
            gp[f, rows, lanes] = (up * slope).astype(BF16)
        acc[rows] += dot_nt(gp[f, rows], win[f])

    def expert_number(ix, ic):
        return 2 * lax.rem(x + ix, 2) + lax.rem(c + ic, 2)

    def moe_step(i, carry):
        ix = i // 4
        outer, inner = lax.rem(i // 2, 2), lax.rem(i, 2)

        @pl.when(i == 2)
        def _():
            xs_copy.wait_recv()
            cot_copy.wait_recv()

        @pl.when(i == 6)
        def _():
            by_parity(lambda first, second, source: [
                wf_copy(k, j, (first, second)[k]).wait_recv() for k in range(2) for j in range(4)] and None)

        @pl.when(i == 1)
        def _():
            wc_copies[0].wait_recv()
            wc_copies[1].wait_recv()
        expert_rows(jnp.where(ix == 0, outer, inner), expert_number(ix, jnp.where(ix == 0, inner, outer)))

        @pl.when(i == 0)
        def _():
            from_x(2)
            from_z(0)

        @pl.when(i == 1)
        def _():
            from_x(3)
            from_z(1)
            from_z(2)

        @pl.when(i == 3)
        def _():
            from_z(3)
        return carry

    lax.fori_loop(0, 8, moe_step, 0)

    grad_copy = remote(xgb.at[cap:], gback, y_send.at[2], y_recv.at[2], y_peer)
    out_copy = remote(eob.at[cap:], eback, y_send.at[3], y_recv.at[3], y_peer)
    xgb[...] = acc[...].astype(BF16)
    grad_copy.start()
    acc[...] = jnp.zeros_like(acc)
    wc_copies[0].wait_send()
    wc_copies[1].wait_send()
    by_parity(lambda first, second, source: [
        wf_copy(k, j, (first, second)[k]).wait_send() for k in range(2) for j in range(4)] and None)
    by_parity(lambda first, second, source: [wz_copy(j, first).wait_send() for j in range(4)] and None)
    xs_copy.wait_send()

    shard_a = expert_number(1, 0)
    shard_b = expert_number(1, 1)
    shard_c = expert_number(0, 1)
    ends = jnp.logical_or(dp == 0, dp == 3)
    end_z = jnp.where(dp < 2, 0, 3)
    near_mid = (jnp.where(dp < 2, 1, 2), s, y)
    other_mid = (3 - dp, s, y)
    end_peer = (end_z, s, y)
    core_sends = [
        remote(win.at[shard_b], ra_hbm.at[0], ed_send.at[0], ed_recv.at[0], core_peer),
        remote(wout.at[shard_b], ra_hbm.at[1], ed_send.at[1], ed_recv.at[1], core_peer),
        remote(win.at[shard_c], ro_hbm.at[0], ed_send.at[2], ed_recv.at[2], core_peer),
        remote(wout.at[shard_c], ro_hbm.at[1], ed_send.at[3], ed_recv.at[3], core_peer),
    ]

    load_a = [
        pltpu.make_async_copy(ra_hbm.at[0], win.at[shard_b], local_sem.at[1]),
        pltpu.make_async_copy(ra_hbm.at[1], wout.at[shard_b], local_sem.at[2]),
    ]
    load_o = [
        pltpu.make_async_copy(ro_hbm.at[0], win.at[shard_c], local_sem.at[1]),
        pltpu.make_async_copy(ro_hbm.at[1], wout.at[shard_c], local_sem.at[2]),
    ]

    def piece(k):
        return pl.ds(pl.multiple_of(lax.rem(k, 4) * chunk, chunk), chunk)

    def add_to(target, first, second):
        target[...] = first[...] + second[...]

    def by_matrix(k, action):
        @pl.when(k < 4)
        def _():
            action(win, dwin_hbm)

        @pl.when(k >= 4)
        def _():
            action(wout, dwout_hbm)

    def x_grad(k, grads):
        return remote(grads.at[shard_a, piece(k)], grads.at[shard_c, piece(k)],
                      ex_send.at[k], ex_recv.at[k], x_peer)

    def end_grad(k, grads):
        return remote(grads.at[s, piece(k)], grads.at[shard_c, piece(k)], ee_send.at[k], ee_recv.at[k], near_mid)

    def mid_grad(k, grads):
        return remote(grads.at[s, piece(k)], grads.at[shard_a, piece(k)], em_send.at[k], em_recv.at[k], other_mid)

    def back_grad(k, grads, out):
        return remote(grads.at[shard_b, piece(k)], out.at[piece(k)], eb_send.at[k], eb_recv.at[k], end_peer)

    def out_grad(k, grads, out):
        return pltpu.make_async_copy(grads.at[shard_b, piece(k)], out.at[piece(k)], eo_sem.at[k])

    def send_x(k):
        pl.semaphore_wait(free_x, 1)
        by_matrix(k, lambda grads, out: x_grad(k, grads).start())

    def start_x():
        def step(k, carry):
            by_matrix(k, lambda grads, out: add_to(
                grads.at[shard_a, piece(k)], grads.at[shard_a, piece(k)], grads.at[shard_b, piece(k)]))
            pl.semaphore_signal(free_x, inc=1, device_id=x_peer, device_id_type=MESH)

            @pl.when(jnp.logical_and(k >= 1, k < 4))
            def _():
                send_x(k - 1)
            return carry

        lax.fori_loop(0, 8, step, 0)

    def chain(kind, number):
        k = jnp.int32(number)

        def action(grads, out):
            if kind == 1:
                x_grad(k, grads).wait()
                if number < 3:
                    send_x(k + 3)
                add_to(grads.at[s, piece(k)], grads.at[s, piece(k)], grads.at[shard_b, piece(k)])

                @pl.when(ends)
                def _():
                    if number == 0:
                        pl.semaphore_wait(free_z, 1)
                    end_grad(k, grads).start()

                @pl.when(jnp.logical_not(ends))
                def _():
                    pl.semaphore_signal(free_m, inc=1, device_id=other_mid, device_id_type=MESH)
            if kind == 2:
                @pl.when(jnp.logical_not(ends))
                def _():
                    end_grad(k, grads).wait_recv()
                    add_to(grads.at[s, piece(k)], grads.at[s, piece(k)], grads.at[shard_c, piece(k)])
                    pl.semaphore_wait(free_m, 1)
                    mid_grad(k, grads).start()
            if kind == 3:
                @pl.when(jnp.logical_not(ends))
                def _():
                    mid_grad(k, grads).wait_recv()
                    add_to(grads.at[shard_b, piece(k)], grads.at[s, piece(k)], grads.at[shard_a, piece(k)])
                    out_grad(k, grads, out).start()
                    back_grad(k, grads, out).start()

        action(*((win, dwin_hbm) if number < 4 else (wout, dwout_hbm)))

    def chain_all(steps):
        for kind, number in steps:
            chain(kind, number)

    def drain_chain():
        def step(k, carry):
            def action(grads, out):
                @pl.when(ends)
                def _():
                    end_grad(k, grads).wait_send()
                    back_grad(k, grads, out).wait_recv()

                @pl.when(jnp.logical_not(ends))
                def _():
                    mid_grad(k, grads).wait_send()
                    back_grad(k, grads, out).wait_send()
                    out_grad(k, grads, out).wait()
            by_matrix(k, action)
            return carry

        lax.fori_loop(0, 8, step, 0)

    half = width // 2
    tall = width // 2
    corner = 2 * x + y
    sums = [None] * 8

    def sum_step(m, step):
        source, at, out, to = sums[m]
        lanes = slice(at, at + half)
        goal = slice(to, to + half)
        (one, one_peer), (two, two_peer) = [(x, x_peer), (y, y_peer)] if m == 6 else [(y, y_peer), (x, x_peer)]
        low_one = c * tall + one * (tall // 2)
        low_two = low_one + two * (tall // 4)

        def rows(start, size):
            return pl.ds(pl.multiple_of(start, size), size)

        mine = rows(c * tall, tall)
        theirs = rows((1 - c) * tall, tall)
        kept_one = rows(low_one, tall // 2)
        sent_one = rows(c * tall + (1 - one) * (tall // 2), tall // 2)
        kept_two = rows(low_two, tall // 4)
        sent_two = rows(low_one + (1 - two) * (tall // 4), tall // 4)
        in_one = slice(0, tall // 2)
        in_two = slice(tall // 2, 3 * tall // 4)
        final = slice(0, tall // 4)
        slot = (slice((m // 2) * (tall // 4), (m // 2 + 1) * (tall // 4)), slice((m % 2) * half, (m % 2 + 1) * half))

        def core_send():
            return remote(source.at[theirs, lanes], recv_d, rd_send.at[m], rd_recv.at[m], core_peer)

        def one_part():
            return remote(source.at[sent_one, lanes], recv_p.at[m, in_one], rp_send.at[m, 0], rp_recv.at[m, 0], one_peer)

        def two_part():
            return remote(source.at[sent_two, lanes], recv_p.at[m, in_two], rp_send.at[m, 1], rp_recv.at[m, 1], two_peer)

        def end_part():
            return remote(source.at[kept_two, lanes], gback.at[slot], rp_send.at[m, 2], rp_recv.at[m, 2], near_mid)

        def mid_part():
            return remote(source.at[kept_two, lanes], eback.at[slot], rp_send.at[m, 3], rp_recv.at[m, 3], other_mid)

        def back_part():
            return remote(recv_p.at[m, final], out.at[kept_two, goal], rz_send.at[m, 0], rz_recv.at[m, 0], end_peer)

        def own_store():
            return pltpu.make_async_copy(recv_p.at[m, final], out.at[kept_two, goal], own_sem.at[m])

        def two_gather():
            return remote(out.at[kept_two, goal], out.at[kept_two, goal], rz_send.at[m, 1], rz_recv.at[m, 1], two_peer)

        def one_gather():
            return remote(out.at[kept_one, goal], out.at[kept_one, goal], rz_send.at[m, 2], rz_recv.at[m, 2], one_peer)

        def core_gather():
            return remote(out.at[mine, goal], out.at[mine, goal], gd_send.at[m], gd_recv.at[m], core_peer)

        if step == 0:
            if m > 0:
                pl.semaphore_wait(free_d, 1)
            core_send().start()
        if step == 1:
            core_send().wait()
            add_to(source.at[mine, lanes], source.at[mine, lanes], recv_d)
            if m < 7:
                pl.semaphore_signal(free_d, inc=1, device_id=core_peer, device_id_type=MESH)
            one_part().start()
        if step == 2:
            one_part().wait()
            add_to(source.at[kept_one, lanes], source.at[kept_one, lanes], recv_p.at[m, in_one])
            two_part().start()
        if step == 3:
            two_part().wait()
            add_to(source.at[kept_two, lanes], source.at[kept_two, lanes], recv_p.at[m, in_two])

            @pl.when(ends)
            def _():
                if m == 0:
                    pl.semaphore_wait(free_e, 1)
                end_part().start()
        if step == 4:
            @pl.when(jnp.logical_not(ends))
            def _():
                end_part().wait_recv()
                add_to(source.at[kept_two, lanes], source.at[kept_two, lanes], gback.at[slot])
                mid_part().start()
        if step == 5:
            @pl.when(jnp.logical_not(ends))
            def _():
                mid_part().wait_recv()
                add_to(recv_p.at[m, final], source.at[kept_two, lanes], eback.at[slot])
                own_store().start()
                back_part().start()
        if step == 6:
            @pl.when(ends)
            def _():
                end_part().wait_send()
                back_part().wait_recv()

            @pl.when(jnp.logical_not(ends))
            def _():
                mid_part().wait_send()
                own_store().wait()
                back_part().wait_send()
            two_gather().start()
        if step == 7:
            two_gather().wait()
            one_gather().start()
        if step == 8:
            one_gather().wait()
            core_gather().start()
        if step == 9:
            core_gather().wait()

    def run(steps):
        for one in steps:
            if one[0] == "c":
                chain(one[1], one[2])
            if one[0] == "s":
                sum_step(one[1], one[2])
            if one[0] == "x":
                send_x(jnp.int32(one[1]))
            if one[0] == "f":
                far_send_on(one[1])

    def weight_grads(i):
        f = expert_number(1 - i // 2, lax.rem(i + 1, 2))
        win[f] = dot_tn(xs[...], gp[f]).astype(BF16)

        @pl.when(i == 0)
        def _():
            core_sends[0].start()

        @pl.when(i == 2)
        def _():
            core_sends[2].start()
            for k in range(2):
                load_a[k].wait()
            start_x()
        acc[...] += dot_nn(hid[f], wout[f])
        wout[f] = dot_tn(hid[f], cs[...]).astype(BF16)

    def grads_step(i, carry):
        weight_grads(i)

        @pl.when(i == 0)
        def _():
            core_sends[1].start()

        @pl.when(i == 1)
        def _():
            for k in range(2):
                core_sends[k].wait()
                load_a[k].start()

        @pl.when(i == 2)
        def _():
            core_sends[3].start()
        return carry

    lax.fori_loop(0, 4, grads_step, 0)
    eob[...] = acc[...].astype(BF16)
    out_copy.start()
    for k in range(2):
        core_sends[2 + k].wait()
        load_o[k].start()

    for k in range(2):
        load_o[k].wait()
    add_to(win.at[s], win.at[s], win.at[shard_c])
    add_to(wout.at[s], wout.at[s], wout.at[shard_c])

    @pl.when(jnp.logical_not(ends))
    def _():
        pl.semaphore_signal(free_z, inc=1, device_id=end_peer, device_id_type=MESH)

    grad_copy.wait_recv()
    acc[...] = jnp.zeros_like(acc)
    gg_ref[...] = jnp.zeros_like(gg_ref)

    def take_back(r, own, returned):
        picked = pl.ds(pl.multiple_of(r * span, span), span)
        return dot_tn(route[0, :, picked], own) + dot_tn(route[1, :, picked], returned)

    def ffn_back(r, carry):
        rows = pl.ds(pl.multiple_of(r * span, span), span)
        grad = take_back(r, xgb[0:cap], gback[...])
        xhat, root = norm_parts(mid[r])
        gg_ref[0:1] += jnp.sum(grad * xhat, axis=0, keepdims=True)
        whole = cot_ref[rows].astype(F32) + norm_back(grad, gain_f, xhat, root)
        preg[r] = whole
        branch = whole.astype(BF16)
        att = oa[r]
        acc[...] += dot_nn(att.astype(BF16), branch)
        up = dot_nt(wo_ref[...], branch)
        up3 = up.reshape(H, HD, span)
        inner = jnp.sum(up3 * att.reshape(H, HD, span), axis=1, keepdims=True)
        for g in range(2):
            factor = facs[r, :, g:g + 1]
            dl[r, :, g:g + 1] = inner * factor
            flipped = (up3 * factor).reshape(width, span).astype(BF16)
            dot[g, r] = flipped
            do[g, r] = flipped.T
        oa[r] = jnp.zeros_like(oa[r])
        return carry

    chain(1, 0)
    lax.fori_loop(0, 2, ffn_back, 0)

    @pl.when(jnp.logical_not(ends))
    def _():
        pl.semaphore_signal(free_e, inc=1, device_id=end_peer, device_id_type=MESH)

    xs[...] = acc[...].astype(BF16)
    sums[0] = (xs, 0, dwo_hbm, 0)
    sums[1] = (xs, half, dwo_hbm, half)
    sum_step(0, 0)
    run([("c", 1, 1)])

    def attend_back(r, p, slot, g, parts, places):
        lanes = pair_lanes(p)
        q_two = apart(qs[r, :, lanes], first_half, 0)
        do_two = apart(do[g, r, :, lanes], first_half, 0)
        dot_two = apart(dot[g, r, lanes, :], first_rows, 1)
        inner = jnp.concatenate([dl[r, 2 * p, g:g + 1], dl[r, 2 * p + 1, g:g + 1]], axis=1)
        grad_q = [0.0, 0.0]
        for part, place in zip(parts, places):
            weights = ebuf[slot, place]
            k_flipped = ks[part, r, :, lanes].T
            grad_p = dot_nn(vs[part, r, :, lanes], dot_two)
            grad_s = (weights.astype(F32) * (grad_p - inner)).astype(BF16)
            place_rows = pl.ds(pl.multiple_of(r * span, span), span)
            hid[part, place_rows, lanes] = dot_nn(grad_s, q_two).astype(BF16)
            gp[part, place_rows, lanes] = dot_nn(weights, do_two).astype(BF16)
            for hh in range(2):
                columns = slice(hh * span, (hh + 1) * span)
                grad_q[hh] = grad_q[hh] + dot_nn(k_flipped[hh * HD:(hh + 1) * HD], grad_s[:, columns])
        for hh in range(2):
            oa[r, head_rows(p, hh), :] += grad_q[hh]

    def back_loop(g, parts, places, hf, extra):
        wide = len(parts) == 2

        def fetch(i):
            r, p, slot = i // 3, 3 * hf + lax.rem(i, 3), lax.rem(i, 2)
            return e_near(r, p, slot, False, wide) if g == 0 else e_far(r, p, slot, False)

        fetch(0).start()

        def step(i, carry):
            @pl.when(i < 5)
            def _():
                fetch(i + 1).start()
            fetch(i).wait()
            attend_back(i // 3, 3 * hf + lax.rem(i, 3), lax.rem(i, 2), g, parts, places)
            for at, steps in extra.items():
                @pl.when(jnp.logical_and(i == at, x == 1))
                def _():
                    run(steps)
            return carry

        lax.fori_loop(0, 6, step, 0)

    def gain_part(part, grad):
        gg_ref[1:2] += jnp.sum(grad * nb[part].reshape(local, width).astype(F32), axis=0, keepdims=True)

    def normed_grad(part):
        grad = dot_nt(hid[part, 0:local], wk_ref[...]) + dot_nt(gp[part, 0:local], wv_ref[...])
        gain_part(part, grad)
        return grad

    far_core = remote(cs.at[0:local], dnr0, dn_send.at[0], dn_recv.at[0], core_peer)
    def far_x(k):
        rows = slice(k * span // 4, (k + 1) * span // 4)
        return remote(cs.at[rows], dnr0.at[rows], far_send.at[k], far_recv.at[k], x_peer)

    def far_send_on(k):
        @pl.when(x == 1)
        def _():
            far_x(k).start()

    near_core = [
        remote(hid.at[r, local:local + span], nd_hbm.at[r], near_send.at[r], near_recv.at[r], core_peer) for r in range(2)]

    out_done = [
        pltpu.make_async_copy(cs.at[r * span:(r + 1) * span], out_hbm.at[r], local_sem.at[4 + r]) for r in range(2)]

    def out_add(r, carry):
        rows = pl.ds(pl.multiple_of(r * span, span), span)
        cs[rows] = (mid[r] + take_back(r, eob[0:cap], eback[...])).astype(BF16)
        return carry

    def near_both(hf, extra):
        @pl.when(c == 0)
        def _():
            back_loop(0, [s], [1], hf, extra)

        @pl.when(c == 1)
        def _():
            back_loop(0, [s - 1, s], [0, 1], hf, extra)

    def late(*lists):
        @pl.when(x == 0)
        def _():
            for extra in lists:
                for at in sorted(extra):
                    run(extra[at])

    def all_parts(grads, hf):
        columns = slice(hf * half, (hf + 1) * half)
        acc[:, 0:half] = jnp.zeros_like(acc[:, 0:half])

        def step(part, carry):
            acc[:, 0:half] += dot_tn(nb[part].reshape(local, width), grads[part, 0:local, columns])
            return carry

        @pl.when(x == 1)
        def _():
            lax.fori_loop(0, 2, step, 0)

        @pl.when(c == 1)
        def _():
            step(s - 1, 0)

        step(s, 0)
        return acc[:, 0:half].astype(BF16)

    def query_part(hf):
        columns = slice(hf * half, (hf + 1) * half)
        for r in range(2):
            qs[r, :, columns] = (oa[r, columns, :] * (HD ** -0.5)).astype(BF16).T
        return dot_tn(nb[s].reshape(local, width), qs[:, :, columns].reshape(local, half)).astype(BF16)

    @pl.when(x == 1)
    def _():
        back_loop(1, [0, 1], [0, 1], 0, FAR_ONE)
    grad_copy.wait_send()
    near_both(0, NEAR_ONE)
    late(FAR_ONE, NEAR_ONE)
    out_copy.wait()
    lax.fori_loop(0, 2, out_add, 0)
    for r in range(2):
        out_done[r].start()
    run(AFTER_ONE[0])
    xgb[:, 0:half] = all_parts(hid, 0)
    sums[2] = (xgb, 0, dwk_hbm, 0)
    run(AFTER_ONE[1])
    xgb[:, half:width] = all_parts(gp, 0)
    sums[3] = (xgb, half, dwv_hbm, 0)
    run(AFTER_ONE[2])
    eob[:, 0:half] = query_part(0)
    sums[4] = (eob, 0, dwq_hbm, 0)
    run(AFTER_ONE[3])
    for r in range(2):
        out_done[r].wait()

    @pl.when(x == 1)
    def _():
        back_loop(1, [0, 1], [0, 1], 1, FAR_TWO)
        cs[0:local] = normed_grad(1 - c).astype(BF16)
        far_core.start()
        mine_far = normed_grad(c)
        far_core.wait()
        cs[0:local] = (mine_far + dnr0[...].astype(F32)).astype(BF16)

    near_both(1, NEAR_TWO)
    late(FAR_TWO, NEAR_TWO)

    @pl.when(c == 1)
    def _():
        behind = normed_grad(s - 1).astype(BF16)
        for r in range(2):
            hid[r, local:local + span] = behind[r * span:(r + 1) * span]
            near_core[r].start()

    tokens_again = pltpu.make_async_copy(tokens_hbm, do.at[1], local_sem.at[0])
    tokens_again.start()
    run(AFTER_TWO[0])
    key_part = all_parts(hid, 1)
    eob[:, half:width] = key_part
    sums[5] = (eob, half, dwk_hbm, half)
    run(AFTER_TWO[1])
    values_part = all_parts(gp, 1)
    late_sums = gp.at[lax.rem(s + 1, 4)]
    late_sums[:, 0:half] = values_part
    sums[6] = (late_sums, 0, dwv_hbm, half)
    run(AFTER_TWO[2])
    late_sums[:, half:width] = query_part(1)
    sums[7] = (late_sums, half, dwq_hbm, half)
    run(AFTER_TWO[3])
    from_query = dot_nt(qs[...].reshape(local, width), wq_ref[...])
    gain_part(s, from_query)
    acc[0:local] = normed_grad(s) + from_query
    gg_ref[1:2] = gg_ref[1:2] / gain_a

    def gain_sum(first, mine, count, peers, sems):
        gsum[first + mine] = gg_ref[...]
        copies = [
            remote(gsum.at[first + mine], gsum.at[first + mine], gn_send.at[sems + k], gn_recv.at[sems + k], peer)
            for k, peer in enumerate(peers)]
        for one in copies:
            one.start()
        return copies

    def gain_total(first, count, copies):
        for one in copies:
            one.wait()
        total = gsum[first]
        for k in range(1, count):
            total = total + gsum[first + k]
        gg_ref[...] = total

    copies = gain_sum(0, c, 2, [core_peer], 0)
    run(TAIL[0])
    gain_total(0, 2, copies)
    copies = gain_sum(2, corner, 4, plane_peers, 1)
    run(TAIL[1])
    gain_total(2, 4, copies)
    copies = gain_sum(6, dp, 4, z_peers, 4)
    run(TAIL[2])
    @pl.when(c == 0)
    def _():
        for r in range(2):
            near_core[r].wait_recv()
        loaded = pltpu.make_async_copy(nd_hbm, do.at[0], local_sem.at[3])
        loaded.start()
        loaded.wait()
        acc[0:local] += do[0].reshape(local, width).astype(F32)

    @pl.when(x == 0)
    def _():
        for k in range(8):
            far_x(k).wait_recv()
        acc[0:local] += dnr0[...].astype(F32)

    tokens_again.wait()

    def first_back(r, carry):
        rows = pl.ds(pl.multiple_of(r * span, span), span)
        grad = acc[rows]
        xhat, root = norm_parts(do[1, r].astype(F32))
        mid[r] = preg[r] + norm_back(grad, gain_a, xhat, root)
        return carry

    lax.fori_loop(0, 2, first_back, 0)
    ig_done = pltpu.make_async_copy(mid, ig_hbm, local_sem.at[0])
    ig_done.start()

    run(TAIL[3])
    gain_total(6, 4, copies)
    gain_a_out[...] = gg_ref[1:2].reshape(width)
    gain_f_out[...] = gg_ref[0:1].reshape(width)
    for m in range(8):
        sum_step(m, 9)
    drain_chain()
    ig_done.wait()
    by_parity(lambda first, second, source: [wx_copy(j, first, source).wait_send() for j in range(4)] and None)

    @pl.when(x == 1)
    def _():
        for k in range(8):
            far_x(k).wait_send()

    @pl.when(x == 0)
    def _():
        for r in range(2):
            token_copy(r).wait_send()

    @pl.when(c == 1)
    def _():
        for r in range(2):
            near_core[r].wait_send()

    @pl.when(c == 0)
    def _():
        for r in range(2):
            core_copy(r).wait_send()


def block(tokens, cot, ids, table, lengths, gain_a, gain_f, wq, wk, wv, wo, w_in, w_out):
    rows, span, width = tokens.shape
    local = rows * span
    cap = 3 * local // 4
    vmem = pl.BlockSpec(memory_space=pltpu.VMEM)
    hbm = pl.BlockSpec(memory_space=pl.ANY)
    smem = pl.BlockSpec(memory_space=pltpu.SMEM)
    sem = pltpu.SemaphoreType.DMA
    signal = pltpu.SemaphoreType.REGULAR
    square = (width, width)
    blocks = (4, rows, span, width)
    flipped = (2, rows, width, span)
    shape = jax.ShapeDtypeStruct
    return pl.pallas_call(
        block_kernel,
        out_shape=(
            shape((rows, span, width), BF16),
            shape((rows, span, width), F32),
            shape(square, BF16), shape(square, BF16), shape(square, BF16), shape(square, BF16),
            shape(square, BF16), shape(square, BF16),
            shape((width,), F32), shape((width,), F32),
            shape((2, rows, 6, 2, span, 2 * span), BF16),
            shape((2,) + square, BF16), shape((2,) + square, BF16), shape((rows, span, width), BF16),
        ),
        in_specs=[hbm, vmem, vmem, vmem, smem, vmem, vmem, vmem, vmem, vmem, vmem, hbm, hbm],
        out_specs=(hbm,) * 8 + (vmem, vmem, hbm, hbm, hbm, hbm),
        scratch_shapes=[
            pltpu.VMEM(blocks, BF16),
            pltpu.VMEM(square, BF16),
            pltpu.VMEM(square, BF16),
            pltpu.VMEM((rows, span, width), BF16),
            pltpu.VMEM(blocks, BF16),
            pltpu.VMEM(blocks, BF16),
            pltpu.VMEM(flipped, BF16),
            pltpu.VMEM((2, 2, span, 2 * span), BF16),
            pltpu.VMEM((rows, width, span), F32),
            pltpu.VMEM((rows, H, 2, span), F32),
            pltpu.VMEM((rows, H, 2, span), F32),
            pltpu.VMEM((rows, H, 2, span), F32),
            pltpu.VMEM((2, cap, local), BF16),
            pltpu.VMEM((2 * cap, width), BF16),
            pltpu.VMEM((2 * cap, width), BF16),
            pltpu.VMEM((2, rows, span, width), BF16),
            pltpu.VMEM((rows, span, width), F32),
            pltpu.VMEM((4,) + square, BF16),
            pltpu.VMEM((4,) + square, BF16),
            pltpu.VMEM((2 * cap, width), F32),
            pltpu.VMEM((rows, span, width), F32),
            pltpu.VMEM((4, 2 * cap, width), BF16),
            pltpu.VMEM((4, 2 * cap, width), BF16),
            pltpu.VMEM((cap, width), BF16),
            pltpu.VMEM((cap, width), BF16),
            pltpu.VMEM((local, width), BF16),
            sem((6,)), sem((2,)), sem((2,)), sem((2,)), sem((2,)), sem((2,)), sem((2,)), sem((2,)),
            sem((4,)), sem((4,)), sem((4,)), sem((4,)), sem((8,)), sem((8,)), sem((2,)), sem((2,)),
            sem((4,)), sem((4,)), sem((3,)), sem((3,)), sem((8,)), sem((8,)),
            pltpu.VMEM((width // 2, width // 2), BF16),
            pltpu.VMEM((8, 3 * width // 8, width // 2), BF16),
            pltpu.VMEM((8, width), F32),
            pltpu.VMEM((10, 8, width), F32),
            sem((4,)), sem((4,)), sem((8,)), sem((8,)), sem((8,)), sem((8,)), sem((8,)), sem((8,)), sem((8,)), sem((8,)),
            sem((8,)), signal, signal, signal, signal, signal,
            sem((8,)), sem((8,)), sem((8, 4)), sem((8, 4)), sem((8, 3)), sem((8, 3)), sem((8,)), sem((8,)),
            sem((8,)), sem((7,)), sem((7,)), sem((2,)), sem((2,)),
        ],
        compiler_params=pltpu.CompilerParams(collective_id=1, has_side_effects=True, vmem_limit_bytes=62 << 20),
        name="block_step",
    )(tokens, cot, ids, table, lengths, gain_a, gain_f, wq, wk, wv, wo, w_in, w_out)


def finish_kernel(*refs):
    sources, targets = refs[:10], refs[10:20]
    low, wide, kept_low, kept_wide, in_sem, out_sem = refs[20:]
    loads = [pltpu.make_async_copy(sources[k], low.at[k], in_sem.at[k]) for k in range(6)]
    kept = [kept_low, kept_wide]
    loads += [pltpu.make_async_copy(sources[6 + k], kept[k], in_sem.at[6 + k]) for k in range(2)]
    stores = [pltpu.make_async_copy(wide.at[k], targets[k], out_sem.at[k]) for k in range(6)]
    stores += [pltpu.make_async_copy(kept[k], targets[6 + k], out_sem.at[6 + k]) for k in range(2)]
    for one in loads:
        one.start()
    for k in range(8, 10):
        targets[k][...] = sources[k][...]
    for k in range(6):
        loads[k].wait()
        wide[k] = low[k].astype(F32)
        stores[k].start()
    for k in range(6, 8):
        loads[k].wait()
        stores[k].start()
    for one in stores:
        one.wait()


def finish(squares, output, input_grad, gains):
    width = squares[0].shape[0]
    shape = jax.ShapeDtypeStruct
    arrays = list(squares) + [output, input_grad] + list(gains)
    hbm = pl.BlockSpec(memory_space=pl.ANY)
    vmem = pl.BlockSpec(memory_space=pltpu.VMEM)
    kinds = [F32] * 6 + [BF16, F32, F32, F32]
    done = pl.pallas_call(
        finish_kernel,
        out_shape=[shape(one.shape, kind) for one, kind in zip(arrays, kinds)],
        in_specs=[hbm] * 8 + [vmem] * 2,
        out_specs=[hbm] * 8 + [vmem] * 2,
        scratch_shapes=[
            pltpu.VMEM((6, width, width), BF16),
            pltpu.VMEM((6, width, width), F32),
            pltpu.VMEM(output.shape, BF16),
            pltpu.VMEM(input_grad.shape, F32),
            pltpu.SemaphoreType.DMA((8,)),
            pltpu.SemaphoreType.DMA((8,)),
        ],
        compiler_params=pltpu.CompilerParams(vmem_limit_bytes=62 << 20),
        name="finish",
    )(*arrays)
    return done[:6], done[6], done[7], done[8:]


def norm_rows(values, gain):
    average = jnp.mean(values, axis=-1, keepdims=True)
    centred = values - average
    spread = jnp.mean(centred * centred, axis=-1, keepdims=True)
    return centred * lax.rsqrt(spread + epsilon) * gain


def gelu_grad(pre, upstream):
    unused, pullback = jax.vjp(jax.nn.gelu, pre)
    return pullback(upstream)[0]


def split_heads(matrix):
    return matrix.reshape(matrix.shape[0], matrix.shape[1], H, HD).transpose(2, 0, 1, 3)


def join_heads(stacked):
    return stacked.transpose(1, 2, 0, 3).reshape(stacked.shape[1], stacked.shape[2], H * HD)


def per_device_plain(
    tokens,
    token_ids,
    hash_table,
    lengths,
    gain_attn,
    w_query,
    w_key,
    w_value,
    w_output,
    gain_ffn,
    w_in,
    w_out,
    cotangent,
):
    row_count, span, width = tokens.shape
    local_tok = row_count * span
    whole = span * lax.axis_size("seq")
    place = lax.axis_index("seq")
    scale = HD ** (-0.5)
    inputs = tokens.reshape(local_tok, width).astype(jnp.float32)
    key_positions = jnp.arange(whole, dtype=jnp.int32)
    query_positions = place * span + jnp.arange(span, dtype=jnp.int32)
    ends = jnp.cumsum(lengths, axis=1)
    key_document = jnp.sum(
        (key_positions[None, :, None] >= ends[:, None, :]).astype(jnp.int32), axis=2
    )
    query_document = jnp.sum(
        (query_positions[None, :, None] >= ends[:, None, :]).astype(jnp.int32), axis=2
    )
    visible = (key_positions[None, None, :] <= query_positions[None, :, None]) & (
        query_document[:, :, None] == key_document[:, None, :]
    )
    normed, first_norm_back = jax.vjp(norm_rows, inputs, gain_attn)
    normed_low = normed.astype(jnp.bfloat16)
    query = jnp.dot(normed_low, w_query, preferred_element_type=jnp.float32).astype(jnp.bfloat16)
    keys = jnp.dot(normed_low, w_key, preferred_element_type=jnp.float32).astype(jnp.bfloat16)
    values = jnp.dot(normed_low, w_value, preferred_element_type=jnp.float32).astype(jnp.bfloat16)
    own_pair = jnp.concatenate([keys, values], axis=1).reshape(row_count, span, 2 * width)
    all_pairs = lax.all_gather(own_pair, "seq", axis=1, tiled=True)

    def pair_heads(pairs):
        return (split_heads(pairs[:, :, :width]), split_heads(pairs[:, :, width:]))

    query_heads = split_heads(query.reshape(row_count, span, width))
    key_heads, value_heads = pair_heads(all_pairs)

    def head_forward(parts):
        query_one, key_one, value_one = parts
        scores = (
            jnp.einsum("rqd,rkd->rqk", query_one, key_one, preferred_element_type=jnp.float32)
            * scale
        )
        scores = jnp.where(visible, scores, masked_score)
        peak = jnp.max(scores, axis=2, keepdims=True)
        weights = jnp.exp(scores - peak)
        totals = jnp.sum(weights, axis=2, keepdims=True)
        probs = (weights / totals).astype(jnp.bfloat16)
        mixed = jnp.einsum("rqk,rkd->rqd", probs, value_one, preferred_element_type=jnp.float32)
        return (mixed, (peak + jnp.log(totals))[:, :, 0])

    mixed_heads, log_totals = lax.map(head_forward, (query_heads, key_heads, value_heads))
    attended = join_heads(mixed_heads).reshape(local_tok, width).astype(jnp.bfloat16)
    middle = inputs + jnp.dot(attended, w_output, preferred_element_type=jnp.float32)
    ffn_norm, second_norm_back = jax.vjp(norm_rows, middle, gain_ffn)
    ffn_in = ffn_norm.astype(jnp.bfloat16)
    experts = lax.axis_size("expert")
    capacity = min(2 * local_tok // experts, 3 * local_tok // 4)
    expert_of = jnp.take(hash_table, token_ids.reshape(local_tok), axis=0)
    labels = jnp.arange(experts, dtype=jnp.int32)
    onehot = (expert_of[:, None] == labels[None, :]).astype(jnp.int32)
    own_rank = jnp.sum((jnp.cumsum(onehot, axis=0) - 1) * onehot, axis=1)
    slots = expert_of * capacity + own_rank
    sources = (
        jnp.full((experts * capacity,), local_tok, jnp.int32)
        .at[slots]
        .set(jnp.arange(local_tok, dtype=jnp.int32))
    )

    def to_slots(rows_low):
        padded = jnp.concatenate([rows_low, jnp.zeros((1, width), rows_low.dtype)], axis=0)
        return jnp.take(padded, sources, axis=0).reshape(experts, capacity, width)

    received = lax.all_to_all(
        to_slots(ffn_in), "expert", split_axis=0, concat_axis=0, tiled=True
    ).reshape(-1, width)
    full_in, full_out = (
        lax.all_gather(w_in, "seq", axis=2, tiled=True),
        lax.all_gather(w_out, "seq", axis=1, tiled=True),
    )
    full_in = full_in[0]
    full_out = full_out[0]
    first = jnp.dot(received, full_in, preferred_element_type=jnp.float32)
    produced = jnp.dot(
        jax.nn.gelu(first).astype(jnp.bfloat16), full_out, preferred_element_type=jnp.float32
    ).astype(jnp.bfloat16)
    returned = lax.all_to_all(
        produced.reshape(experts, capacity, width),
        "expert",
        split_axis=0,
        concat_axis=0,
        tiled=True,
    ).reshape(-1, width)
    output = middle + jnp.take(returned, slots, axis=0).astype(jnp.float32)
    upstream = cotangent.reshape(local_tok, width)
    grad_received_out = lax.all_to_all(
        to_slots(upstream), "expert", split_axis=0, concat_axis=0, tiled=True
    ).reshape(-1, width)
    pre = jnp.dot(received, full_in, preferred_element_type=jnp.float32)
    hidden = jax.nn.gelu(pre).astype(jnp.bfloat16)
    grad_full_out = jnp.einsum(
        "rf,rd->fd", hidden, grad_received_out, preferred_element_type=jnp.float32
    )
    grad_hidden = jnp.einsum(
        "rd,fd->rf", grad_received_out, full_out, preferred_element_type=jnp.float32
    )
    grad_pre = gelu_grad(pre, grad_hidden).astype(jnp.bfloat16)
    grad_full_in = jnp.einsum("rd,rf->df", received, grad_pre, preferred_element_type=jnp.float32)
    grad_received = jnp.einsum(
        "rf,df->rd", grad_pre, full_in, preferred_element_type=jnp.float32
    ).astype(jnp.bfloat16)
    grad_in_part, grad_out_part = (
        lax.psum_scatter(
            grad_full_in[None].astype(jnp.bfloat16), "seq", scatter_dimension=2, tiled=True
        ).astype(jnp.float32),
        lax.psum_scatter(
            grad_full_out[None].astype(jnp.bfloat16), "seq", scatter_dimension=1, tiled=True
        ).astype(jnp.float32),
    )
    grad_in, grad_out = (
        lax.psum(grad_in_part.astype(jnp.bfloat16), "dp").astype(jnp.float32),
        lax.psum(grad_out_part.astype(jnp.bfloat16), "dp").astype(jnp.float32),
    )
    grad_back = lax.all_to_all(
        grad_received.reshape(experts, capacity, width),
        "expert",
        split_axis=0,
        concat_axis=0,
        tiled=True,
    ).reshape(-1, width)
    grad_ffn_in = jnp.take(grad_back, slots, axis=0).astype(jnp.float32)
    grad_middle_norm, grad_gain_ffn = second_norm_back(grad_ffn_in)
    grad_middle = upstream.astype(jnp.float32) + grad_middle_norm
    grad_branch = grad_middle.astype(jnp.bfloat16)
    grad_w_output = jnp.einsum(
        "cd,ce->de", attended, grad_branch, preferred_element_type=jnp.float32
    )
    grad_attended = jnp.einsum(
        "ce,de->cd", grad_branch, w_output, preferred_element_type=jnp.float32
    ).astype(jnp.bfloat16)
    again_pairs = lax.all_gather(own_pair, "seq", axis=1, tiled=True)
    key_back, value_back = pair_heads(again_pairs)

    def head_backward(parts):
        query_one, key_one, value_one, grad_one, log_one = parts
        scores = (
            jnp.einsum("rqd,rkd->rqk", query_one, key_one, preferred_element_type=jnp.float32)
            * scale
        )
        scores = jnp.where(visible, scores, masked_score)
        probs_full = jnp.exp(scores - log_one[:, :, None])
        probs = probs_full.astype(jnp.bfloat16)
        grad_probs = jnp.einsum(
            "rqd,rkd->rqk", grad_one, value_one, preferred_element_type=jnp.float32
        )
        inner = jnp.sum(probs_full * grad_probs, axis=2, keepdims=True)
        grad_scores = (probs_full * (grad_probs - inner)).astype(jnp.bfloat16)
        grad_query_one = (
            jnp.einsum("rqk,rkd->rqd", grad_scores, key_one, preferred_element_type=jnp.float32)
            * scale
        )
        grad_key_one = (
            jnp.einsum("rqk,rqd->rkd", grad_scores, query_one, preferred_element_type=jnp.float32)
            * scale
        )
        grad_value_one = jnp.einsum(
            "rqk,rqd->rkd", probs, grad_one, preferred_element_type=jnp.float32
        )
        return (grad_query_one, grad_key_one, grad_value_one)

    grad_att_heads = split_heads(grad_attended.reshape(row_count, span, width))
    grad_query_heads, grad_key_heads, grad_value_heads = lax.map(
        head_backward, (query_heads, key_back, value_back, grad_att_heads, log_totals)
    )
    grad_query_rows = join_heads(grad_query_heads).reshape(local_tok, width).astype(jnp.bfloat16)
    pair_grads = jnp.concatenate([join_heads(grad_key_heads), join_heads(grad_value_heads)], axis=2)
    own_grads = (
        lax.psum_scatter(pair_grads, "seq", scatter_dimension=1, tiled=True)
        .reshape(local_tok, 2 * width)
        .astype(jnp.bfloat16)
    )
    grad_key_rows = own_grads[:, :width]
    grad_value_rows = own_grads[:, width:]
    grad_w_query = jnp.einsum(
        "cd,ce->de", normed_low, grad_query_rows, preferred_element_type=jnp.float32
    )
    grad_w_key = jnp.einsum(
        "cd,ce->de", normed_low, grad_key_rows, preferred_element_type=jnp.float32
    )
    grad_w_value = jnp.einsum(
        "cd,ce->de", normed_low, grad_value_rows, preferred_element_type=jnp.float32
    )
    grad_normed = jnp.einsum(
        "ce,de->cd", grad_query_rows, w_query, preferred_element_type=jnp.float32
    )
    grad_normed = grad_normed + jnp.einsum(
        "ce,de->cd", grad_key_rows, w_key, preferred_element_type=jnp.float32
    )
    grad_normed = grad_normed + jnp.einsum(
        "ce,de->cd", grad_value_rows, w_value, preferred_element_type=jnp.float32
    )
    grad_inputs_norm, grad_gain_attn = first_norm_back(grad_normed)
    input_grad = grad_middle + grad_inputs_norm
    summed = lax.psum(
        (grad_gain_attn, grad_w_query, grad_w_key, grad_w_value, grad_w_output, grad_gain_ffn),
        ("dp", "seq", "expert"),
    )
    shaped_output = output.astype(jnp.bfloat16).reshape(row_count, span, width)
    shaped_grad = input_grad.reshape(row_count, span, width)
    return (
        shaped_output,
        shaped_grad,
        summed[0],
        summed[1],
        summed[2],
        summed[3],
        summed[4],
        summed[5],
        grad_in,
        grad_out,
    )


def per_device(
    tokens,
    token_ids,
    hash_table,
    lengths,
    gain_attn,
    w_query,
    w_key,
    w_value,
    w_output,
    gain_ffn,
    w_in,
    w_out,
    cotangent,
):
    row_count, span, width = tokens.shape
    local_tok = row_count * span
    output, input_grad, grad_q, grad_k, grad_v, grad_o, grad_in, grad_out, grad_gain_a, grad_gain_f = block(
        tokens, cotangent.reshape(local_tok, width), token_ids, hash_table.reshape(-1, 128), lengths,
        gain_attn, gain_ffn,
        w_query, w_key, w_value, w_output, w_in[0], w_out[0])[:10]
    squares, output, input_grad, gains = finish(
        (grad_q, grad_k, grad_v, grad_o, grad_in, grad_out), output, input_grad, (grad_gain_a, grad_gain_f))
    return (
        output,
        input_grad,
        gains[0],
        squares[0],
        squares[1],
        squares[2],
        squares[3],
        gains[1],
        squares[4][None],
        squares[5][None],
    )


def solution(mesh):
    sizes = (mesh.shape["dp"], mesh.shape["seq"], mesh.shape["expert"])
    return jax.shard_map(
        per_device if sizes == (4, 4, 2) else per_device_plain,
        mesh=mesh,
        in_specs=(
            P(("dp", "expert"), "seq", None),
            P(("dp", "expert"), "seq"),
            P(),
            P(("dp", "expert"), None),
            P(),
            P(),
            P(),
            P(),
            P(),
            P(),
            P("expert", None, "seq"),
            P("expert", "seq", None),
            P(("dp", "expert"), "seq", None),
        ),
        out_specs=(
            P(("dp", "expert"), "seq", None),
            P(("dp", "expert"), "seq", None),
            P(),
            P(),
            P(),
            P(),
            P(),
            P(),
            P("expert", None, "seq"),
            P("expert", "seq", None),
        ),
        check_vma=False,
    )
```
